32 devices in a mesh: grp: 2 (over y), orb: 4 (over z), cmp: 4 (over x, core).
Axes of the slice: x: 2, y: 2, z: 4, core: 2. Of those that a mesh axis runs over, the one named last changes fastest.
Arguments:
- psi: float32 [64, 64, 1024], P(('grp', 'orb'), 'cmp'), parts along dimension 0, may hold values from -6 to 6
- potential: float32 [128, 1024], P(('grp', 'cmp')), parts along dimension 0, may hold values from -2 to 2
- extent: int32 [64], P('grp'), parts along dimension 0, may hold values from 256 to 1024, as said below
Outputs:
- psi_new: float32 [64, 64, 1024], P(('grp', 'orb'), 'cmp'), parts along dimension 0
- density: float32 [128, 1024], P(('grp', 'cmp'), 'orb'), parts along dimension 0
The draws below stay inside these ranges and needn't reach their ends.
There are 2 independent parts, one for each index of `grp`. The reference program is written for one: setup_inputs(seed, part) draws one part's arguments, and reference() takes and returns one part's arrays. A program takes and returns all parts, laid end to end along the dimension named above; each array names one. Nothing has to cross between parts.
Inputs may be any that keep to these rules, and one draw needn't show every extreme that they name: `extent`: some orbital's region covers the whole plane in every draw.
All inputs are finite; a program needn't handle non-finite values.
Results may differ from the reference program's by a relative error of at most 0.00007.
Values sent between devices are 32-bit elements; how exact they have to be, the bound alone decides.
No kernel may reach another device: no remote copies, remote signals or barrier semaphores. Data moves between devices by JAX's collectives and lax.ppermute only.
A program may use at most 64 MiB of HBM per device.

```python
import math
import jax
import jax.numpy as jnp
from jax import lax

GP = 1024
NORB = 32
GX = 64


def draw_extent(key, part):
    key = jax.random.fold_in(key, 7)
    first, second = jax.random.split(key)
    base = jax.random.randint(first, (NORB,), GP // 4, GP + 1)
    widest = jax.random.randint(second, (), 0, NORB)
    return jnp.where(jnp.arange(NORB) == widest, GP, base).astype(jnp.int32)


def level_of(key, dims, pieces, smallest, top_value):
    factor_of, own = 1.0, jax.random.fold_in(key, 6)
    for dim, blocks in pieces:
        steps = jnp.exp(jax.random.uniform(jax.random.fold_in(own, dim), (blocks,), jnp.float32, smallest / len(pieces), top_value / len(pieces)))
        factor_of = factor_of * jnp.repeat(steps, dims[dim] // blocks).reshape([-1 if axis == dim else 1 for axis in range(len(dims))])
    return factor_of


def scatter_about(key, dims, width, limit, cuts=(), kind=jnp.bfloat16):
    values = jax.random.normal(key, dims, jnp.float32) * width
    if len(cuts) > 0:
        values = level_of(key, dims, cuts, -0.22, 0.18) * values
    return jnp.clip(values, min=-limit, max=limit).astype(kind)


def setup_inputs(seed: int = 0, part: int = 0) -> dict:
    seeds = jax.random.split(jax.random.key(seed), 4)
    own_keys = jax.random.split(jax.random.fold_in(seeds[3], part), 4)
    return {
        "psi": scatter_about(own_keys[0], (NORB, GX, GP), 1.0, 6.0, ((0, 4), (1, 4)), jnp.float32),
        "potential": jnp.clip(jax.random.uniform(own_keys[1], (GX, GP), jnp.float32, -2.0, 2.0) * level_of(own_keys[1], (GX, GP), ((0, 4),), -0.4, 0.0), -2.0, 2.0),
        "extent": draw_extent(jax.random.fold_in(jax.random.fold_in(seeds[3], part), 71), part),
    }


step_length = 0.2
reach = 14


def laplace(field, axis):
    total = (-math.pi ** 2 / 3.0) * field
    for shift_by in range(1, reach + 1):
        weight = 2.0 * (-1.0) ** (shift_by + 1) / (shift_by * shift_by)
        total = total + weight * (jnp.roll(field, shift_by, axis) + jnp.roll(field, -shift_by, axis))
    return total


def reference(psi, potential, extent):
    column = jnp.arange(GP, dtype=jnp.int32)
    live = (column[None, :] < extent[:, None]).astype(jnp.float32)
    phi = psi * live[:, None, :]

    def apply_one(pair):
        field, region = pair
        kinetic = -0.5 * (laplace(field, 0) + laplace(field, 1))
        return region[None, :] * (kinetic + potential * field)

    hphi = lax.map(apply_one, (phi, live))
    flat_phi = phi.reshape(NORB, GX * GP)
    flat_h = hphi.reshape(NORB, GX * GP)
    correlation = lax.dot_general(flat_phi, flat_h, (((1,), (1,)), ((), ())), precision=lax.Precision.HIGHEST) / (GX * GP)
    grad = flat_h - jnp.dot(correlation.T, flat_phi, precision=lax.Precision.HIGHEST)
    psi_new = (flat_phi - step_length * grad).reshape(NORB, GX, GP)
    density = jnp.sum(psi_new * psi_new, axis=0) / NORB
    return psi_new, density
```

```python
import functools
import math

import jax
import jax.numpy as jnp
import numpy as np
from jax import lax
from jax.experimental import pallas as pl
from jax.experimental.pallas import tpu as pltpu
from jax.sharding import PartitionSpec as P

step_length = 0.2
reach = 14
lanes = 128


def padded_2(cells, sides, width):
    for axis, dim in sides:
        count = lax.axis_size(axis)
        head = lax.slice_in_dim(cells, 0, width, axis=dim)
        tail = lax.slice_in_dim(cells, cells.shape[dim] - width, cells.shape[dim], axis=dim)
        cells = jnp.concatenate(
            [
                lax.ppermute(tail, axis, [(i, (i + 1) % count) for i in range(count)]),
                cells,
                lax.ppermute(head, axis, [((i + 1) % count, i) for i in range(count)]),
            ],
            axis=dim,
        )
    return cells


def band_matrix(length):
    rows = lax.broadcasted_iota(jnp.int32, (length + 2 * reach, length), 0)
    cols = lax.broadcasted_iota(jnp.int32, (length + 2 * reach, length), 1)
    spread = jnp.abs(rows - reach - cols)
    safe = jnp.maximum(spread, 1).astype(jnp.float32)
    signed = jnp.where(spread % 2 == 1, 2.0, -2.0) / (safe * safe)
    value = jnp.where(spread == 0, -math.pi**2 / 3.0, signed)
    return jnp.where(spread <= reach, value, 0.0)


def across_planes(padded, planes):
    return jnp.einsum("awp,wy->ayp", padded, band_matrix(planes), precision=lax.Precision.HIGHEST)


def along_grid(field):
    orbs, planes, grid_p = field.shape
    width = 128
    blocks = field.reshape(orbs, planes, grid_p // width, width)
    before = jnp.roll(blocks[..., width - reach :], 1, axis=2)
    after = jnp.roll(blocks[..., :reach], -1, axis=2)
    window = jnp.concatenate([before, blocks, after], axis=3)
    result = jnp.einsum(
        "axnw,wq->axnq", window, band_matrix(width), precision=lax.Precision.HIGHEST
    )
    return result.reshape(orbs, planes, grid_p)


def general_device(psi, potential, extent):
    orb_dev, planes, grid_p = psi.shape
    n_orb = lax.axis_size("orb")
    norbitals = orb_dev * n_orb
    cells = planes * lax.axis_size("cmp") * grid_p
    column = lax.broadcasted_iota(jnp.int32, (norbitals, grid_p), 1)
    live_all = (column < extent[:, None]).astype(jnp.float32)
    own_live = lax.dynamic_slice_in_dim(live_all, lax.axis_index("orb") * orb_dev, orb_dev, 0)
    phi = psi * own_live[:, None, :]
    padded = padded_2(phi, (("cmp", 1),), reach)
    kinetic = -0.5 * (across_planes(padded, planes) + along_grid(phi))
    hphi = own_live[:, None, :] * (kinetic + potential[None] * phi)
    phi_c, hphi_c = (
        lax.all_to_all(phi, "orb", split_axis=2, concat_axis=0, tiled=True),
        lax.all_to_all(hphi, "orb", split_axis=2, concat_axis=0, tiled=True),
    )
    flat_phi = phi_c.reshape(norbitals, -1)
    flat_h = hphi_c.reshape(norbitals, -1)
    partial_correlation = lax.dot_general(
        flat_phi,
        flat_h,
        (((1,), (1,)), ((), ())),
        precision=lax.Precision.HIGHEST,
        preferred_element_type=jnp.float32,
    )
    correlation = lax.psum(partial_correlation, ("orb", "cmp")) / cells
    grad_c = (flat_h - jnp.dot(correlation.T, flat_phi, precision=lax.Precision.HIGHEST)).reshape(
        phi_c.shape
    )
    grad = lax.all_to_all(grad_c, "orb", split_axis=0, concat_axis=2, tiled=True)
    psi_new = phi - step_length * grad
    density = (
        lax.psum_scatter(jnp.sum(psi_new * psi_new, axis=0), "orb", scatter_dimension=1, tiled=True)
        / norbitals
    )
    return (psi_new, density)


def weight(spread):
    spread = np.abs(spread)
    safe = np.maximum(spread, 1).astype(np.float64)
    value = np.where(spread % 2 == 1, 2.0, -2.0) / (safe * safe)
    value = np.where(spread == 0, -math.pi**2 / 3.0, value)
    return np.where(spread <= reach, value, 0.0).astype(np.float32)


def two_parts(value):
    high = value.astype(jnp.bfloat16)
    return high, (value - high.astype(np.float32)).astype(jnp.bfloat16)


def column_band():
    rows = np.arange(2 * lanes)[:, None]
    cols = np.arange(lanes)[None, :]
    high, low = two_parts(weight(rows - cols - reach))
    return np.concatenate([high, low], axis=1)


def plane_band(planes):
    rows = np.arange(planes)[:, None]
    cols = np.arange(3 * planes)[None, :]
    high, low = two_parts(weight(cols - planes - rows))
    return np.concatenate([high, high, low], axis=1)


def in_vmem():
    return pl.BlockSpec(memory_space=pltpu.VMEM)


def in_smem():
    return pl.BlockSpec(memory_space=pltpu.SMEM)


def columns_of(shape):
    return lax.broadcasted_iota(jnp.int32, shape, len(shape) - 1)


def local_kernel(psi_ref, potential_ref, extent_ref, band_ref, out_ref, phi_ref):
    orbs, planes, grid_p = psi_ref.shape
    tiles = grid_p // lanes
    column = columns_of((planes, grid_p))
    for o in range(orbs):
        phi_ref[o * planes : (o + 1) * planes, :] = jnp.where(
            column < extent_ref[o], psi_ref[o], 0.0
        )
    moved = pltpu.roll(phi_ref[...], reach, 1)
    high, low = two_parts(moved)
    for t in range(tiles):
        here, after = t * lanes, (t + 1) % tiles * lanes
        high_t = jnp.concatenate([high[:, here : here + lanes], high[:, after : after + lanes]], 1)
        low_t = jnp.concatenate([low[:, here : here + lanes], low[:, after : after + lanes]], 1)
        both = jnp.dot(high_t, band_ref[...], preferred_element_type=jnp.float32)
        rest = jnp.dot(low_t, band_ref[:, :lanes], preferred_element_type=jnp.float32)
        second = both[:, :lanes] + both[:, lanes:] + rest
        field = phi_ref[:, here : here + lanes].reshape(orbs, planes, lanes)
        out_ref[:, :, here : here + lanes] = (
            potential_ref[:, here : here + lanes][None] * field
            - 0.5 * second.reshape(orbs, planes, lanes)
        )


def plane_kernel(before_ref, psi_ref, after_ref, local_ref, extent_ref, band_ref, out_ref):
    orbs, planes, grid_p = psi_ref.shape
    column = columns_of((planes, grid_p))
    for o in range(orbs):
        slab = jnp.concatenate([before_ref[o], psi_ref[o], after_ref[o]], axis=0)
        high, low = two_parts(slab)
        second = jnp.dot(
            band_ref[...],
            jnp.concatenate([high, low, high], axis=0),
            preferred_element_type=jnp.float32,
        )
        out_ref[o] = jnp.where(column < extent_ref[o], local_ref[o] - 0.5 * second, 0.0)


def overlap_kernel(scale, n_fields, own_fields, *refs):
    fields = refs[:n_fields]
    images = refs[n_fields : n_fields + 2]
    extent_ref, out_ref, rows_ref = refs[n_fields + 2 :]
    orbs, planes, grid_p = fields[0].shape
    column = columns_of((planes, grid_p))
    pieces = [(p, t) for p in range(0, planes, 8) for t in range(0, grid_p, lanes)]
    for f, field_ref in enumerate(fields):

        def one(a, carry):
            phi = jnp.where(column < extent_ref[f * orbs + a], field_ref[a], 0.0)
            for b in range(2 * orbs):
                image = images[b // orbs]
                total = None
                for p, t in pieces:
                    term = phi[p : p + 8, t : t + lanes] * image[b % orbs, p : p + 8, t : t + lanes]
                    total = term if total is None else total + term
                rows_ref[b, pl.ds(f * orbs + a, 1), :] = jnp.sum(total, axis=0, keepdims=True)
            return carry

        lax.fori_loop(0, orbs, one, 0)
    for b in range(2 * orbs):
        out_ref[:, b : b + 1] = jnp.sum(rows_ref[b], axis=1, keepdims=True) * scale


def combined(phi_ref, base, coefficient, chunk):
    total = list(base)
    for a in range(phi_ref.shape[0]):
        phi = phi_ref[a, :, chunk]
        for b in range(len(total)):
            total[b] = total[b] + coefficient(a, b) * phi
    return total


def density_kernel(
    own_ref, pair_ref, third_ref, fourth_ref, image_ref, ward_ref, corr_ref, extent_ref, mid_ref,
    out_ref, phi_ref,
):
    orbs, planes, grid_p = own_ref.shape
    width = 2 * lanes

    @pl.when(mid_ref[0] == 1)
    def _():
        column = columns_of((planes, grid_p))
        for f, field_ref in enumerate((own_ref, pair_ref, third_ref, fourth_ref)):
            for a in range(orbs):
                phi_ref[f * orbs + a] = jnp.where(
                    column < extent_ref[f * orbs + a], field_ref[a], 0.0
                )

        def one(c, carry):
            chunk = pl.ds(pl.multiple_of(c * width, width), width)
            density = jnp.zeros((planes, width), jnp.float32)
            for part, half_ref in enumerate((image_ref, ward_ref)):
                base = [
                    phi_ref[part * orbs + b, :, chunk] - step_length * half_ref[b, :, chunk]
                    for b in range(orbs)
                ]
                total = combined(
                    phi_ref, base, lambda a, b: step_length * corr_ref[a, part * orbs + b], chunk
                )
                for value in total:
                    density = density + value * value
            out_ref[:, chunk] = density * (1.0 / phi_ref.shape[0])
            return carry

        lax.fori_loop(0, grid_p // width, one, 0)

    @pl.when(mid_ref[0] != 1)
    def _():
        out_ref[...] = jnp.zeros_like(out_ref)


def update_kernel(
    own_ref, pair_ref, third_in, third_out, fourth_in, fourth_out, image_ref, corr_ref, extent_ref,
    mid_ref, out_ref, phi_ref,
):
    orbs, planes, grid_p = own_ref.shape
    width = 2 * lanes
    column = columns_of((planes, grid_p))

    def put(first, field_ref):
        for a in range(orbs):
            phi_ref[first + a] = jnp.where(column < extent_ref[first + a], field_ref[a], 0.0)

    put(0, own_ref)
    put(orbs, pair_ref)

    @pl.when(mid_ref[0] == 1)
    def _():
        put(2 * orbs, third_in)
        put(3 * orbs, fourth_in)

    @pl.when(mid_ref[0] != 1)
    def _():
        put(2 * orbs, third_out)
        put(3 * orbs, fourth_out)

    def one(c, carry):
        chunk = pl.ds(pl.multiple_of(c * width, width), width)
        base = [phi_ref[b, :, chunk] - step_length * image_ref[b, :, chunk] for b in range(orbs)]
        total = combined(phi_ref, base, lambda a, b: step_length * corr_ref[a, b], chunk)
        for b in range(orbs):
            out_ref[b, :, chunk] = total[b]
        return carry

    lax.fori_loop(0, grid_p // width, one, 0)


params = pltpu.CompilerParams(vmem_limit_bytes=24 * 2**20)
small = pl.CostEstimate(flops=1, bytes_accessed=1, transcendentals=0)


def line_device(psi, potential, extent):
    orbs, planes, grid_p = psi.shape
    n_cmp = lax.axis_size("cmp")
    norbitals = 4 * orbs
    cells = planes * n_cmp * grid_p
    z = lax.axis_index("orb")
    inner = (z == 1) | (z == 2)
    swap = [(0, 1), (1, 0), (2, 3), (3, 2)]
    across = [(1, 2), (2, 1)]
    outward = [(1, 0), (2, 3)]
    inward = [(0, 1), (3, 2)]

    third_of = jnp.where(z < 2, 2, 1)
    fourth_of = jnp.where(z < 2, 3, 0)
    by_owner = extent.reshape(4, orbs)
    order = jnp.stack([z, z ^ 1, third_of, fourth_of])
    extents = jnp.take(by_owner, order, axis=0).reshape(-1)
    own_extent = extents[:orbs]
    is_inner = inner.astype(jnp.int32).reshape(1)

    block = jax.ShapeDtypeStruct(psi.shape, jnp.float32)

    pair = lax.ppermute(psi, "orb", swap)
    third_in = lax.ppermute(psi, "orb", across)
    before = lax.ppermute(psi, "cmp", [(i, (i + 1) % n_cmp) for i in range(n_cmp)])
    after = lax.ppermute(psi, "cmp", [((i + 1) % n_cmp, i) for i in range(n_cmp)])

    local = pl.pallas_call(
        local_kernel,
        out_shape=block,
        in_specs=[in_vmem(), in_vmem(), in_smem(), in_vmem()],
        out_specs=in_vmem(),
        scratch_shapes=[pltpu.VMEM((orbs * planes, grid_p), jnp.float32)],
        compiler_params=params,
        cost_estimate=small,
    )(psi, potential, own_extent, jnp.asarray(column_band()))
    image = pl.pallas_call(
        plane_kernel,
        out_shape=block,
        in_specs=[in_vmem()] * 4 + [in_smem(), in_vmem()],
        out_specs=in_vmem(),
        compiler_params=params,
        cost_estimate=small,
    )(before, psi, after, local, own_extent, jnp.asarray(plane_band(planes)))

    ward = lax.ppermute(image, "orb", inward)
    fourth_in = lax.ppermute(pair, "orb", across)
    third_out = lax.ppermute(third_in, "orb", outward)
    fourth_out = lax.ppermute(fourth_in, "orb", outward)

    ward, fourth_in, third_out = lax.optimization_barrier((ward, fourth_in, third_out))

    part = pl.pallas_call(
        functools.partial(overlap_kernel, 1.0 / cells, 4, 3),
        out_shape=jax.ShapeDtypeStruct((norbitals, 2 * orbs), jnp.float32),
        in_specs=[in_vmem()] * 6 + [in_smem()],
        out_specs=in_vmem(),
        scratch_shapes=[pltpu.VMEM((2 * orbs, norbitals, lanes), jnp.float32)],
        compiler_params=params,
        cost_estimate=small,
    )(psi, pair, third_in, fourth_in, image, ward, extents)
    near = lax.ppermute(part, "cmp", [(i, i ^ 1) for i in range(n_cmp)])
    far = lax.ppermute(part, "cmp", [(i, i ^ 2) for i in range(n_cmp)])
    farther = lax.ppermute(part, "cmp", [(i, i ^ 3) for i in range(n_cmp)])
    correlation = (part + near) + (far + farther)

    given = lax.ppermute(correlation, "orb", outward)
    given = given.reshape(4, orbs, 2 * orbs)[:, :, orbs:]
    given = jnp.concatenate([given[1], given[0], given[2], given[3]], axis=0)
    own_correlation = jnp.where(inner, correlation[:, :orbs], given)

    density = pl.pallas_call(
        density_kernel,
        out_shape=jax.ShapeDtypeStruct((planes, grid_p), jnp.float32),
        in_specs=[in_vmem()] * 6 + [in_smem()] * 3,
        out_specs=in_vmem(),
        scratch_shapes=[pltpu.VMEM((norbitals, planes, grid_p), jnp.float32)],
        compiler_params=params,
        cost_estimate=small,
    )(psi, pair, third_in, fourth_in, image, ward, correlation, extents, is_inner)

    share = grid_p // 4
    owned = lambda who: lax.dynamic_slice_in_dim(density, who * share, share, 1)
    total = owned(z)
    total = total + lax.ppermute(owned(z ^ 1), "orb", [(1, 0), (2, 3)])
    total = total + lax.ppermute(owned(z ^ 2), "orb", [(1, 3), (2, 0)])
    total = total + lax.ppermute(owned(z ^ 3), "orb", [(1, 2), (2, 1)])

    psi_new = pl.pallas_call(
        update_kernel,
        out_shape=block,
        in_specs=[in_vmem()] * 7 + [in_smem()] * 3,
        out_specs=in_vmem(),
        scratch_shapes=[pltpu.VMEM((norbitals, planes, grid_p), jnp.float32)],
        compiler_params=params,
        cost_estimate=small,
    )(
        psi, pair, third_in, third_out, fourth_in, fourth_out, image, own_correlation, extents,
        is_inner,
    )
    return (psi_new, total)


def per_device(psi, potential, extent):
    orbs, planes, grid_p = psi.shape
    fits = (
        lax.axis_size("orb") == 4
        and lax.axis_size("cmp") == 4
        and orbs == 8
        and planes == 16
        and grid_p % (4 * lanes) == 0
    )
    return (line_device if fits else general_device)(psi, potential, extent)


def solution(mesh):
    return jax.shard_map(
        per_device,
        mesh=mesh,
        in_specs=(P(("grp", "orb"), "cmp", None), P(("grp", "cmp"), None), P("grp")),
        out_specs=(P(("grp", "orb"), "cmp", None), P(("grp", "cmp"), "orb")),
        check_vma=False,
    )
```

```python
import functools
import math

import jax
import jax.numpy as jnp
import numpy as np
from jax import lax
from jax.experimental import pallas as pl
from jax.experimental.pallas import tpu as pltpu
from jax.sharding import PartitionSpec as P

step_length = 0.2
reach = 14
lanes = 128


def padded_2(cells, sides, width):
    for axis, dim in sides:
        count = lax.axis_size(axis)
        head = lax.slice_in_dim(cells, 0, width, axis=dim)
        tail = lax.slice_in_dim(cells, cells.shape[dim] - width, cells.shape[dim], axis=dim)
        cells = jnp.concatenate(
            [
                lax.ppermute(tail, axis, [(i, (i + 1) % count) for i in range(count)]),
                cells,
                lax.ppermute(head, axis, [((i + 1) % count, i) for i in range(count)]),
            ],
            axis=dim,
        )
    return cells


def band_matrix(length):
    rows = lax.broadcasted_iota(jnp.int32, (length + 2 * reach, length), 0)
    cols = lax.broadcasted_iota(jnp.int32, (length + 2 * reach, length), 1)
    spread = jnp.abs(rows - reach - cols)
    safe = jnp.maximum(spread, 1).astype(jnp.float32)
    signed = jnp.where(spread % 2 == 1, 2.0, -2.0) / (safe * safe)
    value = jnp.where(spread == 0, -math.pi**2 / 3.0, signed)
    return jnp.where(spread <= reach, value, 0.0)


def across_planes(padded, planes):
    return jnp.einsum("awp,wy->ayp", padded, band_matrix(planes), precision=lax.Precision.HIGHEST)


def along_grid(field):
    orbs, planes, grid_p = field.shape
    width = 128
    blocks = field.reshape(orbs, planes, grid_p // width, width)
    before = jnp.roll(blocks[..., width - reach :], 1, axis=2)
    after = jnp.roll(blocks[..., :reach], -1, axis=2)
    window = jnp.concatenate([before, blocks, after], axis=3)
    result = jnp.einsum(
        "axnw,wq->axnq", window, band_matrix(width), precision=lax.Precision.HIGHEST
    )
    return result.reshape(orbs, planes, grid_p)


def general_device(psi, potential, extent):
    orb_dev, planes, grid_p = psi.shape
    n_orb = lax.axis_size("orb")
    norbitals = orb_dev * n_orb
    cells = planes * lax.axis_size("cmp") * grid_p
    column = lax.broadcasted_iota(jnp.int32, (norbitals, grid_p), 1)
    live_all = (column < extent[:, None]).astype(jnp.float32)
    own_live = lax.dynamic_slice_in_dim(live_all, lax.axis_index("orb") * orb_dev, orb_dev, 0)
    phi = psi * own_live[:, None, :]
    padded = padded_2(phi, (("cmp", 1),), reach)
    kinetic = -0.5 * (across_planes(padded, planes) + along_grid(phi))
    hphi = own_live[:, None, :] * (kinetic + potential[None] * phi)
    phi_c, hphi_c = (
        lax.all_to_all(phi, "orb", split_axis=2, concat_axis=0, tiled=True),
        lax.all_to_all(hphi, "orb", split_axis=2, concat_axis=0, tiled=True),
    )
    flat_phi = phi_c.reshape(norbitals, -1)
    flat_h = hphi_c.reshape(norbitals, -1)
    partial_correlation = lax.dot_general(
        flat_phi,
        flat_h,
        (((1,), (1,)), ((), ())),
        precision=lax.Precision.HIGHEST,
        preferred_element_type=jnp.float32,
    )
    correlation = lax.psum(partial_correlation, ("orb", "cmp")) / cells
    grad_c = (flat_h - jnp.dot(correlation.T, flat_phi, precision=lax.Precision.HIGHEST)).reshape(
        phi_c.shape
    )
    grad = lax.all_to_all(grad_c, "orb", split_axis=0, concat_axis=2, tiled=True)
    psi_new = phi - step_length * grad
    density = (
        lax.psum_scatter(jnp.sum(psi_new * psi_new, axis=0), "orb", scatter_dimension=1, tiled=True)
        / norbitals
    )
    return (psi_new, density)


def weight(spread):
    spread = np.abs(spread)
    safe = np.maximum(spread, 1).astype(np.float64)
    value = np.where(spread % 2 == 1, 2.0, -2.0) / (safe * safe)
    value = np.where(spread == 0, -math.pi**2 / 3.0, value)
    return np.where(spread <= reach, value, 0.0).astype(np.float32)


def two_parts(value):
    high = value.astype(jnp.bfloat16)
    return high, (value - high.astype(np.float32)).astype(jnp.bfloat16)


def column_band():
    rows = np.arange(2 * lanes)[:, None]
    cols = np.arange(lanes)[None, :]
    high, low = two_parts(weight(rows - cols - reach))
    return np.concatenate([high, low], axis=1)


def plane_bands(planes):
    rows = np.arange(planes)[:, None]
    cols = np.arange(planes)[None, :]
    both = []
    for side in (-planes, planes):
        band = np.concatenate(
            [weight(cols + side - rows), weight(cols - rows), weight(cols - side - rows)], axis=1
        )
        high, low = two_parts(band)
        both.append(np.concatenate([high, high, low], axis=1))
    return np.stack(both)


def in_vmem():
    return pl.BlockSpec(memory_space=pltpu.VMEM)


def in_smem():
    return pl.BlockSpec(memory_space=pltpu.SMEM)


def columns_of(shape):
    return lax.broadcasted_iota(jnp.int32, shape, len(shape) - 1)


def owner_of(place_ref, f):
    z = place_ref[0]
    if f < 2:
        return z if f == 0 else jnp.where(z % 2 == 0, z + 1, z - 1)
    left, right = (2, 1) if f == 2 else (3, 0)
    return jnp.where(z < 2, left, right)


def masked(field_ref, a, extent_ref, owner):
    orbs, planes, grid_p = field_ref.shape
    column = columns_of((planes, grid_p))
    return jnp.where(column < extent_ref[owner * orbs + a], field_ref[a], 0.0)


def split_into(parts_ref, field_ref, extent_ref, owner):
    orbs, planes, _ = field_ref.shape
    for a in range(orbs):
        high, low = two_parts(masked(field_ref, a, extent_ref, owner))
        parts_ref[a * planes : (a + 1) * planes, :] = high
        parts_ref[(orbs + a) * planes : (orbs + a + 1) * planes, :] = low


def split_kernel(f, field_ref, extent_ref, place_ref, parts_ref):
    split_into(parts_ref, field_ref, extent_ref, owner_of(place_ref, f))


def local_kernel(f, psi_ref, potential_ref, extent_ref, place_ref, band_ref, out_ref, parts_ref, phi_ref):
    orbs, planes, grid_p = psi_ref.shape
    tiles = grid_p // lanes
    owner = owner_of(place_ref, f)
    for a in range(orbs):
        phi = masked(psi_ref, a, extent_ref, owner)
        phi_ref[a * planes : (a + 1) * planes, :] = phi
        high, low = two_parts(phi)
        parts_ref[a * planes : (a + 1) * planes, :] = high
        parts_ref[(orbs + a) * planes : (orbs + a + 1) * planes, :] = low
    high, low = two_parts(pltpu.roll(phi_ref[...], reach, 1))
    for t in range(tiles):
        here, after = t * lanes, (t + 1) % tiles * lanes
        high_t = jnp.concatenate([high[:, here : here + lanes], high[:, after : after + lanes]], 1)
        low_t = jnp.concatenate([low[:, here : here + lanes], low[:, after : after + lanes]], 1)
        both = jnp.dot(high_t, band_ref[...], preferred_element_type=jnp.float32)
        rest = jnp.dot(low_t, band_ref[:, :lanes], preferred_element_type=jnp.float32)
        second = both[:, :lanes] + both[:, lanes:] + rest
        field = phi_ref[:, here : here + lanes].reshape(orbs, planes, lanes)
        out_ref[:, :, here : here + lanes] = (
            potential_ref[:, here : here + lanes][None] * field
            - 0.5 * second.reshape(orbs, planes, lanes)
        )


def plane_kernel(
    f, far_ref, psi_ref, near_ref, local_ref, extent_ref, place_ref, band_ref, out_ref, parts_ref
):
    orbs, planes, grid_p = psi_ref.shape
    column = columns_of((planes, grid_p))
    owner = owner_of(place_ref, f)
    band = band_ref[place_ref[1]]
    for a in range(orbs):
        slab = jnp.concatenate([far_ref[a], psi_ref[a], near_ref[a]], axis=0)
        high, low = two_parts(slab)
        second = jnp.dot(
            band, jnp.concatenate([high, low, high], axis=0), preferred_element_type=jnp.float32
        )
        image = jnp.where(
            column < extent_ref[owner * orbs + a], local_ref[a] - 0.5 * second, 0.0
        )
        out_ref[a] = image
        high, low = two_parts(image)
        parts_ref[a * planes : (a + 1) * planes, :] = high
        parts_ref[(orbs + a) * planes : (orbs + a + 1) * planes, :] = low


def overlaps(field_ref, image_ref, planes):
    half = field_ref.shape[0] // 2
    product = lax.dot_general(
        field_ref[...],
        image_ref[...],
        (((1,), (1,)), ((), ())),
        preferred_element_type=jnp.float32,
    )
    product = product[:half] + product[half:]
    product = product[:, :half] + product[:, half:]
    row = lax.broadcasted_iota(jnp.int32, (half, half), 0)
    col = lax.broadcasted_iota(jnp.int32, (half, half), 1)
    product = jnp.where(row % planes == col % planes, product, 0.0)
    return jnp.sum(product.reshape(half // planes, planes, half), axis=1)


def overlap_kernel(planes, n_fields, *refs):
    fields, image_ref, out_ref = refs[:n_fields], refs[n_fields], refs[n_fields + 1]
    for f, field_ref in enumerate(fields):
        value = overlaps(field_ref, image_ref, planes)
        out_ref[f * value.shape[0] : (f + 1) * value.shape[0], :] = value


def correlation_kernel(
    planes, scale, own_ref, pair_ref, third_ref, fourth_ref, image_ref, ward_ref, early_ref, out_ref
):
    half = own_ref.shape[0] // 2
    orbs = half // planes
    ward = [overlaps(ref, ward_ref, planes) for ref in (own_ref, pair_ref, third_ref, fourth_ref)]
    last = overlaps(fourth_ref, image_ref, planes)
    wide = jnp.concatenate(
        [jnp.concatenate([early_ref[...], last], axis=0), jnp.concatenate(ward, axis=0)], axis=1
    )
    row = lax.broadcasted_iota(jnp.int32, (2 * half, 2 * orbs), 0)
    col = lax.broadcasted_iota(jnp.int32, (2 * half, 2 * orbs), 1)
    gather = jnp.where(row // planes == col, scale, 0.0)
    out_ref[...] = jnp.dot(
        wide, gather, precision=lax.Precision.HIGHEST, preferred_element_type=jnp.float32
    )


def sum_kernel(*refs):
    total = refs[0][...]
    for ref in refs[1:-1]:
        total = total + ref[...]
    refs[-1][...] = total


def spread_out(corr, planes):
    n_a, n_b = corr.shape

    def iota(shape, dim):
        return lax.broadcasted_iota(jnp.int32, shape, dim)

    take_b = (iota((n_b * planes, n_b), 0) // planes == iota((n_b * planes, n_b), 1)).astype(
        jnp.float32
    )
    take_a = (iota((n_a, n_a * planes), 1) // planes == iota((n_a, n_a * planes), 0)).astype(
        jnp.float32
    )
    rows = lax.dot_general(
        take_b,
        corr * step_length,
        (((1,), (1,)), ((), ())),
        precision=lax.Precision.HIGHEST,
        preferred_element_type=jnp.float32,
    )
    full = jnp.dot(
        rows, take_a, precision=lax.Precision.HIGHEST, preferred_element_type=jnp.float32
    )
    shape = (n_b * planes, n_a * planes)
    full = jnp.where(iota(shape, 0) % planes == iota(shape, 1) % planes, full, 0.0)
    return two_parts(full)


def projections(high, low, fields, chunk):
    half = fields[0].shape[0] // 2
    total = None
    for f, field_ref in enumerate(fields):
        here = slice(f * half, (f + 1) * half)
        left = jnp.concatenate(
            [
                jnp.concatenate([high[:, here], high[:, here]], axis=1),
                jnp.concatenate([low[:, here], low[:, here]], axis=1),
            ],
            axis=0,
        )
        term = jnp.dot(left, field_ref[:, chunk], preferred_element_type=jnp.float32)
        total = term if total is None else total + term
    n = total.shape[0] // 2
    return total[:n] + total[n:]


def density_kernel(
    own_ref, pair_ref, own_parts, pair_parts, third_parts, fourth_parts, image_ref, ward_ref,
    corr_ref, extent_ref, place_ref, *refs,
):
    orbs, planes, grid_p = own_ref.shape
    width = 2 * lanes
    share = grid_p // 4
    out_ref, all_ref = refs[:4], refs[4]
    z = place_ref[0]
    inner = (z == 1) | (z == 2)

    @pl.when(inner)
    def _():
        high, low = spread_out(corr_ref[...], planes)
        fields = (own_parts, pair_parts, third_parts, fourth_parts)
        limits = [
            [extent_ref[owner_of(place_ref, f) * orbs + a] for a in range(orbs)] for f in range(2)
        ]
        for c in range(grid_p // width):
            chunk = slice(c * width, (c + 1) * width)
            column = columns_of((planes, width)) + c * width
            change = projections(high, low, fields, chunk)
            density = jnp.zeros((planes, width), jnp.float32)
            for f, (field_ref, half_ref) in enumerate(((own_ref, image_ref), (pair_ref, ward_ref))):
                for a in range(orbs):
                    at = (f * orbs + a) * planes
                    phi = jnp.where(column < limits[f][a], field_ref[a, :, chunk], 0.0)
                    value = phi - step_length * half_ref[a, :, chunk] + change[at : at + planes]
                    density = density + value * value
            all_ref[:, chunk] = density * (1.0 / (4 * orbs))
        for k, part_ref in enumerate(out_ref):
            first = pl.multiple_of(jnp.bitwise_xor(z, k) * share, share)
            part_ref[...] = all_ref[:, pl.ds(first, share)]

    @pl.when(jnp.logical_not(inner))
    def _():
        for part_ref in out_ref:
            part_ref[...] = jnp.zeros_like(part_ref)


def update_kernel(
    own_ref, own_parts, pair_parts, third_in, third_out, fourth_in, fourth_out, image_ref,
    corr_ref, given_ref, extent_ref, place_ref, out_ref, third_parts, fourth_parts,
):
    orbs, planes, grid_p = own_ref.shape
    width = 2 * lanes
    z = place_ref[0]
    inner = (z == 1) | (z == 2)

    @pl.when(jnp.logical_not(inner))
    def _():
        split_into(third_parts, third_out, extent_ref, owner_of(place_ref, 2))
        split_into(fourth_parts, fourth_out, extent_ref, owner_of(place_ref, 3))

    def write(corr, fields):
        high, low = spread_out(corr, planes)
        for c in range(grid_p // width):
            chunk = slice(c * width, (c + 1) * width)
            column = columns_of((planes, width)) + c * width
            change = projections(high, low, fields, chunk)
            for a in range(orbs):
                phi = jnp.where(column < extent_ref[z * orbs + a], own_ref[a, :, chunk], 0.0)
                out_ref[a, :, chunk] = (
                    phi
                    - step_length * image_ref[a, :, chunk]
                    + change[a * planes : (a + 1) * planes]
                )

    @pl.when(inner)
    def _():
        write(corr_ref[:, :orbs], (own_parts, pair_parts, third_in, fourth_in))

    @pl.when(jnp.logical_not(inner))
    def _():
        corr = given_ref[:, orbs:]
        corr = jnp.concatenate([corr[orbs : 2 * orbs], corr[:orbs], corr[2 * orbs :]], axis=0)
        write(corr, (own_parts, pair_parts, third_parts, fourth_parts))


def call(kernel, out_shape, specs, scratch=()):
    return pl.pallas_call(
        kernel,
        out_shape=out_shape,
        in_specs=[in_smem() if spec == "s" else in_vmem() for spec in specs],
        out_specs=jax.tree.map(lambda _: in_vmem(), out_shape),
        scratch_shapes=list(scratch),
        compiler_params=pltpu.CompilerParams(vmem_limit_bytes=10 * 2**20),
        cost_estimate=pl.CostEstimate(flops=1, bytes_accessed=1, transcendentals=0),
    )


def line_device(psi, potential, extent):
    orbs, planes, grid_p = psi.shape
    n_cmp = lax.axis_size("cmp")
    rows = orbs * planes
    cells = planes * n_cmp * grid_p
    z = lax.axis_index("orb")
    place = jnp.stack([z, lax.axis_index("cmp") % 2])
    swap = [(0, 1), (1, 0), (2, 3), (3, 2)]
    across = [(1, 2), (2, 1)]
    outward = [(1, 0), (2, 3)]
    to_near = [(i, i ^ 1) for i in range(n_cmp)]
    to_far = [(i, i ^ 3) for i in range(n_cmp)]

    block = jax.ShapeDtypeStruct(psi.shape, jnp.float32)
    parts = jax.ShapeDtypeStruct((2 * rows, grid_p), jnp.bfloat16)
    field = pltpu.VMEM((rows, grid_p), jnp.float32)
    columns = jnp.asarray(column_band())
    bands = jnp.asarray(plane_bands(planes))

    pair = lax.ppermute(psi, "orb", swap)
    third = lax.ppermute(psi, "orb", across)
    far = lax.ppermute(psi, "cmp", to_far)
    near = lax.ppermute(psi, "cmp", to_near)

    local, own_parts = call(functools.partial(local_kernel, 0), (block, parts), "vvssv", [field])(
        psi, potential, extent, place, columns
    )
    pair, local, own_parts = lax.optimization_barrier((pair, local, own_parts))
    pair_far = lax.ppermute(pair, "cmp", to_far)
    pair_near = lax.ppermute(pair, "cmp", to_near)
    fourth = lax.ppermute(pair, "orb", across)
    third_out = lax.ppermute(third, "orb", outward)

    image, image_parts = call(functools.partial(plane_kernel, 0), (block, parts), "vvvvssv")(
        far, psi, near, local, extent, place, bands
    )
    ward_local, pair_parts = call(
        functools.partial(local_kernel, 1), (block, parts), "vvssv", [field]
    )(pair, potential, extent, place, columns)
    third_parts = call(functools.partial(split_kernel, 2), parts, "vss")(third, extent, place)
    early = call(
        functools.partial(overlap_kernel, planes, 3),
        jax.ShapeDtypeStruct((3 * orbs, rows), jnp.float32),
        "vvvv",
    )(own_parts, pair_parts, third_parts, image_parts)

    fourth, ward_local, early = lax.optimization_barrier((fourth, ward_local, early))
    ward, ward_parts = call(functools.partial(plane_kernel, 1), (block, parts), "vvvvssv")(
        pair_far, pair, pair_near, ward_local, extent, place, bands
    )
    fourth_out = lax.ppermute(fourth, "orb", outward)
    fourth_parts = call(functools.partial(split_kernel, 3), parts, "vss")(fourth, extent, place)
    part = call(
        functools.partial(correlation_kernel, planes, 1.0 / cells),
        jax.ShapeDtypeStruct((4 * orbs, 2 * orbs), jnp.float32),
        "vvvvvvv",
    )(own_parts, pair_parts, third_parts, fourth_parts, image_parts, ward_parts, early)
    shares = [lax.ppermute(part, "cmp", [(i, i ^ k) for i in range(n_cmp)]) for k in (1, 2, 3)]
    correlation = call(sum_kernel, jax.ShapeDtypeStruct(part.shape, jnp.float32), "vvvv")(
        part, *shares
    )
    correlation, third_out = lax.optimization_barrier((correlation, third_out))
    given = lax.ppermute(correlation, "orb", outward)

    share = jax.ShapeDtypeStruct((planes, grid_p // 4), jnp.float32)
    pieces = call(
        density_kernel, [share] * 4, "vvvvvvvvvss", [pltpu.VMEM((planes, grid_p), jnp.float32)]
    )(
        psi, pair, own_parts, pair_parts, third_parts, fourth_parts, image, ward, correlation,
        extent, place,
    )
    sent = [
        lax.ppermute(pieces[1], "orb", outward),
        lax.ppermute(pieces[2], "orb", [(1, 3), (2, 0)]),
        lax.ppermute(pieces[3], "orb", across),
    ]

    psi_new = call(
        update_kernel, block, "vvvvvvvvvvss", [pltpu.VMEM(parts.shape, parts.dtype)] * 2
    )(
        psi, own_parts, pair_parts, third_parts, third_out, fourth_parts, fourth_out, image,
        correlation, given, extent, place,
    )
    density = call(sum_kernel, share, "vvvv")(pieces[0], *sent)
    return (psi_new, density)


def per_device(psi, potential, extent):
    orbs, planes, grid_p = psi.shape
    fits = (
        lax.axis_size("orb") == 4
        and lax.axis_size("cmp") == 4
        and orbs == 8
        and planes == 16
        and grid_p % (4 * lanes) == 0
    )
    return (line_device if fits else general_device)(psi, potential, extent)


def solution(mesh):
    return jax.shard_map(
        per_device,
        mesh=mesh,
        in_specs=(P(("grp", "orb"), "cmp", None), P(("grp", "cmp"), None), P("grp")),
        out_specs=(P(("grp", "orb"), "cmp", None), P(("grp", "cmp"), "orb")),
        check_vma=False,
    )
```

```python
import functools
import math

import jax
import jax.numpy as jnp
import numpy as np
from jax import lax
from jax.experimental import pallas as pl
from jax.experimental.pallas import tpu as pltpu
from jax.sharding import PartitionSpec as P

step_length = 0.2
reach = 14
lanes = 128


def padded_2(cells, sides, width):
    for axis, dim in sides:
        count = lax.axis_size(axis)
        head = lax.slice_in_dim(cells, 0, width, axis=dim)
        tail = lax.slice_in_dim(cells, cells.shape[dim] - width, cells.shape[dim], axis=dim)
        cells = jnp.concatenate(
            [
                lax.ppermute(tail, axis, [(i, (i + 1) % count) for i in range(count)]),
                cells,
                lax.ppermute(head, axis, [((i + 1) % count, i) for i in range(count)]),
            ],
            axis=dim,
        )
    return cells


def band_matrix(length):
    rows = lax.broadcasted_iota(jnp.int32, (length + 2 * reach, length), 0)
    cols = lax.broadcasted_iota(jnp.int32, (length + 2 * reach, length), 1)
    spread = jnp.abs(rows - reach - cols)
    safe = jnp.maximum(spread, 1).astype(jnp.float32)
    signed = jnp.where(spread % 2 == 1, 2.0, -2.0) / (safe * safe)
    value = jnp.where(spread == 0, -math.pi**2 / 3.0, signed)
    return jnp.where(spread <= reach, value, 0.0)


def across_planes(padded, planes):
    return jnp.einsum("awp,wy->ayp", padded, band_matrix(planes), precision=lax.Precision.HIGHEST)


def along_grid(field):
    orbs, planes, grid_p = field.shape
    width = 128
    blocks = field.reshape(orbs, planes, grid_p // width, width)
    before = jnp.roll(blocks[..., width - reach :], 1, axis=2)
    after = jnp.roll(blocks[..., :reach], -1, axis=2)
    window = jnp.concatenate([before, blocks, after], axis=3)
    result = jnp.einsum(
        "axnw,wq->axnq", window, band_matrix(width), precision=lax.Precision.HIGHEST
    )
    return result.reshape(orbs, planes, grid_p)


def general_device(psi, potential, extent):
    orb_dev, planes, grid_p = psi.shape
    n_orb = lax.axis_size("orb")
    norbitals = orb_dev * n_orb
    cells = planes * lax.axis_size("cmp") * grid_p
    column = lax.broadcasted_iota(jnp.int32, (norbitals, grid_p), 1)
    live_all = (column < extent[:, None]).astype(jnp.float32)
    own_live = lax.dynamic_slice_in_dim(live_all, lax.axis_index("orb") * orb_dev, orb_dev, 0)
    phi = psi * own_live[:, None, :]
    padded = padded_2(phi, (("cmp", 1),), reach)
    kinetic = -0.5 * (across_planes(padded, planes) + along_grid(phi))
    hphi = own_live[:, None, :] * (kinetic + potential[None] * phi)
    phi_c, hphi_c = (
        lax.all_to_all(phi, "orb", split_axis=2, concat_axis=0, tiled=True),
        lax.all_to_all(hphi, "orb", split_axis=2, concat_axis=0, tiled=True),
    )
    flat_phi = phi_c.reshape(norbitals, -1)
    flat_h = hphi_c.reshape(norbitals, -1)
    partial_correlation = lax.dot_general(
        flat_phi,
        flat_h,
        (((1,), (1,)), ((), ())),
        precision=lax.Precision.HIGHEST,
        preferred_element_type=jnp.float32,
    )
    correlation = lax.psum(partial_correlation, ("orb", "cmp")) / cells
    grad_c = (flat_h - jnp.dot(correlation.T, flat_phi, precision=lax.Precision.HIGHEST)).reshape(
        phi_c.shape
    )
    grad = lax.all_to_all(grad_c, "orb", split_axis=0, concat_axis=2, tiled=True)
    psi_new = phi - step_length * grad
    density = (
        lax.psum_scatter(jnp.sum(psi_new * psi_new, axis=0), "orb", scatter_dimension=1, tiled=True)
        / norbitals
    )
    return (psi_new, density)


def weight(spread):
    spread = np.abs(spread)
    safe = np.maximum(spread, 1).astype(np.float64)
    value = np.where(spread % 2 == 1, 2.0, -2.0) / (safe * safe)
    value = np.where(spread == 0, -math.pi**2 / 3.0, value)
    return np.where(spread <= reach, value, 0.0).astype(np.float32)


def two_parts(value):
    high = value.astype(jnp.bfloat16)
    return high, (value - high.astype(np.float32)).astype(jnp.bfloat16)


def column_band():
    rows = np.arange(2 * lanes)[:, None]
    cols = np.arange(lanes)[None, :]
    high, low = two_parts(weight(rows - cols - reach))
    return np.concatenate([high, low], axis=1)


def plane_bands(planes):
    rows = np.arange(planes)[:, None]
    cols = np.arange(planes)[None, :]
    both = []
    for side in (-planes, planes):
        band = np.concatenate(
            [weight(cols + side - rows), weight(cols - rows), weight(cols - side - rows)], axis=1
        )
        high, low = two_parts(band)
        both.append(np.concatenate([high, high, low], axis=1))
    return np.stack(both)


def columns_of(shape):
    return lax.broadcasted_iota(jnp.int32, shape, len(shape) - 1)


def owner_of(place_ref, f):
    z = place_ref[0, 0]
    if f < 2:
        return z if f == 0 else jnp.where(z % 2 == 0, z + 1, z - 1)
    left, right = (2, 1) if f == 2 else (3, 0)
    return jnp.where(z < 2, left, right)


def masked(field_ref, a, extent_ref, owner):
    orbs, planes, grid_p = field_ref.shape
    column = columns_of((planes, grid_p))
    return jnp.where(column < extent_ref[owner * orbs + a], field_ref[a], 0.0)


def split_into(parts_ref, field_ref, extent_ref, owner):
    orbs, planes, _ = field_ref.shape
    for a in range(orbs):
        high, low = two_parts(masked(field_ref, a, extent_ref, owner))
        parts_ref[a * planes : (a + 1) * planes, :] = high
        parts_ref[(orbs + a) * planes : (orbs + a + 1) * planes, :] = low


def split_kernel(f, field_ref, extent_ref, place_ref, parts_ref):
    split_into(parts_ref, field_ref, extent_ref, owner_of(place_ref, f))


def local_kernel(f, psi_ref, potential_ref, extent_ref, place_ref, band_ref, out_ref, parts_ref, phi_ref):
    orbs, planes, grid_p = psi_ref.shape
    tiles = grid_p // lanes
    owner = owner_of(place_ref, f)
    for a in range(orbs):
        phi = masked(psi_ref, a, extent_ref, owner)
        phi_ref[a * planes : (a + 1) * planes, :] = phi
        high, low = two_parts(phi)
        parts_ref[a * planes : (a + 1) * planes, :] = high
        parts_ref[(orbs + a) * planes : (orbs + a + 1) * planes, :] = low
    high, low = two_parts(pltpu.roll(phi_ref[...], reach, 1))
    for t in range(tiles):
        here, after = t * lanes, (t + 1) % tiles * lanes
        high_t = jnp.concatenate([high[:, here : here + lanes], high[:, after : after + lanes]], 1)
        low_t = jnp.concatenate([low[:, here : here + lanes], low[:, after : after + lanes]], 1)
        both = jnp.dot(high_t, band_ref[...], preferred_element_type=jnp.float32)
        rest = jnp.dot(low_t, band_ref[:, :lanes], preferred_element_type=jnp.float32)
        second = both[:, :lanes] + both[:, lanes:] + rest
        field = phi_ref[:, here : here + lanes].reshape(orbs, planes, lanes)
        out_ref[:, :, here : here + lanes] = (
            potential_ref[:, here : here + lanes][None] * field
            - 0.5 * second.reshape(orbs, planes, lanes)
        )


def plane_kernel(
    f, far_ref, psi_ref, near_ref, local_ref, extent_ref, place_ref, band_ref, out_ref, parts_ref
):
    orbs, planes, grid_p = psi_ref.shape
    column = columns_of((planes, grid_p))
    owner = owner_of(place_ref, f)
    band = band_ref[place_ref[0, 1]]
    for a in range(orbs):
        slab = jnp.concatenate([far_ref[a], psi_ref[a], near_ref[a]], axis=0)
        high, low = two_parts(slab)
        second = jnp.dot(
            band, jnp.concatenate([high, low, high], axis=0), preferred_element_type=jnp.float32
        )
        image = jnp.where(
            column < extent_ref[owner * orbs + a], local_ref[a] - 0.5 * second, 0.0
        )
        out_ref[a] = image
        high, low = two_parts(image)
        parts_ref[a * planes : (a + 1) * planes, :] = high
        parts_ref[(orbs + a) * planes : (orbs + a + 1) * planes, :] = low


def overlaps(field_ref, image_ref, planes):
    half = field_ref.shape[0] // 2
    product = lax.dot_general(
        field_ref[...],
        image_ref[...],
        (((1,), (1,)), ((), ())),
        preferred_element_type=jnp.float32,
    )
    product = product[:half] + product[half:]
    product = product[:, :half] + product[:, half:]
    row = lax.broadcasted_iota(jnp.int32, (half, half), 0)
    col = lax.broadcasted_iota(jnp.int32, (half, half), 1)
    product = jnp.where(row % planes == col % planes, product, 0.0)
    return jnp.sum(product.reshape(half // planes, planes, half), axis=1)


def overlap_kernel(planes, n_fields, *refs):
    fields, image_ref, out_ref = refs[:n_fields], refs[n_fields], refs[n_fields + 1]
    for f, field_ref in enumerate(fields):
        value = overlaps(field_ref, image_ref, planes)
        out_ref[f * value.shape[0] : (f + 1) * value.shape[0], :] = value


def correlation_kernel(
    planes, scale, own_ref, pair_ref, third_ref, fourth_ref, image_ref, ward_ref, early_ref, out_ref
):
    half = own_ref.shape[0] // 2
    orbs = half // planes
    ward = [overlaps(ref, ward_ref, planes) for ref in (own_ref, pair_ref, third_ref, fourth_ref)]
    last = overlaps(fourth_ref, image_ref, planes)
    wide = jnp.concatenate(
        [jnp.concatenate([early_ref[...], last], axis=0), jnp.concatenate(ward, axis=0)], axis=1
    )
    row = lax.broadcasted_iota(jnp.int32, (2 * half, 2 * orbs), 0)
    col = lax.broadcasted_iota(jnp.int32, (2 * half, 2 * orbs), 1)
    gather = jnp.where(row // planes == col, scale, 0.0)
    out_ref[...] = jnp.dot(
        wide, gather, precision=lax.Precision.HIGHEST, preferred_element_type=jnp.float32
    )


def sum_kernel(*refs):
    rows = refs[-1].shape[0]
    total = refs[0][...]
    for ref in refs[1:-1]:
        total = total + ref[:rows, :]
    refs[-1][...] = total


def spread_out(corr, planes):
    n_a, n_b = corr.shape
    shift = planes.bit_length() - 1
    shape = (n_b * planes, n_a * planes)

    def iota(shape, dim):
        return lax.broadcasted_iota(jnp.int32, shape, dim)

    def ones_where(mask):
        return jnp.where(mask, 1.0, 0.0).astype(jnp.bfloat16)

    take_b = ones_where(
        jnp.right_shift(iota((shape[0], n_b), 0), shift) == iota((shape[0], n_b), 1)
    )
    take_a = ones_where(
        jnp.right_shift(iota((n_a, shape[1]), 1), shift) == iota((n_a, shape[1]), 0)
    )
    same_plane = (jnp.bitwise_xor(iota(shape, 0), iota(shape, 1)) & (planes - 1)) == 0

    def spread(part):
        rows = lax.dot_general(
            take_b, part, (((1,), (1,)), ((), ())), preferred_element_type=jnp.float32
        ).astype(jnp.bfloat16)
        full = jnp.dot(rows, take_a, preferred_element_type=jnp.float32)
        return jnp.where(same_plane, full, 0.0).astype(jnp.bfloat16)

    high, low = two_parts(corr * step_length)
    return spread(high), spread(low)


def projections(high, low, fields, chunk):
    half = fields[0].shape[0] // 2
    total = None
    for f in range(0, len(fields), 2):
        pair = fields[f : f + 2]
        terms = [
            (low[:, f * half : (f + 2) * half], jnp.concatenate([r[:half, chunk] for r in pair], 0))
        ]
        for g, field_ref in enumerate(pair):
            here = high[:, (f + g) * half : (f + g + 1) * half]
            terms.append((jnp.concatenate([here, here], axis=1), field_ref[:, chunk]))
        for left, right in terms:
            term = jnp.dot(left, right, preferred_element_type=jnp.float32)
            total = term if total is None else total + term
    return total


def step_kernel(
    own_ref, pair_ref, own_parts, pair_parts, third_parts, fourth_parts, image_ref, ward_ref,
    corr_ref, extent_ref, place_ref, kept_ref, out1_ref, out2_ref, out3_ref, new_ref, all_ref,
    own_new, sem,
):
    orbs, planes, grid_p = own_ref.shape
    width = 2 * lanes
    share = grid_p // 4
    z = place_ref[0, 0]
    inner = (z == 1) | (z == 2)

    @pl.when(inner)
    def _():
        out1_ref[planes:, : corr_ref.shape[1]] = corr_ref[...]
        high, low = spread_out(corr_ref[...], planes)
        fields = (own_parts, pair_parts, third_parts, fourth_parts)
        limits = [
            [extent_ref[owner_of(place_ref, f) * orbs + a] for a in range(orbs)] for f in range(2)
        ]
        for c in range(grid_p // width):
            chunk = slice(c * width, (c + 1) * width)
            column = columns_of((planes, width)) + c * width
            change = projections(high, low, fields, chunk)
            density = jnp.zeros((planes, width), jnp.float32)
            for f, (field_ref, half_ref) in enumerate(((own_ref, image_ref), (pair_ref, ward_ref))):
                for a in range(orbs):
                    at = (f * orbs + a) * planes
                    phi = jnp.where(column < limits[f][a], field_ref[a, :, chunk], 0.0)
                    value = phi - step_length * half_ref[a, :, chunk] + change[at : at + planes]
                    density = density + value * value
                    if f == 0:
                        own_new[a, :, chunk] = value
            all_ref[:, chunk] = density * (1.0 / (4 * orbs))
        copy = pltpu.make_async_copy(own_new, new_ref, sem)
        copy.start()
        for k, part_ref in enumerate((kept_ref, out1_ref, out2_ref, out3_ref)):
            first = pl.multiple_of(jnp.bitwise_xor(z, k) * share, share)
            part_ref[:planes, :] = all_ref[:, pl.ds(first, share)]
        copy.wait()

    @pl.when(jnp.logical_not(inner))
    def _():
        kept_ref[...] = jnp.zeros_like(kept_ref)


def outer_kernel(
    own_ref, own_parts, pair_parts, third_ref, fourth_ref, image_ref, given_ref, extent_ref,
    place_ref, old_ref, new_ref, third_parts, fourth_parts, own_new, sem,
):
    orbs, planes, grid_p = own_ref.shape
    width = 2 * lanes
    z = place_ref[0, 0]
    outer = (z == 0) | (z == 3)
    del old_ref

    @pl.when(outer)
    def _():
        split_into(third_parts, third_ref, extent_ref, owner_of(place_ref, 2))
        split_into(fourth_parts, fourth_ref, extent_ref, owner_of(place_ref, 3))
        corr = given_ref[planes:, orbs : 2 * orbs]
        corr = jnp.concatenate([corr[orbs : 2 * orbs], corr[:orbs], corr[2 * orbs :]], axis=0)
        high, low = spread_out(corr, planes)
        fields = (own_parts, pair_parts, third_parts, fourth_parts)
        for c in range(grid_p // width):
            chunk = slice(c * width, (c + 1) * width)
            column = columns_of((planes, width)) + c * width
            change = projections(high, low, fields, chunk)
            for a in range(orbs):
                phi = jnp.where(column < extent_ref[z * orbs + a], own_ref[a, :, chunk], 0.0)
                own_new[a, :, chunk] = (
                    phi
                    - step_length * image_ref[a, :, chunk]
                    + change[a * planes : (a + 1) * planes]
                )
        copy = pltpu.make_async_copy(own_new, new_ref, sem)
        copy.start()
        copy.wait()


def call(kernel, out_shape, specs, scratch=(), out_specs=None, aliases={}):
    kinds = {"s": pltpu.SMEM, "v": pltpu.VMEM, "a": pl.ANY}
    if out_specs is None:
        out_specs = "v" * len(jax.tree.leaves(out_shape))
    places = [pl.BlockSpec(memory_space=kinds[kind]) for kind in out_specs]
    return pl.pallas_call(
        kernel,
        out_shape=out_shape,
        in_specs=[pl.BlockSpec(memory_space=kinds[kind]) for kind in specs],
        out_specs=places if isinstance(out_shape, (tuple, list)) else places[0],
        scratch_shapes=list(scratch),
        input_output_aliases=aliases,
        compiler_params=pltpu.CompilerParams(vmem_limit_bytes=10 * 2**20),
        cost_estimate=pl.CostEstimate(flops=1, bytes_accessed=1, transcendentals=0),
    )


def line_device(psi, potential, extent):
    orbs, planes, grid_p = psi.shape
    n_cmp = lax.axis_size("cmp")
    rows = orbs * planes
    cells = planes * n_cmp * grid_p
    z = lax.axis_index("orb")
    place = jnp.stack([z, lax.axis_index("cmp") % 2]).reshape(1, 2)
    swap = [(0, 1), (1, 0), (2, 3), (3, 2)]
    across = [(1, 2), (2, 1)]
    outward = [(1, 0), (2, 3)]
    to_near = [(i, i ^ 1) for i in range(n_cmp)]
    to_far = [(i, i ^ 3) for i in range(n_cmp)]

    block = jax.ShapeDtypeStruct(psi.shape, jnp.float32)
    parts = jax.ShapeDtypeStruct((2 * rows, grid_p), jnp.bfloat16)
    field = pltpu.VMEM((rows, grid_p), jnp.float32)
    columns = jnp.asarray(column_band())
    bands = jnp.asarray(plane_bands(planes))

    pair = lax.ppermute(psi, "orb", swap)
    third = lax.ppermute(psi, "orb", across)
    place = call(sum_kernel, jax.ShapeDtypeStruct(place.shape, place.dtype), "v")(place)
    slab, place = lax.optimization_barrier((psi, place))
    near = lax.ppermute(slab, "cmp", to_near)
    far = lax.ppermute(slab, "cmp", to_far)

    local, own_parts = call(functools.partial(local_kernel, 0), (block, parts), "vvssv", [field])(
        psi, potential, extent, place, columns
    )
    pair, local, own_parts = lax.optimization_barrier((pair, local, own_parts))
    pair_far = lax.ppermute(pair, "cmp", to_far)
    pair_near = lax.ppermute(pair, "cmp", to_near)
    fourth = lax.ppermute(pair, "orb", across)
    third_out = lax.ppermute(third, "orb", outward)

    image, image_parts = call(functools.partial(plane_kernel, 0), (block, parts), "vvvvssv")(
        far, psi, near, local, extent, place, bands
    )
    ward_local, pair_parts = call(
        functools.partial(local_kernel, 1), (block, parts), "vvssv", [field]
    )(pair, potential, extent, place, columns)
    third_parts = call(functools.partial(split_kernel, 2), parts, "vss")(third, extent, place)
    early = call(
        functools.partial(overlap_kernel, planes, 3),
        jax.ShapeDtypeStruct((3 * orbs, rows), jnp.float32),
        "vvvv",
    )(own_parts, pair_parts, third_parts, image_parts)

    fourth, ward_local, early = lax.optimization_barrier((fourth, ward_local, early))
    ward, ward_parts = call(functools.partial(plane_kernel, 1), (block, parts), "vvvvssv")(
        pair_far, pair, pair_near, ward_local, extent, place, bands
    )
    fourth_out = lax.ppermute(fourth, "orb", outward)
    fourth_parts = call(functools.partial(split_kernel, 3), parts, "vss")(fourth, extent, place)
    part = call(
        functools.partial(correlation_kernel, planes, 1.0 / cells),
        jax.ShapeDtypeStruct((4 * orbs, 2 * orbs), jnp.float32),
        "vvvvvvv",
    )(own_parts, pair_parts, third_parts, fourth_parts, image_parts, ward_parts, early)
    shares = [lax.ppermute(part, "cmp", [(i, i ^ k) for i in range(n_cmp)]) for k in (1, 2, 3)]
    correlation = call(sum_kernel, jax.ShapeDtypeStruct(part.shape, jnp.float32), "vvvv")(
        part, *shares
    )
    correlation, third_out = lax.optimization_barrier((correlation, third_out))

    share = jax.ShapeDtypeStruct((planes, grid_p // 4), jnp.float32)
    wide = jax.ShapeDtypeStruct((planes + 4 * orbs, grid_p // 4), jnp.float32)
    *pieces, new = call(
        step_kernel,
        [share, wide, share, share, block],
        "vvvvvvvvvss",
        [
            pltpu.VMEM((planes, grid_p), jnp.float32),
            pltpu.VMEM(block.shape, jnp.float32),
            pltpu.SemaphoreType.DMA,
        ],
        "vvvva",
    )(
        psi, pair, own_parts, pair_parts, third_parts, fourth_parts, image, ward, correlation,
        extent, place,
    )
    given = lax.ppermute(pieces[1], "orb", outward)
    sent = [
        lax.ppermute(pieces[2], "orb", [(1, 3), (2, 0)]),
        lax.ppermute(pieces[3], "orb", across),
    ]
    new = call(
        outer_kernel,
        block,
        "vvvvvvvssa",
        [pltpu.VMEM(parts.shape, parts.dtype)] * 2
        + [pltpu.VMEM(block.shape, jnp.float32), pltpu.SemaphoreType.DMA],
        "a",
        {9: 0},
    )(
        psi, own_parts, pair_parts, third_out, fourth_out, image, given, extent, place, new
    )
    sent, kept = lax.optimization_barrier((sent, pieces[0], new))[:2]
    density = call(sum_kernel, share, "vvvv")(kept, *sent, given)
    return (new, density)


def per_device(psi, potential, extent):
    orbs, planes, grid_p = psi.shape
    fits = (
        lax.axis_size("orb") == 4
        and lax.axis_size("cmp") == 4
        and orbs == 8
        and planes == 16
        and grid_p % (4 * lanes) == 0
    )
    return (line_device if fits else general_device)(psi, potential, extent)


def solution(mesh):
    return jax.shard_map(
        per_device,
        mesh=mesh,
        in_specs=(P(("grp", "orb"), "cmp", None), P(("grp", "cmp"), None), P("grp")),
        out_specs=(P(("grp", "orb"), "cmp", None), P(("grp", "cmp"), "orb")),
        check_vma=False,
    )
```

```python
import functools
import math

import jax
import jax.numpy as jnp
import numpy as np
from jax import lax
from jax.experimental import pallas as pl
from jax.experimental.pallas import tpu as pltpu
from jax.sharding import PartitionSpec as P

step_length = 0.2
reach = 14
lanes = 128


def padded_2(cells, sides, width):
    for axis, dim in sides:
        count = lax.axis_size(axis)
        head = lax.slice_in_dim(cells, 0, width, axis=dim)
        tail = lax.slice_in_dim(cells, cells.shape[dim] - width, cells.shape[dim], axis=dim)
        cells = jnp.concatenate(
            [
                lax.ppermute(tail, axis, [(i, (i + 1) % count) for i in range(count)]),
                cells,
                lax.ppermute(head, axis, [((i + 1) % count, i) for i in range(count)]),
            ],
            axis=dim,
        )
    return cells


def band_matrix(length):
    rows = lax.broadcasted_iota(jnp.int32, (length + 2 * reach, length), 0)
    cols = lax.broadcasted_iota(jnp.int32, (length + 2 * reach, length), 1)
    spread = jnp.abs(rows - reach - cols)
    safe = jnp.maximum(spread, 1).astype(jnp.float32)
    signed = jnp.where(spread % 2 == 1, 2.0, -2.0) / (safe * safe)
    value = jnp.where(spread == 0, -math.pi**2 / 3.0, signed)
    return jnp.where(spread <= reach, value, 0.0)


def across_planes(padded, planes):
    return jnp.einsum("awp,wy->ayp", padded, band_matrix(planes), precision=lax.Precision.HIGHEST)


def along_grid(field):
    orbs, planes, grid_p = field.shape
    width = 128
    blocks = field.reshape(orbs, planes, grid_p // width, width)
    before = jnp.roll(blocks[..., width - reach :], 1, axis=2)
    after = jnp.roll(blocks[..., :reach], -1, axis=2)
    window = jnp.concatenate([before, blocks, after], axis=3)
    result = jnp.einsum(
        "axnw,wq->axnq", window, band_matrix(width), precision=lax.Precision.HIGHEST
    )
    return result.reshape(orbs, planes, grid_p)


def general_device(psi, potential, extent):
    orb_dev, planes, grid_p = psi.shape
    n_orb = lax.axis_size("orb")
    norbitals = orb_dev * n_orb
    cells = planes * lax.axis_size("cmp") * grid_p
    column = lax.broadcasted_iota(jnp.int32, (norbitals, grid_p), 1)
    live_all = (column < extent[:, None]).astype(jnp.float32)
    own_live = lax.dynamic_slice_in_dim(live_all, lax.axis_index("orb") * orb_dev, orb_dev, 0)
    phi = psi * own_live[:, None, :]
    padded = padded_2(phi, (("cmp", 1),), reach)
    kinetic = -0.5 * (across_planes(padded, planes) + along_grid(phi))
    hphi = own_live[:, None, :] * (kinetic + potential[None] * phi)
    phi_c, hphi_c = (
        lax.all_to_all(phi, "orb", split_axis=2, concat_axis=0, tiled=True),
        lax.all_to_all(hphi, "orb", split_axis=2, concat_axis=0, tiled=True),
    )
    flat_phi = phi_c.reshape(norbitals, -1)
    flat_h = hphi_c.reshape(norbitals, -1)
    partial_correlation = lax.dot_general(
        flat_phi,
        flat_h,
        (((1,), (1,)), ((), ())),
        precision=lax.Precision.HIGHEST,
        preferred_element_type=jnp.float32,
    )
    correlation = lax.psum(partial_correlation, ("orb", "cmp")) / cells
    grad_c = (flat_h - jnp.dot(correlation.T, flat_phi, precision=lax.Precision.HIGHEST)).reshape(
        phi_c.shape
    )
    grad = lax.all_to_all(grad_c, "orb", split_axis=0, concat_axis=2, tiled=True)
    psi_new = phi - step_length * grad
    density = (
        lax.psum_scatter(jnp.sum(psi_new * psi_new, axis=0), "orb", scatter_dimension=1, tiled=True)
        / norbitals
    )
    return (psi_new, density)


def weight(spread):
    spread = np.abs(spread)
    safe = np.maximum(spread, 1).astype(np.float64)
    value = np.where(spread % 2 == 1, 2.0, -2.0) / (safe * safe)
    value = np.where(spread == 0, -math.pi**2 / 3.0, value)
    return np.where(spread <= reach, value, 0.0).astype(np.float32)


def two_parts(value):
    high = value.astype(jnp.bfloat16)
    return high, (value - high.astype(np.float32)).astype(jnp.bfloat16)


def column_band():
    rows = np.arange(2 * lanes)[:, None]
    cols = np.arange(lanes)[None, :]
    high, low = two_parts(weight(rows - cols - reach))
    return np.concatenate([high, low], axis=1)


def plane_bands(planes):
    rows = np.arange(planes)[:, None]
    cols = np.arange(planes)[None, :]
    both = []
    for side in (-planes, planes):
        band = np.concatenate(
            [weight(cols + side - rows), weight(cols - rows), weight(cols - side - rows)], axis=1
        )
        high, low = two_parts(band)
        both.append(np.concatenate([high, high, low], axis=1))
    return np.stack(both)


def columns_kernel(out_ref):
    out_ref[...] = lax.broadcasted_iota(jnp.int32, out_ref.shape, 1)


def owner_of(f):
    z = lax.axis_index("orb")
    if f < 2:
        return z if f == 0 else jnp.where(z % 2 == 0, z + 1, z - 1)
    left, right = (2, 1) if f == 2 else (3, 0)
    return jnp.where(z < 2, left, right)


def on_inner():
    z = lax.axis_index("orb")
    return (z == 1) | (z == 2)


def live_kernel(columns_ref, extent_ref, out_ref):
    orbs = out_ref.shape[0] // 4
    for f in range(4):
        owner = owner_of(f)
        for a in range(orbs):
            row = jnp.where(columns_ref[:1, :] < extent_ref[owner * orbs + a], 1.0, 0.0)
            out_ref[f * orbs + a : f * orbs + a + 1, :] = row


def masked(field_ref, a, live_ref, f):
    at = f * field_ref.shape[0] + a
    return field_ref[a] * live_ref[at : at + 1, :]


def split_into(parts_ref, field_ref, live_ref, f):
    orbs, planes, _ = field_ref.shape
    for a in range(orbs):
        high, low = two_parts(masked(field_ref, a, live_ref, f))
        parts_ref[a * planes : (a + 1) * planes, :] = high
        parts_ref[(orbs + a) * planes : (orbs + a + 1) * planes, :] = low


def split_kernel(f, field_ref, live_ref, parts_ref):
    split_into(parts_ref, field_ref, live_ref, f)


def local_kernel(f, psi_ref, potential_ref, live_ref, band_ref, out_ref, parts_ref, phi_ref):
    orbs, planes, grid_p = psi_ref.shape
    tiles = grid_p // lanes
    for a in range(orbs):
        phi = masked(psi_ref, a, live_ref, f)
        phi_ref[a * planes : (a + 1) * planes, :] = phi
        high, low = two_parts(phi)
        parts_ref[a * planes : (a + 1) * planes, :] = high
        parts_ref[(orbs + a) * planes : (orbs + a + 1) * planes, :] = low
    high, low = two_parts(pltpu.roll(phi_ref[...], reach, 1))
    for t in range(tiles):
        here, after = t * lanes, (t + 1) % tiles * lanes
        high_t = jnp.concatenate([high[:, here : here + lanes], high[:, after : after + lanes]], 1)
        low_t = jnp.concatenate([low[:, here : here + lanes], low[:, after : after + lanes]], 1)
        both = jnp.dot(high_t, band_ref[...], preferred_element_type=jnp.float32)
        rest = jnp.dot(low_t, band_ref[:, :lanes], preferred_element_type=jnp.float32)
        second = both[:, :lanes] + both[:, lanes:] + rest
        field = phi_ref[:, here : here + lanes].reshape(orbs, planes, lanes)
        out_ref[:, :, here : here + lanes] = (
            potential_ref[:, here : here + lanes][None] * field
            - 0.5 * second.reshape(orbs, planes, lanes)
        )


def plane_kernel(
    f, far_ref, psi_ref, near_ref, local_ref, live_ref, band_ref, out_ref, parts_ref
):
    orbs, planes, _ = psi_ref.shape
    band = band_ref[lax.axis_index("cmp") % 2]
    for a in range(orbs):
        slab = jnp.concatenate([far_ref[a], psi_ref[a], near_ref[a]], axis=0)
        high, low = two_parts(slab)
        second = jnp.dot(
            band, jnp.concatenate([high, low, high], axis=0), preferred_element_type=jnp.float32
        )
        image = (local_ref[a] - 0.5 * second) * live_ref[f * orbs + a : f * orbs + a + 1, :]
        out_ref[a] = image
        high, low = two_parts(image)
        parts_ref[a * planes : (a + 1) * planes, :] = high
        parts_ref[(orbs + a) * planes : (orbs + a + 1) * planes, :] = low


def overlaps(field_ref, image_ref, planes):
    half = field_ref.shape[0] // 2
    product = lax.dot_general(
        field_ref[...],
        image_ref[...],
        (((1,), (1,)), ((), ())),
        preferred_element_type=jnp.float32,
    )
    product = product[:half] + product[half:]
    product = product[:, :half] + product[:, half:]
    row = lax.broadcasted_iota(jnp.int32, (half, half), 0)
    col = lax.broadcasted_iota(jnp.int32, (half, half), 1)
    product = jnp.where(row % planes == col % planes, product, 0.0)
    return jnp.sum(product.reshape(half // planes, planes, half), axis=1)


def overlap_kernel(planes, n_fields, *refs):
    fields, image_ref, out_ref = refs[:n_fields], refs[n_fields], refs[n_fields + 1]
    for f, field_ref in enumerate(fields):
        value = overlaps(field_ref, image_ref, planes)
        out_ref[f * value.shape[0] : (f + 1) * value.shape[0], :] = value


def correlation_kernel(
    planes, scale, own_ref, pair_ref, third_ref, fourth_ref, image_ref, ward_ref, early_ref, out_ref
):
    half = own_ref.shape[0] // 2
    orbs = half // planes
    ward = [overlaps(ref, ward_ref, planes) for ref in (own_ref, pair_ref, third_ref, fourth_ref)]
    last = overlaps(fourth_ref, image_ref, planes)
    wide = jnp.concatenate(
        [jnp.concatenate([early_ref[...], last], axis=0), jnp.concatenate(ward, axis=0)], axis=1
    )
    row = lax.broadcasted_iota(jnp.int32, (2 * half, 2 * orbs), 0)
    col = lax.broadcasted_iota(jnp.int32, (2 * half, 2 * orbs), 1)
    gather = jnp.where(row // planes == col, scale, 0.0)
    out_ref[...] = jnp.dot(
        wide, gather, precision=lax.Precision.HIGHEST, preferred_element_type=jnp.float32
    )


def sum_kernel(*refs):
    rows = refs[-1].shape[0]
    total = refs[0][...]
    for ref in refs[1:-1]:
        total = total + ref[:rows, :]
    refs[-1][...] = total


def spread_out(corr, planes):
    n_a, n_b = corr.shape
    shift = planes.bit_length() - 1
    shape = (n_b * planes, n_a * planes)

    def iota(shape, dim):
        return lax.broadcasted_iota(jnp.int32, shape, dim)

    def ones_where(mask):
        return jnp.where(mask, 1.0, 0.0).astype(jnp.bfloat16)

    take_b = ones_where(
        jnp.right_shift(iota((shape[0], n_b), 0), shift) == iota((shape[0], n_b), 1)
    )
    take_a = ones_where(
        jnp.right_shift(iota((n_a, shape[1]), 1), shift) == iota((n_a, shape[1]), 0)
    )
    same_plane = (jnp.bitwise_xor(iota(shape, 0), iota(shape, 1)) & (planes - 1)) == 0

    def spread(part):
        rows = lax.dot_general(
            take_b, part, (((1,), (1,)), ((), ())), preferred_element_type=jnp.float32
        ).astype(jnp.bfloat16)
        full = jnp.dot(rows, take_a, preferred_element_type=jnp.float32)
        return jnp.where(same_plane, full, 0.0).astype(jnp.bfloat16)

    high, low = two_parts(corr * step_length)
    return spread(high), spread(low)


def projections(high, low, fields, chunk):
    half = fields[0].shape[0] // 2
    total = None
    for f in range(0, len(fields), 2):
        pair = fields[f : f + 2]
        terms = [
            (low[:, f * half : (f + 2) * half], jnp.concatenate([r[:half, chunk] for r in pair], 0))
        ]
        for g, field_ref in enumerate(pair):
            here = high[:, (f + g) * half : (f + g + 1) * half]
            terms.append((jnp.concatenate([here, here], axis=1), field_ref[:, chunk]))
        for left, right in terms:
            term = jnp.dot(left, right, preferred_element_type=jnp.float32)
            total = term if total is None else total + term
    return total


def step_kernel(
    own_phi, pair_phi, own_parts, pair_parts, third_parts, fourth_parts, image_ref, ward_ref,
    corr_ref, kept_ref, out1_ref, out2_ref, out3_ref, new_ref, all_ref,
):
    orbs, planes, grid_p = image_ref.shape
    width = 2 * lanes
    share = grid_p // 4

    @pl.when(on_inner())
    def _():
        out1_ref[planes:, : corr_ref.shape[1]] = corr_ref[...]
        high, low = spread_out(corr_ref[...], planes)
        fields = (own_parts, pair_parts, third_parts, fourth_parts)
        for c in range(grid_p // width):
            chunk = slice(c * width, (c + 1) * width)
            change = projections(high, low, fields, chunk)
            density = jnp.zeros((planes, width), jnp.float32)
            for f, (phi_ref, half_ref) in enumerate(((own_phi, image_ref), (pair_phi, ward_ref))):
                for a in range(orbs):
                    at = (f * orbs + a) * planes
                    value = (
                        phi_ref[a * planes : (a + 1) * planes, chunk]
                        - step_length * half_ref[a, :, chunk]
                        + change[at : at + planes]
                    )
                    density = density + value * value
                    if f == 0:
                        new_ref[a, :, chunk] = value
            all_ref[:, chunk] = density * (1.0 / (4 * orbs))
        for k, part_ref in enumerate((kept_ref, out1_ref, out2_ref, out3_ref)):
            first = pl.multiple_of(jnp.bitwise_xor(lax.axis_index("orb"), k) * share, share)
            part_ref[:planes, :] = all_ref[:, pl.ds(first, share)]


def outer_split_kernel(third_ref, fourth_ref, live_ref, third_parts, fourth_parts):
    @pl.when(jnp.logical_not(on_inner()))
    def _():
        split_into(third_parts, third_ref, live_ref, 2)
        split_into(fourth_parts, fourth_ref, live_ref, 3)


def last_kernel(
    own_phi, own_parts, pair_parts, third_parts, fourth_parts, image_ref, given_ref, kept_ref,
    sent2_ref, sent3_ref, inner_new, new_ref, density_ref, own_new, own_density, sems,
):
    orbs, planes, grid_p = image_ref.shape
    width = 2 * lanes

    def write(values_ref):
        copies = [
            pltpu.make_async_copy(values_ref, new_ref, sems.at[0]),
            pltpu.make_async_copy(own_density, density_ref, sems.at[1]),
        ]
        for copy in copies:
            copy.start()
        for copy in copies:
            copy.wait()

    @pl.when(on_inner())
    def _():
        own_density[...] = kept_ref[...] + sent3_ref[...]
        write(inner_new)

    @pl.when(jnp.logical_not(on_inner()))
    def _():
        own_density[...] = given_ref[:planes] + sent2_ref[...]
        corr = given_ref[planes:, orbs : 2 * orbs]
        corr = jnp.concatenate([corr[orbs : 2 * orbs], corr[:orbs], corr[2 * orbs :]], axis=0)
        high, low = spread_out(corr, planes)
        fields = (own_parts, pair_parts, third_parts, fourth_parts)
        for c in range(grid_p // width):
            chunk = slice(c * width, (c + 1) * width)
            change = projections(high, low, fields, chunk)
            for a in range(orbs):
                at = slice(a * planes, (a + 1) * planes)
                own_new[a, :, chunk] = (
                    own_phi[at, chunk] - step_length * image_ref[a, :, chunk] + change[at]
                )
        write(own_new)


def call(kernel, out_shape, specs, scratch=(), out_specs=None):
    kinds = {"s": pltpu.SMEM, "v": pltpu.VMEM, "a": pl.ANY}
    if out_specs is None:
        out_specs = "v" * len(jax.tree.leaves(out_shape))
    places = [pl.BlockSpec(memory_space=kinds[kind]) for kind in out_specs]
    return pl.pallas_call(
        kernel,
        out_shape=out_shape,
        in_specs=[pl.BlockSpec(memory_space=kinds[kind]) for kind in specs],
        out_specs=places if isinstance(out_shape, (tuple, list)) else places[0],
        scratch_shapes=list(scratch),
        compiler_params=pltpu.CompilerParams(vmem_limit_bytes=10 * 2**20),
        cost_estimate=pl.CostEstimate(flops=1, bytes_accessed=1, transcendentals=0),
    )


def line_device(psi, potential, extent):
    orbs, planes, grid_p = psi.shape
    n_cmp = lax.axis_size("cmp")
    rows = orbs * planes
    cells = planes * n_cmp * grid_p
    swap = [(0, 1), (1, 0), (2, 3), (3, 2)]
    across = [(1, 2), (2, 1), (0, 0), (3, 3)]
    to_near = [(i, i ^ 1) for i in range(n_cmp)]
    to_far = [(i, i ^ 3) for i in range(n_cmp)]

    block = jax.ShapeDtypeStruct(psi.shape, jnp.float32)
    parts = jax.ShapeDtypeStruct((2 * rows, grid_p), jnp.bfloat16)
    flat = jax.ShapeDtypeStruct((rows, grid_p), jnp.float32)
    columns = jnp.asarray(column_band())
    bands = jnp.asarray(plane_bands(planes))

    pair = lax.ppermute(psi, "orb", swap)
    third = lax.ppermute(psi, "orb", across)
    grid = call(columns_kernel, jax.ShapeDtypeStruct((8, grid_p), jnp.int32), "")()
    slab, grid = lax.optimization_barrier((psi, grid))
    near = lax.ppermute(slab, "cmp", to_near)
    far = lax.ppermute(slab, "cmp", to_far)

    live = call(live_kernel, jax.ShapeDtypeStruct((4 * orbs, grid_p), jnp.float32), "vs")(
        grid, extent
    )
    local, own_parts, own_phi = call(
        functools.partial(local_kernel, 0), (block, parts, flat), "vvvv"
    )(psi, potential, live, columns)
    pair, local, own_parts = lax.optimization_barrier((pair, local, own_parts))
    pair_far = lax.ppermute(pair, "cmp", to_far)
    pair_near = lax.ppermute(pair, "cmp", to_near)
    fourth = lax.ppermute(pair, "orb", across)
    third_out = lax.ppermute(third, "orb", swap)

    image, image_parts = call(functools.partial(plane_kernel, 0), (block, parts), "vvvvvv")(
        far, psi, near, local, live, bands
    )
    ward_local, pair_parts, pair_phi = call(
        functools.partial(local_kernel, 1), (block, parts, flat), "vvvv"
    )(pair, potential, live, columns)
    third_parts = call(functools.partial(split_kernel, 2), parts, "vv")(third, live)
    early = call(
        functools.partial(overlap_kernel, planes, 3),
        jax.ShapeDtypeStruct((3 * orbs, rows), jnp.float32),
        "vvvv",
    )(own_parts, pair_parts, third_parts, image_parts)

    fourth, ward_local, early = lax.optimization_barrier((fourth, ward_local, early))
    fourth_out = lax.ppermute(fourth, "orb", swap)
    ward, ward_parts = call(functools.partial(plane_kernel, 1), (block, parts), "vvvvvv")(
        pair_far, pair, pair_near, ward_local, live, bands
    )
    fourth_parts = call(functools.partial(split_kernel, 3), parts, "vv")(fourth, live)
    part = call(
        functools.partial(correlation_kernel, planes, 1.0 / cells),
        jax.ShapeDtypeStruct((4 * orbs, 2 * orbs), jnp.float32),
        "vvvvvvv",
    )(own_parts, pair_parts, third_parts, fourth_parts, image_parts, ward_parts, early)
    shares = [lax.ppermute(part, "cmp", [(i, i ^ k) for i in range(n_cmp)]) for k in (1, 2, 3)]
    correlation = call(sum_kernel, jax.ShapeDtypeStruct(part.shape, jnp.float32), "vvvv")(
        part, *shares
    )
    correlation, third_out = lax.optimization_barrier((correlation, third_out))

    share = jax.ShapeDtypeStruct((planes, grid_p // 4), jnp.float32)
    wide = jax.ShapeDtypeStruct((planes + 4 * orbs, grid_p // 4), jnp.float32)
    kept, first, second, last, inner_new = call(
        step_kernel,
        [share, wide, share, share, block],
        "vvvvvvvvv",
        [pltpu.VMEM((planes, grid_p), jnp.float32)],
    )(
        own_phi, pair_phi, own_parts, pair_parts, third_parts, fourth_parts, image, ward,
        correlation,
    )
    given = lax.ppermute(first, "orb", swap)
    sent2 = lax.ppermute(second, "orb", [(i, i ^ 2) for i in range(4)])
    sent3 = lax.ppermute(last, "orb", across)
    third_held, fourth_held = call(outer_split_kernel, (parts, parts), "vvv")(
        third_out, fourth_out, live
    )
    given, third_held = lax.optimization_barrier((given, third_held))
    new, density = call(
        last_kernel,
        [block, share],
        "vvvvvvvvvvv",
        [
            pltpu.VMEM(block.shape, jnp.float32),
            pltpu.VMEM(share.shape, jnp.float32),
            pltpu.SemaphoreType.DMA((2,)),
        ],
        "aa",
    )(
        own_phi, own_parts, pair_parts, third_held, fourth_held, image, given, kept, sent2, sent3,
        inner_new,
    )
    return (new, density)


def per_device(psi, potential, extent):
    orbs, planes, grid_p = psi.shape
    fits = (
        lax.axis_size("orb") == 4
        and lax.axis_size("cmp") == 4
        and orbs == 8
        and planes == 16
        and grid_p % (4 * lanes) == 0
    )
    return (line_device if fits else general_device)(psi, potential, extent)


def solution(mesh):
    return jax.shard_map(
        per_device,
        mesh=mesh,
        in_specs=(P(("grp", "orb"), "cmp", None), P(("grp", "cmp"), None), P("grp")),
        out_specs=(P(("grp", "orb"), "cmp", None), P(("grp", "cmp"), "orb")),
        check_vma=False,
    )
```

```python
import functools
import math

import jax
import jax.numpy as jnp
import numpy as np
from jax import lax
from jax.experimental import pallas as pl
from jax.experimental.pallas import tpu as pltpu
from jax.sharding import PartitionSpec as P

step_length = 0.2
reach = 14
lanes = 128


def padded_2(cells, sides, width):
    for axis, dim in sides:
        count = lax.axis_size(axis)
        head = lax.slice_in_dim(cells, 0, width, axis=dim)
        tail = lax.slice_in_dim(cells, cells.shape[dim] - width, cells.shape[dim], axis=dim)
        cells = jnp.concatenate(
            [
                lax.ppermute(tail, axis, [(i, (i + 1) % count) for i in range(count)]),
                cells,
                lax.ppermute(head, axis, [((i + 1) % count, i) for i in range(count)]),
            ],
            axis=dim,
        )
    return cells


def band_matrix(length):
    rows = lax.broadcasted_iota(jnp.int32, (length + 2 * reach, length), 0)
    cols = lax.broadcasted_iota(jnp.int32, (length + 2 * reach, length), 1)
    spread = jnp.abs(rows - reach - cols)
    safe = jnp.maximum(spread, 1).astype(jnp.float32)
    signed = jnp.where(spread % 2 == 1, 2.0, -2.0) / (safe * safe)
    value = jnp.where(spread == 0, -math.pi**2 / 3.0, signed)
    return jnp.where(spread <= reach, value, 0.0)


def across_planes(padded, planes):
    return jnp.einsum("awp,wy->ayp", padded, band_matrix(planes), precision=lax.Precision.HIGHEST)


def along_grid(field):
    orbs, planes, grid_p = field.shape
    width = 128
    blocks = field.reshape(orbs, planes, grid_p // width, width)
    before = jnp.roll(blocks[..., width - reach :], 1, axis=2)
    after = jnp.roll(blocks[..., :reach], -1, axis=2)
    window = jnp.concatenate([before, blocks, after], axis=3)
    result = jnp.einsum(
        "axnw,wq->axnq", window, band_matrix(width), precision=lax.Precision.HIGHEST
    )
    return result.reshape(orbs, planes, grid_p)


def general_device(psi, potential, extent):
    orb_dev, planes, grid_p = psi.shape
    n_orb = lax.axis_size("orb")
    norbitals = orb_dev * n_orb
    cells = planes * lax.axis_size("cmp") * grid_p
    column = lax.broadcasted_iota(jnp.int32, (norbitals, grid_p), 1)
    live_all = (column < extent[:, None]).astype(jnp.float32)
    own_live = lax.dynamic_slice_in_dim(live_all, lax.axis_index("orb") * orb_dev, orb_dev, 0)
    phi = psi * own_live[:, None, :]
    padded = padded_2(phi, (("cmp", 1),), reach)
    kinetic = -0.5 * (across_planes(padded, planes) + along_grid(phi))
    hphi = own_live[:, None, :] * (kinetic + potential[None] * phi)
    phi_c, hphi_c = (
        lax.all_to_all(phi, "orb", split_axis=2, concat_axis=0, tiled=True),
        lax.all_to_all(hphi, "orb", split_axis=2, concat_axis=0, tiled=True),
    )
    flat_phi = phi_c.reshape(norbitals, -1)
    flat_h = hphi_c.reshape(norbitals, -1)
    partial_correlation = lax.dot_general(
        flat_phi,
        flat_h,
        (((1,), (1,)), ((), ())),
        precision=lax.Precision.HIGHEST,
        preferred_element_type=jnp.float32,
    )
    correlation = lax.psum(partial_correlation, ("orb", "cmp")) / cells
    grad_c = (flat_h - jnp.dot(correlation.T, flat_phi, precision=lax.Precision.HIGHEST)).reshape(
        phi_c.shape
    )
    grad = lax.all_to_all(grad_c, "orb", split_axis=0, concat_axis=2, tiled=True)
    psi_new = phi - step_length * grad
    density = (
        lax.psum_scatter(jnp.sum(psi_new * psi_new, axis=0), "orb", scatter_dimension=1, tiled=True)
        / norbitals
    )
    return (psi_new, density)


def weight(spread):
    spread = np.abs(spread)
    safe = np.maximum(spread, 1).astype(np.float64)
    value = np.where(spread % 2 == 1, 2.0, -2.0) / (safe * safe)
    value = np.where(spread == 0, -math.pi**2 / 3.0, value)
    return np.where(spread <= reach, value, 0.0).astype(np.float32)


def two_parts(value):
    high = value.astype(jnp.bfloat16)
    return high, (value - high.astype(np.float32)).astype(jnp.bfloat16)


def column_band():
    rows = np.arange(2 * lanes)[:, None]
    cols = np.arange(lanes)[None, :]
    high, low = two_parts(weight(rows - cols - reach))
    return np.concatenate([high, low], axis=1)


def plane_bands(planes):
    rows = np.arange(planes)[:, None]
    cols = np.arange(planes)[None, :]
    both = []
    for side in (-planes, planes):
        band = np.concatenate(
            [weight(cols + side - rows), weight(cols - rows), weight(cols - side - rows)], axis=1
        )
        high, low = two_parts(band)
        both.append(np.concatenate([high, high, low], axis=1))
    return np.stack(both)


def columns_kernel(out_ref):
    out_ref[...] = lax.broadcasted_iota(jnp.int32, out_ref.shape, 1)


def owner_of(f):
    z = lax.axis_index("orb")
    if f < 2:
        return z if f == 0 else jnp.where(z % 2 == 0, z + 1, z - 1)
    left, right = (2, 1) if f == 2 else (3, 0)
    return jnp.where(z < 2, left, right)


def on_inner():
    z = lax.axis_index("orb")
    return (z == 1) | (z == 2)


def live_kernel(columns_ref, extent_ref, out_ref):
    orbs = out_ref.shape[0] // 4
    for f in range(4):
        owner = owner_of(f)
        for a in range(orbs):
            row = jnp.where(columns_ref[:1, :] < extent_ref[owner * orbs + a], 1.0, 0.0)
            out_ref[f * orbs + a : f * orbs + a + 1, :] = row


def masked(field_ref, a, live_ref, f):
    at = f * field_ref.shape[0] + a
    return field_ref[a] * live_ref[at : at + 1, :]


def split_into(parts_ref, field_ref, live_ref, f):
    orbs, planes, _ = field_ref.shape
    for a in range(orbs):
        high, low = two_parts(masked(field_ref, a, live_ref, f))
        parts_ref[a * planes : (a + 1) * planes, :] = high
        parts_ref[(orbs + a) * planes : (orbs + a + 1) * planes, :] = low


def split_kernel(f, field_ref, live_ref, parts_ref):
    split_into(parts_ref, field_ref, live_ref, f)


def local_kernel(f, psi_ref, potential_ref, live_ref, band_ref, out_ref, parts_ref, phi_ref):
    orbs, planes, grid_p = psi_ref.shape
    tiles = grid_p // lanes
    for a in range(orbs):
        phi = masked(psi_ref, a, live_ref, f)
        phi_ref[a * planes : (a + 1) * planes, :] = phi
        high, low = two_parts(phi)
        parts_ref[a * planes : (a + 1) * planes, :] = high
        parts_ref[(orbs + a) * planes : (orbs + a + 1) * planes, :] = low
    high, low = two_parts(pltpu.roll(phi_ref[...], reach, 1))
    for t in range(tiles):
        here, after = t * lanes, (t + 1) % tiles * lanes
        high_t = jnp.concatenate([high[:, here : here + lanes], high[:, after : after + lanes]], 1)
        low_t = jnp.concatenate([low[:, here : here + lanes], low[:, after : after + lanes]], 1)
        both = jnp.dot(high_t, band_ref[...], preferred_element_type=jnp.float32)
        rest = jnp.dot(low_t, band_ref[:, :lanes], preferred_element_type=jnp.float32)
        second = both[:, :lanes] + both[:, lanes:] + rest
        field = phi_ref[:, here : here + lanes].reshape(orbs, planes, lanes)
        out_ref[:, :, here : here + lanes] = (
            potential_ref[:, here : here + lanes][None] * field
            - 0.5 * second.reshape(orbs, planes, lanes)
        )


def plane_kernel(
    f, far_ref, psi_ref, near_ref, local_ref, live_ref, band_ref, out_ref, parts_ref
):
    orbs, planes, _ = psi_ref.shape
    band = band_ref[lax.axis_index("cmp") % 2]
    for a in range(orbs):
        slab = jnp.concatenate([far_ref[a], psi_ref[a], near_ref[a]], axis=0)
        high, low = two_parts(slab)
        second = jnp.dot(
            band, jnp.concatenate([high, low, high], axis=0), preferred_element_type=jnp.float32
        )
        image = (local_ref[a] - 0.5 * second) * live_ref[f * orbs + a : f * orbs + a + 1, :]
        out_ref[a] = image
        high, low = two_parts(image)
        parts_ref[a * planes : (a + 1) * planes, :] = high
        parts_ref[(orbs + a) * planes : (orbs + a + 1) * planes, :] = low


def overlaps(field_ref, image_ref, planes):
    half = field_ref.shape[0] // 2
    product = lax.dot_general(
        field_ref[...],
        image_ref[...],
        (((1,), (1,)), ((), ())),
        preferred_element_type=jnp.float32,
    )
    product = product[:half] + product[half:]
    product = product[:, :half] + product[:, half:]
    row = lax.broadcasted_iota(jnp.int32, (half, half), 0)
    col = lax.broadcasted_iota(jnp.int32, (half, half), 1)
    product = jnp.where(row % planes == col % planes, product, 0.0)
    return jnp.sum(product.reshape(half // planes, planes, half), axis=1)


def overlap_kernel(planes, n_fields, *refs):
    fields, image_ref, out_ref = refs[:n_fields], refs[n_fields], refs[n_fields + 1]
    for f, field_ref in enumerate(fields):
        value = overlaps(field_ref, image_ref, planes)
        out_ref[f * value.shape[0] : (f + 1) * value.shape[0], :] = value


def correlation_kernel(
    planes, scale, own_ref, pair_ref, third_ref, fourth_ref, image_ref, ward_ref, early_ref, out_ref
):
    half = own_ref.shape[0] // 2
    orbs = half // planes
    ward = [overlaps(ref, ward_ref, planes) for ref in (own_ref, pair_ref, third_ref, fourth_ref)]
    last = overlaps(fourth_ref, image_ref, planes)
    wide = jnp.concatenate(
        [jnp.concatenate([early_ref[...], last], axis=0), jnp.concatenate(ward, axis=0)], axis=1
    )
    row = lax.broadcasted_iota(jnp.int32, (2 * half, 2 * orbs), 0)
    col = lax.broadcasted_iota(jnp.int32, (2 * half, 2 * orbs), 1)
    gather = jnp.where(row // planes == col, scale, 0.0)
    out_ref[...] = jnp.dot(
        wide, gather, precision=lax.Precision.HIGHEST, preferred_element_type=jnp.float32
    )


def sum_kernel(*refs):
    rows = refs[-1].shape[0]
    total = refs[0][...]
    for ref in refs[1:-1]:
        total = total + ref[:rows, :]
    refs[-1][...] = total


def spread_out(corr, planes):
    n_a, n_b = corr.shape
    shift = planes.bit_length() - 1
    shape = (n_b * planes, n_a * planes)

    def iota(shape, dim):
        return lax.broadcasted_iota(jnp.int32, shape, dim)

    def ones_where(mask):
        return jnp.where(mask, 1.0, 0.0).astype(jnp.bfloat16)

    take_b = ones_where(
        jnp.right_shift(iota((shape[0], n_b), 0), shift) == iota((shape[0], n_b), 1)
    )
    take_a = ones_where(
        jnp.right_shift(iota((n_a, shape[1]), 1), shift) == iota((n_a, shape[1]), 0)
    )
    same_plane = (jnp.bitwise_xor(iota(shape, 0), iota(shape, 1)) & (planes - 1)) == 0

    def spread(part):
        rows = lax.dot_general(
            take_b, part, (((1,), (1,)), ((), ())), preferred_element_type=jnp.float32
        ).astype(jnp.bfloat16)
        full = jnp.dot(rows, take_a, preferred_element_type=jnp.float32)
        return jnp.where(same_plane, full, 0.0).astype(jnp.bfloat16)

    high, low = two_parts(corr * step_length)
    return spread(high), spread(low)


def projections(high, low, fields, chunk):
    half = fields[0].shape[0] // 2
    total = None
    for f in range(0, len(fields), 2):
        pair = fields[f : f + 2]
        terms = [
            (low[:, f * half : (f + 2) * half], jnp.concatenate([r[:half, chunk] for r in pair], 0))
        ]
        for g, field_ref in enumerate(pair):
            here = high[:, (f + g) * half : (f + g + 1) * half]
            terms.append((jnp.concatenate([here, here], axis=1), field_ref[:, chunk]))
        for left, right in terms:
            term = jnp.dot(left, right, preferred_element_type=jnp.float32)
            total = term if total is None else total + term
    return total


def step_kernel(
    own_phi, pair_phi, own_parts, pair_parts, third_parts, fourth_parts, image_ref, ward_ref,
    corr_ref, kept_ref, out1_ref, out2_ref, out3_ref, new_ref, all_ref,
):
    orbs, planes, grid_p = image_ref.shape
    width = 2 * lanes
    share = grid_p // 4

    @pl.when(on_inner())
    def _():
        out1_ref[planes:, : corr_ref.shape[1]] = corr_ref[...]
        high, low = spread_out(corr_ref[...], planes)
        fields = (own_parts, pair_parts, third_parts, fourth_parts)
        for c in range(grid_p // width):
            chunk = slice(c * width, (c + 1) * width)
            change = projections(high, low, fields, chunk)
            density = jnp.zeros((planes, width), jnp.float32)
            for f, (phi_ref, half_ref) in enumerate(((own_phi, image_ref), (pair_phi, ward_ref))):
                for a in range(orbs):
                    at = (f * orbs + a) * planes
                    value = (
                        phi_ref[a * planes : (a + 1) * planes, chunk]
                        - step_length * half_ref[a, :, chunk]
                        + change[at : at + planes]
                    )
                    density = density + value * value
                    if f == 0:
                        new_ref[a, :, chunk] = value
            all_ref[:, chunk] = density * (1.0 / (4 * orbs))
        for k, part_ref in enumerate((kept_ref, out1_ref, out2_ref, out3_ref)):
            first = pl.multiple_of(jnp.bitwise_xor(lax.axis_index("orb"), k) * share, share)
            part_ref[:planes, :] = all_ref[:, pl.ds(first, share)]


def outer_split_kernel(third_ref, fourth_ref, live_ref, third_parts, fourth_parts):
    @pl.when(jnp.logical_not(on_inner()))
    def _():
        split_into(third_parts, third_ref, live_ref, 2)
        split_into(fourth_parts, fourth_ref, live_ref, 3)


def last_kernel(
    own_phi, own_parts, pair_parts, third_parts, fourth_parts, image_ref, given_ref, kept_ref,
    sent2_ref, sent3_ref, inner_new, new_ref, density_ref, own_new, own_density, sems,
):
    orbs, planes, grid_p = image_ref.shape
    width = 2 * lanes

    def write(values_ref):
        copies = [
            pltpu.make_async_copy(values_ref, new_ref, sems.at[0]),
            pltpu.make_async_copy(own_density, density_ref, sems.at[1]),
        ]
        for copy in copies:
            copy.start()
        for copy in copies:
            copy.wait()

    @pl.when(on_inner())
    def _():
        own_density[...] = kept_ref[...] + sent3_ref[...]
        write(inner_new)

    @pl.when(jnp.logical_not(on_inner()))
    def _():
        own_density[...] = given_ref[:planes] + sent2_ref[...]
        corr = given_ref[planes:, orbs : 2 * orbs]
        corr = jnp.concatenate([corr[orbs : 2 * orbs], corr[:orbs], corr[2 * orbs :]], axis=0)
        high, low = spread_out(corr, planes)
        fields = (own_parts, pair_parts, third_parts, fourth_parts)
        for c in range(grid_p // width):
            chunk = slice(c * width, (c + 1) * width)
            change = projections(high, low, fields, chunk)
            for a in range(orbs):
                at = slice(a * planes, (a + 1) * planes)
                own_new[a, :, chunk] = (
                    own_phi[at, chunk] - step_length * image_ref[a, :, chunk] + change[at]
                )
        write(own_new)


def call(kernel, out_shape, specs, scratch=(), out_specs=None):
    kinds = {"s": pltpu.SMEM, "v": pltpu.VMEM, "a": pl.ANY}
    if out_specs is None:
        out_specs = "v" * len(jax.tree.leaves(out_shape))
    places = [pl.BlockSpec(memory_space=kinds[kind]) for kind in out_specs]
    return pl.pallas_call(
        kernel,
        out_shape=out_shape,
        in_specs=[pl.BlockSpec(memory_space=kinds[kind]) for kind in specs],
        out_specs=places if isinstance(out_shape, (tuple, list)) else places[0],
        scratch_shapes=list(scratch),
        compiler_params=pltpu.CompilerParams(vmem_limit_bytes=10 * 2**20),
        cost_estimate=pl.CostEstimate(flops=1, bytes_accessed=1, transcendentals=0),
    )


def line_device(psi, potential, extent):
    orbs, planes, grid_p = psi.shape
    n_cmp = lax.axis_size("cmp")
    rows = orbs * planes
    cells = planes * n_cmp * grid_p
    swap = [(0, 1), (1, 0), (2, 3), (3, 2)]
    across = [(1, 2), (2, 1), (0, 0), (3, 3)]
    to_near = [(i, i ^ 1) for i in range(n_cmp)]
    to_far = [(i, i ^ 3) for i in range(n_cmp)]

    block = jax.ShapeDtypeStruct(psi.shape, jnp.float32)
    parts = jax.ShapeDtypeStruct((2 * rows, grid_p), jnp.bfloat16)
    flat = jax.ShapeDtypeStruct((rows, grid_p), jnp.float32)
    columns = jnp.asarray(column_band())
    bands = jnp.asarray(plane_bands(planes))

    pair = lax.ppermute(psi, "orb", swap)
    third = lax.ppermute(psi, "orb", across)
    grid = call(columns_kernel, jax.ShapeDtypeStruct((8, grid_p), jnp.int32), "")()
    slab, grid = lax.optimization_barrier((psi, grid))
    near = lax.ppermute(slab, "cmp", to_near)
    far = lax.ppermute(slab, "cmp", to_far)

    live = call(live_kernel, jax.ShapeDtypeStruct((4 * orbs, grid_p), jnp.float32), "vs")(
        grid, extent
    )
    local, own_parts, own_phi = call(
        functools.partial(local_kernel, 0), (block, parts, flat), "vvvv"
    )(psi, potential, live, columns)
    pair, local, own_parts = lax.optimization_barrier((pair, local, own_parts))
    fourth = lax.ppermute(pair, "orb", across)
    third_out = lax.ppermute(third, "orb", swap)
    third_parts = call(functools.partial(split_kernel, 2), parts, "vv")(third, live)
    turn, third_parts = lax.optimization_barrier((pair, third_parts))
    pair_far = lax.ppermute(turn, "cmp", to_far)
    pair_near = lax.ppermute(pair, "cmp", to_near)

    image, image_parts = call(functools.partial(plane_kernel, 0), (block, parts), "vvvvvv")(
        far, psi, near, local, live, bands
    )
    ward_local, pair_parts, pair_phi = call(
        functools.partial(local_kernel, 1), (block, parts, flat), "vvvv"
    )(pair, potential, live, columns)
    early = call(
        functools.partial(overlap_kernel, planes, 3),
        jax.ShapeDtypeStruct((3 * orbs, rows), jnp.float32),
        "vvvv",
    )(own_parts, pair_parts, third_parts, image_parts)

    fourth, ward_local, early = lax.optimization_barrier((fourth, ward_local, early))
    fourth_out = lax.ppermute(fourth, "orb", swap)
    ward, ward_parts = call(functools.partial(plane_kernel, 1), (block, parts), "vvvvvv")(
        pair_far, pair, pair_near, ward_local, live, bands
    )
    fourth_parts = call(functools.partial(split_kernel, 3), parts, "vv")(fourth, live)
    part = call(
        functools.partial(correlation_kernel, planes, 1.0 / cells),
        jax.ShapeDtypeStruct((4 * orbs, 2 * orbs), jnp.float32),
        "vvvvvvv",
    )(own_parts, pair_parts, third_parts, fourth_parts, image_parts, ward_parts, early)
    small = jax.ShapeDtypeStruct(part.shape, jnp.float32)
    chip = call(sum_kernel, small, "vv")(part, lax.ppermute(part, "cmp", to_near))
    correlation = call(sum_kernel, small, "vv")(chip, lax.ppermute(chip, "cmp", to_far))
    correlation, third_out = lax.optimization_barrier((correlation, third_out))

    share = jax.ShapeDtypeStruct((planes, grid_p // 4), jnp.float32)
    wide = jax.ShapeDtypeStruct((planes + 4 * orbs, grid_p // 4), jnp.float32)
    kept, first, second, last, inner_new = call(
        step_kernel,
        [share, wide, share, share, block],
        "vvvvvvvvv",
        [pltpu.VMEM((planes, grid_p), jnp.float32)],
    )(
        own_phi, pair_phi, own_parts, pair_parts, third_parts, fourth_parts, image, ward,
        correlation,
    )
    given = lax.ppermute(first, "orb", swap)
    sent2 = lax.ppermute(second, "orb", [(i, i ^ 2) for i in range(4)])
    sent3 = lax.ppermute(last, "orb", across)
    third_held, fourth_held = call(outer_split_kernel, (parts, parts), "vvv")(
        third_out, fourth_out, live
    )
    given, third_held = lax.optimization_barrier((given, third_held))
    new, density = call(
        last_kernel,
        [block, share],
        "vvvvvvvvvvv",
        [
            pltpu.VMEM(block.shape, jnp.float32),
            pltpu.VMEM(share.shape, jnp.float32),
            pltpu.SemaphoreType.DMA((2,)),
        ],
        "aa",
    )(
        own_phi, own_parts, pair_parts, third_held, fourth_held, image, given, kept, sent2, sent3,
        inner_new,
    )
    return (new, density)


def per_device(psi, potential, extent):
    orbs, planes, grid_p = psi.shape
    fits = (
        lax.axis_size("orb") == 4
        and lax.axis_size("cmp") == 4
        and orbs == 8
        and planes == 16
        and grid_p % (4 * lanes) == 0
    )
    return (line_device if fits else general_device)(psi, potential, extent)


def solution(mesh):
    return jax.shard_map(
        per_device,
        mesh=mesh,
        in_specs=(P(("grp", "orb"), "cmp", None), P(("grp", "cmp"), None), P("grp")),
        out_specs=(P(("grp", "orb"), "cmp", None), P(("grp", "cmp"), "orb")),
        check_vma=False,
    )
```

```python
import functools
import math

import jax
import jax.numpy as jnp
import numpy as np
from jax import lax
from jax.experimental import pallas as pl
from jax.experimental.pallas import tpu as pltpu
from jax.sharding import PartitionSpec as P

step_length = 0.2
reach = 14
lanes = 128


def padded_2(cells, sides, width):
    for axis, dim in sides:
        count = lax.axis_size(axis)
        head = lax.slice_in_dim(cells, 0, width, axis=dim)
        tail = lax.slice_in_dim(cells, cells.shape[dim] - width, cells.shape[dim], axis=dim)
        cells = jnp.concatenate(
            [
                lax.ppermute(tail, axis, [(i, (i + 1) % count) for i in range(count)]),
                cells,
                lax.ppermute(head, axis, [((i + 1) % count, i) for i in range(count)]),
            ],
            axis=dim,
        )
    return cells


def band_matrix(length):
    rows = lax.broadcasted_iota(jnp.int32, (length + 2 * reach, length), 0)
    cols = lax.broadcasted_iota(jnp.int32, (length + 2 * reach, length), 1)
    spread = jnp.abs(rows - reach - cols)
    safe = jnp.maximum(spread, 1).astype(jnp.float32)
    signed = jnp.where(spread % 2 == 1, 2.0, -2.0) / (safe * safe)
    value = jnp.where(spread == 0, -math.pi**2 / 3.0, signed)
    return jnp.where(spread <= reach, value, 0.0)


def across_planes(padded, planes):
    return jnp.einsum("awp,wy->ayp", padded, band_matrix(planes), precision=lax.Precision.HIGHEST)


def along_grid(field):
    orbs, planes, grid_p = field.shape
    width = 128
    blocks = field.reshape(orbs, planes, grid_p // width, width)
    before = jnp.roll(blocks[..., width - reach :], 1, axis=2)
    after = jnp.roll(blocks[..., :reach], -1, axis=2)
    window = jnp.concatenate([before, blocks, after], axis=3)
    result = jnp.einsum(
        "axnw,wq->axnq", window, band_matrix(width), precision=lax.Precision.HIGHEST
    )
    return result.reshape(orbs, planes, grid_p)


def general_device(psi, potential, extent):
    orb_dev, planes, grid_p = psi.shape
    n_orb = lax.axis_size("orb")
    norbitals = orb_dev * n_orb
    cells = planes * lax.axis_size("cmp") * grid_p
    column = lax.broadcasted_iota(jnp.int32, (norbitals, grid_p), 1)
    live_all = (column < extent[:, None]).astype(jnp.float32)
    own_live = lax.dynamic_slice_in_dim(live_all, lax.axis_index("orb") * orb_dev, orb_dev, 0)
    phi = psi * own_live[:, None, :]
    padded = padded_2(phi, (("cmp", 1),), reach)
    kinetic = -0.5 * (across_planes(padded, planes) + along_grid(phi))
    hphi = own_live[:, None, :] * (kinetic + potential[None] * phi)
    phi_c, hphi_c = (
        lax.all_to_all(phi, "orb", split_axis=2, concat_axis=0, tiled=True),
        lax.all_to_all(hphi, "orb", split_axis=2, concat_axis=0, tiled=True),
    )
    flat_phi = phi_c.reshape(norbitals, -1)
    flat_h = hphi_c.reshape(norbitals, -1)
    partial_correlation = lax.dot_general(
        flat_phi,
        flat_h,
        (((1,), (1,)), ((), ())),
        precision=lax.Precision.HIGHEST,
        preferred_element_type=jnp.float32,
    )
    correlation = lax.psum(partial_correlation, ("orb", "cmp")) / cells
    grad_c = (flat_h - jnp.dot(correlation.T, flat_phi, precision=lax.Precision.HIGHEST)).reshape(
        phi_c.shape
    )
    grad = lax.all_to_all(grad_c, "orb", split_axis=0, concat_axis=2, tiled=True)
    psi_new = phi - step_length * grad
    density = (
        lax.psum_scatter(jnp.sum(psi_new * psi_new, axis=0), "orb", scatter_dimension=1, tiled=True)
        / norbitals
    )
    return (psi_new, density)


def weight(spread):
    spread = np.abs(spread)
    safe = np.maximum(spread, 1).astype(np.float64)
    value = np.where(spread % 2 == 1, 2.0, -2.0) / (safe * safe)
    value = np.where(spread == 0, -math.pi**2 / 3.0, value)
    return np.where(spread <= reach, value, 0.0).astype(np.float32)


def two_parts(value):
    high = value.astype(jnp.bfloat16)
    return high, (value - high.astype(np.float32)).astype(jnp.bfloat16)


def column_band():
    rows = np.arange(2 * lanes)[:, None]
    cols = np.arange(lanes)[None, :]
    high, low = two_parts(weight(rows - cols - reach))
    return np.concatenate([high, low], axis=1)


def plane_bands(planes):
    rows = np.arange(planes)[:, None]
    cols = np.arange(planes)[None, :]
    both = []
    for side in (-planes, planes):
        band = np.concatenate(
            [weight(cols + side - rows), weight(cols - rows), weight(cols - side - rows)], axis=1
        )
        high, low = two_parts(band)
        both.append(np.concatenate([high, high, low], axis=1))
    return np.stack(both)


def columns_kernel(out_ref):
    out_ref[...] = lax.broadcasted_iota(jnp.int32, out_ref.shape, 1)


def owner_of(f):
    z = lax.axis_index("orb")
    if f < 2:
        return z if f == 0 else jnp.where(z % 2 == 0, z + 1, z - 1)
    left, right = (2, 1) if f == 2 else (3, 0)
    return jnp.where(z < 2, left, right)


def on_inner():
    z = lax.axis_index("orb")
    return (z == 1) | (z == 2)


def live_kernel(columns_ref, extent_ref, out_ref):
    orbs = out_ref.shape[0] // 4
    for f in range(4):
        owner = owner_of(f)
        for a in range(orbs):
            row = jnp.where(columns_ref[:1, :] < extent_ref[owner * orbs + a], 1.0, 0.0)
            out_ref[f * orbs + a : f * orbs + a + 1, :] = row


def masked(field_ref, a, live_ref, f):
    at = f * field_ref.shape[0] + a
    return field_ref[a] * live_ref[at : at + 1, :]


def split_into(parts_ref, field_ref, live_ref, f):
    orbs, planes, _ = field_ref.shape
    for a in range(orbs):
        high, low = two_parts(masked(field_ref, a, live_ref, f))
        parts_ref[a * planes : (a + 1) * planes, :] = high
        parts_ref[(orbs + a) * planes : (orbs + a + 1) * planes, :] = low


def split_kernel(f, field_ref, live_ref, parts_ref):
    split_into(parts_ref, field_ref, live_ref, f)


def local_kernel(f, psi_ref, potential_ref, live_ref, band_ref, out_ref, parts_ref, phi_ref):
    orbs, planes, grid_p = psi_ref.shape
    tiles = grid_p // lanes
    for a in range(orbs):
        phi = masked(psi_ref, a, live_ref, f)
        phi_ref[a * planes : (a + 1) * planes, :] = phi
        high, low = two_parts(phi)
        parts_ref[a * planes : (a + 1) * planes, :] = high
        parts_ref[(orbs + a) * planes : (orbs + a + 1) * planes, :] = low
    high, low = two_parts(pltpu.roll(phi_ref[...], reach, 1))
    for t in range(tiles):
        here, after = t * lanes, (t + 1) % tiles * lanes
        high_t = jnp.concatenate([high[:, here : here + lanes], high[:, after : after + lanes]], 1)
        low_t = jnp.concatenate([low[:, here : here + lanes], low[:, after : after + lanes]], 1)
        both = jnp.dot(high_t, band_ref[...], preferred_element_type=jnp.float32)
        rest = jnp.dot(low_t, band_ref[:, :lanes], preferred_element_type=jnp.float32)
        second = both[:, :lanes] + both[:, lanes:] + rest
        field = phi_ref[:, here : here + lanes].reshape(orbs, planes, lanes)
        out_ref[:, :, here : here + lanes] = (
            potential_ref[:, here : here + lanes][None] * field
            - 0.5 * second.reshape(orbs, planes, lanes)
        )


def plane_kernel(
    f, far_ref, psi_ref, near_ref, local_ref, live_ref, band_ref, out_ref, parts_ref
):
    orbs, planes, _ = psi_ref.shape
    band = band_ref[lax.axis_index("cmp") % 2]
    for a in range(orbs):
        slab = jnp.concatenate([far_ref[a], psi_ref[a], near_ref[a]], axis=0)
        high, low = two_parts(slab)
        second = jnp.dot(
            band, jnp.concatenate([high, low, high], axis=0), preferred_element_type=jnp.float32
        )
        image = (local_ref[a] - 0.5 * second) * live_ref[f * orbs + a : f * orbs + a + 1, :]
        out_ref[a] = image
        high, low = two_parts(image)
        parts_ref[a * planes : (a + 1) * planes, :] = high
        parts_ref[(orbs + a) * planes : (orbs + a + 1) * planes, :] = low


def overlaps(field_ref, image_ref, planes):
    half = field_ref.shape[0] // 2
    product = lax.dot_general(
        field_ref[...],
        image_ref[...],
        (((1,), (1,)), ((), ())),
        preferred_element_type=jnp.float32,
    )
    product = product[:half] + product[half:]
    product = product[:, :half] + product[:, half:]
    row = lax.broadcasted_iota(jnp.int32, (half, half), 0)
    col = lax.broadcasted_iota(jnp.int32, (half, half), 1)
    product = jnp.where(row % planes == col % planes, product, 0.0)
    return jnp.sum(product.reshape(half // planes, planes, half), axis=1)


def overlap_kernel(planes, n_fields, *refs):
    fields, image_ref, out_ref = refs[:n_fields], refs[n_fields], refs[n_fields + 1]
    for f, field_ref in enumerate(fields):
        value = overlaps(field_ref, image_ref, planes)
        out_ref[f * value.shape[0] : (f + 1) * value.shape[0], :] = value


def correlation_kernel(
    planes, scale, own_ref, pair_ref, third_ref, fourth_ref, ward_ref, early_ref, last_ref, out_ref
):
    half = own_ref.shape[0] // 2
    orbs = half // planes
    ward = [overlaps(ref, ward_ref, planes) for ref in (own_ref, pair_ref, third_ref, fourth_ref)]
    wide = jnp.concatenate(
        [
            jnp.concatenate([early_ref[...], last_ref[...]], axis=0),
            jnp.concatenate(ward, axis=0),
        ],
        axis=1,
    )
    row = lax.broadcasted_iota(jnp.int32, (2 * half, 2 * orbs), 0)
    col = lax.broadcasted_iota(jnp.int32, (2 * half, 2 * orbs), 1)
    gather = jnp.where(row // planes == col, scale, 0.0)
    out_ref[...] = jnp.dot(
        wide, gather, precision=lax.Precision.HIGHEST, preferred_element_type=jnp.float32
    )


def sum_kernel(*refs):
    rows = refs[-1].shape[0]
    total = refs[0][...]
    for ref in refs[1:-1]:
        total = total + ref[:rows, :]
    refs[-1][...] = total


def spread_out(corr, planes):
    n_a, n_b = corr.shape
    shift = planes.bit_length() - 1
    shape = (n_b * planes, n_a * planes)

    def iota(shape, dim):
        return lax.broadcasted_iota(jnp.int32, shape, dim)

    def ones_where(mask):
        return jnp.where(mask, 1.0, 0.0).astype(jnp.bfloat16)

    take_b = ones_where(
        jnp.right_shift(iota((shape[0], n_b), 0), shift) == iota((shape[0], n_b), 1)
    )
    take_a = ones_where(
        jnp.right_shift(iota((n_a, shape[1]), 1), shift) == iota((n_a, shape[1]), 0)
    )
    same_plane = (jnp.bitwise_xor(iota(shape, 0), iota(shape, 1)) & (planes - 1)) == 0

    def spread(part):
        rows = lax.dot_general(
            take_b, part, (((1,), (1,)), ((), ())), preferred_element_type=jnp.float32
        ).astype(jnp.bfloat16)
        full = jnp.dot(rows, take_a, preferred_element_type=jnp.float32)
        return jnp.where(same_plane, full, 0.0).astype(jnp.bfloat16)

    high, low = two_parts(corr * step_length)
    return spread(high), spread(low)


def projections(high, low, fields, chunk):
    half = fields[0].shape[0] // 2
    total = None
    for f in range(0, len(fields), 2):
        pair = fields[f : f + 2]
        terms = [
            (low[:, f * half : (f + 2) * half], jnp.concatenate([r[:half, chunk] for r in pair], 0))
        ]
        for g, field_ref in enumerate(pair):
            here = high[:, (f + g) * half : (f + g + 1) * half]
            terms.append((jnp.concatenate([here, here], axis=1), field_ref[:, chunk]))
        for left, right in terms:
            term = jnp.dot(left, right, preferred_element_type=jnp.float32)
            total = term if total is None else total + term
    return total


def step_kernel(
    own_phi, pair_phi, own_parts, pair_parts, third_parts, fourth_parts, image_ref, ward_ref,
    corr_ref, kept_ref, out1_ref, out2_ref, out3_ref, new_ref, all_ref,
):
    orbs, planes, grid_p = image_ref.shape
    width = 2 * lanes
    share = grid_p // 4

    @pl.when(on_inner())
    def _():
        held, across = corr_ref.shape[0] // 4, corr_ref.shape[1]
        for k in range(4):
            out1_ref[planes:, k * across : (k + 1) * across] = corr_ref[k * held : (k + 1) * held]
        high, low = spread_out(corr_ref[...], planes)
        fields = (own_parts, pair_parts, third_parts, fourth_parts)
        for c in range(grid_p // width):
            chunk = slice(c * width, (c + 1) * width)
            change = projections(high, low, fields, chunk)
            density = jnp.zeros((planes, width), jnp.float32)
            for f, (phi_ref, half_ref) in enumerate(((own_phi, image_ref), (pair_phi, ward_ref))):
                for a in range(orbs):
                    at = (f * orbs + a) * planes
                    value = (
                        phi_ref[a * planes : (a + 1) * planes, chunk]
                        - step_length * half_ref[a, :, chunk]
                        + change[at : at + planes]
                    )
                    density = density + value * value
                    if f == 0:
                        new_ref[a, :, chunk] = value
            all_ref[:, chunk] = density * (1.0 / (4 * orbs))
        for k, part_ref in enumerate((kept_ref, out1_ref, out2_ref, out3_ref)):
            first = pl.multiple_of(jnp.bitwise_xor(lax.axis_index("orb"), k) * share, share)
            part_ref[:planes, :] = all_ref[:, pl.ds(first, share)]


def outer_split_kernel(third_ref, fourth_ref, live_ref, third_parts, fourth_parts):
    @pl.when(jnp.logical_not(on_inner()))
    def _():
        split_into(third_parts, third_ref, live_ref, 2)
        split_into(fourth_parts, fourth_ref, live_ref, 3)


def last_kernel(
    own_phi, own_parts, pair_parts, third_parts, fourth_parts, image_ref, sent2_ref, sent3_ref,
    given_ref, kept_ref, inner_new, new_ref, density_ref, own_new, own_density, sems,
):
    orbs, planes, grid_p = image_ref.shape
    width = 2 * lanes

    def write(values_ref):
        copies = [
            pltpu.make_async_copy(values_ref, new_ref, sems.at[0]),
            pltpu.make_async_copy(own_density, density_ref, sems.at[1]),
        ]
        for copy in copies:
            copy.start()
        for copy in copies:
            copy.wait()

    @pl.when(on_inner())
    def _():
        own_density[...] = kept_ref[...] + sent3_ref[...]
        write(inner_new)

    @pl.when(jnp.logical_not(on_inner()))
    def _():
        own_density[...] = given_ref[:planes] + sent2_ref[:planes]
        corr = jnp.concatenate(
            [
                given_ref[planes:, (2 * k + 1) * orbs : (2 * k + 2) * orbs]
                for k in (1, 0, 2, 3)
            ],
            axis=0,
        )
        high, low = spread_out(corr, planes)
        fields = (own_parts, pair_parts, third_parts, fourth_parts)
        for c in range(grid_p // width):
            chunk = slice(c * width, (c + 1) * width)
            change = projections(high, low, fields, chunk)
            for a in range(orbs):
                at = slice(a * planes, (a + 1) * planes)
                own_new[a, :, chunk] = (
                    own_phi[at, chunk] - step_length * image_ref[a, :, chunk] + change[at]
                )
        write(own_new)


def call(kernel, out_shape, specs, scratch=(), out_specs=None):
    kinds = {"s": pltpu.SMEM, "v": pltpu.VMEM, "a": pl.ANY}
    if out_specs is None:
        out_specs = "v" * len(jax.tree.leaves(out_shape))
    places = [pl.BlockSpec(memory_space=kinds[kind]) for kind in out_specs]
    return pl.pallas_call(
        kernel,
        out_shape=out_shape,
        in_specs=[pl.BlockSpec(memory_space=kinds[kind]) for kind in specs],
        out_specs=places if isinstance(out_shape, (tuple, list)) else places[0],
        scratch_shapes=list(scratch),
        compiler_params=pltpu.CompilerParams(vmem_limit_bytes=10 * 2**20),
        cost_estimate=pl.CostEstimate(flops=1, bytes_accessed=1, transcendentals=0),
    )


def line_device(psi, potential, extent):
    orbs, planes, grid_p = psi.shape
    n_cmp = lax.axis_size("cmp")
    rows = orbs * planes
    cells = planes * n_cmp * grid_p
    swap = [(0, 1), (1, 0), (2, 3), (3, 2)]
    line = ("orb", "cmp")
    to_near = [(i, i ^ 1) for i in range(n_cmp)]
    to_far = [(i, i ^ 3) for i in range(n_cmp)]

    def with_outer(inner_pairs):
        outer_pairs = [(z * n_cmp + i, z * n_cmp + k) for z in (0, 3) for i, k in to_near]
        return inner_pairs + outer_pairs

    across = with_outer([(z * n_cmp + i, (3 - z) * n_cmp + i) for z in (1, 2) for i in range(n_cmp)])
    inner_far = with_outer([(z * n_cmp + i, z * n_cmp + k) for z in (1, 2) for i, k in to_far])

    block = jax.ShapeDtypeStruct(psi.shape, jnp.float32)
    parts = jax.ShapeDtypeStruct((2 * rows, grid_p), jnp.bfloat16)
    flat = jax.ShapeDtypeStruct((rows, grid_p), jnp.float32)
    columns = jnp.asarray(column_band())
    bands = jnp.asarray(plane_bands(planes))

    pair = lax.ppermute(psi, "orb", swap)
    third = lax.ppermute(psi, line, across)
    grid = call(columns_kernel, jax.ShapeDtypeStruct((8, grid_p), jnp.int32), "")()
    slab, grid = lax.optimization_barrier((psi, grid))
    near = lax.ppermute(slab, "cmp", to_near)
    far = lax.ppermute(slab, "cmp", to_far)

    live = call(live_kernel, jax.ShapeDtypeStruct((4 * orbs, grid_p), jnp.float32), "vs")(
        grid, extent
    )
    local, own_parts, own_phi = call(
        functools.partial(local_kernel, 0), (block, parts, flat), "vvvv"
    )(psi, potential, live, columns)
    pair, local, own_parts = lax.optimization_barrier((pair, local, own_parts))
    fourth = lax.ppermute(pair, line, across)
    third_out = lax.ppermute(third, "orb", swap)
    third_parts = call(functools.partial(split_kernel, 2), parts, "vv")(third, live)
    turn, third_parts = lax.optimization_barrier((pair, third_parts))
    pair_far = lax.ppermute(turn, line, inner_far)
    pair_near = lax.ppermute(pair, "cmp", to_near)

    image, image_parts = call(functools.partial(plane_kernel, 0), (block, parts), "vvvvvv")(
        far, psi, near, local, live, bands
    )
    ward_local, pair_parts, pair_phi = call(
        functools.partial(local_kernel, 1), (block, parts, flat), "vvvv"
    )(pair, potential, live, columns)
    early = call(
        functools.partial(overlap_kernel, planes, 3),
        jax.ShapeDtypeStruct((3 * orbs, rows), jnp.float32),
        "vvvv",
    )(own_parts, pair_parts, third_parts, image_parts)

    fourth, ward_local, early = lax.optimization_barrier((fourth, ward_local, early))
    fourth_out = lax.ppermute(fourth, "orb", swap)
    ward, ward_parts = call(functools.partial(plane_kernel, 1), (block, parts), "vvvvvv")(
        pair_far, pair, pair_near, ward_local, live, bands
    )
    fourth_parts = call(functools.partial(split_kernel, 3), parts, "vv")(fourth, live)
    fourth_parts, third_out = lax.optimization_barrier((fourth_parts, third_out))
    last = call(
        functools.partial(overlap_kernel, planes, 1),
        jax.ShapeDtypeStruct((orbs, rows), jnp.float32),
        "vv",
    )(fourth_parts, image_parts)
    part = call(
        functools.partial(correlation_kernel, planes, 1.0 / cells),
        jax.ShapeDtypeStruct((4 * orbs, 2 * orbs), jnp.float32),
        "vvvvvvv",
    )(own_parts, pair_parts, third_parts, fourth_parts, ward_parts, early, last)
    small = jax.ShapeDtypeStruct(part.shape, jnp.float32)
    chip = call(sum_kernel, small, "vv")(part, lax.ppermute(part, "cmp", to_near))
    correlation = call(sum_kernel, small, "vv")(chip, lax.ppermute(chip, line, inner_far))

    share = jax.ShapeDtypeStruct((planes, grid_p // 4), jnp.float32)
    wide = jax.ShapeDtypeStruct((planes + orbs, grid_p // 4), jnp.float32)
    first_sent = jax.ShapeDtypeStruct((2 * planes, grid_p // 4), jnp.float32)
    kept, first, second, last, inner_new = call(
        step_kernel,
        [share, wide, first_sent, share, block],
        "vvvvvvvvv",
        [pltpu.VMEM((planes, grid_p), jnp.float32)],
    )(
        own_phi, pair_phi, own_parts, pair_parts, third_parts, fourth_parts, image, ward,
        correlation,
    )
    given = lax.ppermute(first, "orb", swap)
    sent2 = lax.ppermute(second, "orb", [(i, i ^ 2) for i in range(4)])
    sent3 = lax.ppermute(last, line, across)
    third_held, fourth_held = call(outer_split_kernel, (parts, parts), "vvv")(
        third_out, fourth_out, live
    )
    sent2, sent3, third_held = lax.optimization_barrier((sent2, sent3, third_held))
    new, density = call(
        last_kernel,
        [block, share],
        "vvvvvvvvvvv",
        [
            pltpu.VMEM(block.shape, jnp.float32),
            pltpu.VMEM(share.shape, jnp.float32),
            pltpu.SemaphoreType.DMA((2,)),
        ],
        "aa",
    )(
        own_phi, own_parts, pair_parts, third_held, fourth_held, image, sent2, sent3, given, kept,
        inner_new,
    )
    return (new, density)


def per_device(psi, potential, extent):
    orbs, planes, grid_p = psi.shape
    fits = (
        lax.axis_size("orb") == 4
        and lax.axis_size("cmp") == 4
        and orbs == 8
        and planes == 16
        and grid_p % (4 * lanes) == 0
    )
    return (line_device if fits else general_device)(psi, potential, extent)


def solution(mesh):
    return jax.shard_map(
        per_device,
        mesh=mesh,
        in_specs=(P(("grp", "orb"), "cmp", None), P(("grp", "cmp"), None), P("grp")),
        out_specs=(P(("grp", "orb"), "cmp", None), P(("grp", "cmp"), "orb")),
        check_vma=False,
    )
```

```python
import functools
import math

import jax
import jax.numpy as jnp
import numpy as np
from jax import lax
from jax.experimental import pallas as pl
from jax.experimental.pallas import tpu as pltpu
from jax.sharding import PartitionSpec as P

step_length = 0.2
reach = 14
lanes = 128


def padded_2(cells, sides, width):
    for axis, dim in sides:
        count = lax.axis_size(axis)
        head = lax.slice_in_dim(cells, 0, width, axis=dim)
        tail = lax.slice_in_dim(cells, cells.shape[dim] - width, cells.shape[dim], axis=dim)
        cells = jnp.concatenate(
            [
                lax.ppermute(tail, axis, [(i, (i + 1) % count) for i in range(count)]),
                cells,
                lax.ppermute(head, axis, [((i + 1) % count, i) for i in range(count)]),
            ],
            axis=dim,
        )
    return cells


def band_matrix(length):
    rows = lax.broadcasted_iota(jnp.int32, (length + 2 * reach, length), 0)
    cols = lax.broadcasted_iota(jnp.int32, (length + 2 * reach, length), 1)
    spread = jnp.abs(rows - reach - cols)
    safe = jnp.maximum(spread, 1).astype(jnp.float32)
    signed = jnp.where(spread % 2 == 1, 2.0, -2.0) / (safe * safe)
    value = jnp.where(spread == 0, -math.pi**2 / 3.0, signed)
    return jnp.where(spread <= reach, value, 0.0)


def across_planes(padded, planes):
    return jnp.einsum("awp,wy->ayp", padded, band_matrix(planes), precision=lax.Precision.HIGHEST)


def along_grid(field):
    orbs, planes, grid_p = field.shape
    width = 128
    blocks = field.reshape(orbs, planes, grid_p // width, width)
    before = jnp.roll(blocks[..., width - reach :], 1, axis=2)
    after = jnp.roll(blocks[..., :reach], -1, axis=2)
    window = jnp.concatenate([before, blocks, after], axis=3)
    result = jnp.einsum(
        "axnw,wq->axnq", window, band_matrix(width), precision=lax.Precision.HIGHEST
    )
    return result.reshape(orbs, planes, grid_p)


def general_device(psi, potential, extent):
    orb_dev, planes, grid_p = psi.shape
    n_orb = lax.axis_size("orb")
    norbitals = orb_dev * n_orb
    cells = planes * lax.axis_size("cmp") * grid_p
    column = lax.broadcasted_iota(jnp.int32, (norbitals, grid_p), 1)
    live_all = (column < extent[:, None]).astype(jnp.float32)
    own_live = lax.dynamic_slice_in_dim(live_all, lax.axis_index("orb") * orb_dev, orb_dev, 0)
    phi = psi * own_live[:, None, :]
    padded = padded_2(phi, (("cmp", 1),), reach)
    kinetic = -0.5 * (across_planes(padded, planes) + along_grid(phi))
    hphi = own_live[:, None, :] * (kinetic + potential[None] * phi)
    phi_c, hphi_c = (
        lax.all_to_all(phi, "orb", split_axis=2, concat_axis=0, tiled=True),
        lax.all_to_all(hphi, "orb", split_axis=2, concat_axis=0, tiled=True),
    )
    flat_phi = phi_c.reshape(norbitals, -1)
    flat_h = hphi_c.reshape(norbitals, -1)
    partial_correlation = lax.dot_general(
        flat_phi,
        flat_h,
        (((1,), (1,)), ((), ())),
        precision=lax.Precision.HIGHEST,
        preferred_element_type=jnp.float32,
    )
    correlation = lax.psum(partial_correlation, ("orb", "cmp")) / cells
    grad_c = (flat_h - jnp.dot(correlation.T, flat_phi, precision=lax.Precision.HIGHEST)).reshape(
        phi_c.shape
    )
    grad = lax.all_to_all(grad_c, "orb", split_axis=0, concat_axis=2, tiled=True)
    psi_new = phi - step_length * grad
    density = (
        lax.psum_scatter(jnp.sum(psi_new * psi_new, axis=0), "orb", scatter_dimension=1, tiled=True)
        / norbitals
    )
    return (psi_new, density)


def weight(spread):
    spread = np.abs(spread)
    safe = np.maximum(spread, 1).astype(np.float64)
    value = np.where(spread % 2 == 1, 2.0, -2.0) / (safe * safe)
    value = np.where(spread == 0, -math.pi**2 / 3.0, value)
    return np.where(spread <= reach, value, 0.0).astype(np.float32)


def two_parts(value):
    high = value.astype(jnp.bfloat16)
    return high, (value - high.astype(np.float32)).astype(jnp.bfloat16)


def column_band():
    rows = np.arange(2 * lanes)[:, None]
    cols = np.arange(lanes)[None, :]
    high, low = two_parts(weight(rows - cols - reach))
    return np.concatenate([high, low], axis=1)


def plane_bands(planes):
    rows = np.arange(planes)[:, None]
    cols = np.arange(planes)[None, :]
    both = []
    for side in (-planes, planes):
        band = np.concatenate(
            [weight(cols + side - rows), weight(cols - rows), weight(cols - side - rows)], axis=1
        )
        high, low = two_parts(band)
        both.append(np.concatenate([high, high, low], axis=1))
    return np.stack(both)


def columns_kernel(out_ref):
    out_ref[...] = lax.broadcasted_iota(jnp.int32, out_ref.shape, 1)


def owner_of(f):
    z = lax.axis_index("orb")
    if f < 2:
        return z if f == 0 else jnp.where(z % 2 == 0, z + 1, z - 1)
    left, right = (2, 1) if f == 2 else (3, 0)
    return jnp.where(z < 2, left, right)


def on_inner():
    z = lax.axis_index("orb")
    return (z == 1) | (z == 2)


def live_kernel(columns_ref, extent_ref, out_ref):
    orbs = out_ref.shape[0] // 4
    for f in range(4):
        owner = owner_of(f)
        for a in range(orbs):
            row = jnp.where(columns_ref[:1, :] < extent_ref[owner * orbs + a], 1.0, 0.0)
            out_ref[f * orbs + a : f * orbs + a + 1, :] = row


def masked(field_ref, a, live_ref, f):
    at = f * field_ref.shape[0] + a
    return field_ref[a] * live_ref[at : at + 1, :]


def split_into(parts_ref, field_ref, live_ref, f):
    orbs, planes, _ = field_ref.shape
    for a in range(orbs):
        high, low = two_parts(masked(field_ref, a, live_ref, f))
        parts_ref[a * planes : (a + 1) * planes, :] = high
        parts_ref[(orbs + a) * planes : (orbs + a + 1) * planes, :] = low


def split_kernel(f, field_ref, live_ref, parts_ref):
    split_into(parts_ref, field_ref, live_ref, f)


def local_kernel(f, psi_ref, potential_ref, live_ref, band_ref, out_ref, parts_ref, phi_ref):
    orbs, planes, grid_p = psi_ref.shape
    tiles = grid_p // lanes
    for a in range(orbs):
        phi = masked(psi_ref, a, live_ref, f)
        phi_ref[a * planes : (a + 1) * planes, :] = phi
        high, low = two_parts(phi)
        parts_ref[a * planes : (a + 1) * planes, :] = high
        parts_ref[(orbs + a) * planes : (orbs + a + 1) * planes, :] = low
    high, low = two_parts(pltpu.roll(phi_ref[...], reach, 1))
    for t in range(tiles):
        here, after = t * lanes, (t + 1) % tiles * lanes
        high_t = jnp.concatenate([high[:, here : here + lanes], high[:, after : after + lanes]], 1)
        low_t = jnp.concatenate([low[:, here : here + lanes], low[:, after : after + lanes]], 1)
        both = jnp.dot(high_t, band_ref[...], preferred_element_type=jnp.float32)
        rest = jnp.dot(low_t, band_ref[:, :lanes], preferred_element_type=jnp.float32)
        second = both[:, :lanes] + both[:, lanes:] + rest
        field = phi_ref[:, here : here + lanes].reshape(orbs, planes, lanes)
        out_ref[:, :, here : here + lanes] = (
            potential_ref[:, here : here + lanes][None] * field
            - 0.5 * second.reshape(orbs, planes, lanes)
        )


def plane_kernel(
    f, far_ref, psi_ref, near_ref, local_ref, live_ref, band_ref, out_ref, parts_ref
):
    orbs, planes, _ = psi_ref.shape
    band = band_ref[lax.axis_index("cmp") % 2]
    for a in range(orbs):
        slab = jnp.concatenate([far_ref[a], psi_ref[a], near_ref[a]], axis=0)
        high, low = two_parts(slab)
        second = jnp.dot(
            band, jnp.concatenate([high, low, high], axis=0), preferred_element_type=jnp.float32
        )
        image = (local_ref[a] - 0.5 * second) * live_ref[f * orbs + a : f * orbs + a + 1, :]
        out_ref[a] = image
        high, low = two_parts(image)
        parts_ref[a * planes : (a + 1) * planes, :] = high
        parts_ref[(orbs + a) * planes : (orbs + a + 1) * planes, :] = low


def overlaps(field_ref, image_ref, planes):
    half = field_ref.shape[0] // 2
    product = lax.dot_general(
        field_ref[...],
        image_ref[...],
        (((1,), (1,)), ((), ())),
        preferred_element_type=jnp.float32,
    )
    product = product[:half] + product[half:]
    product = product[:, :half] + product[:, half:]
    row = lax.broadcasted_iota(jnp.int32, (half, half), 0)
    col = lax.broadcasted_iota(jnp.int32, (half, half), 1)
    product = jnp.where(row % planes == col % planes, product, 0.0)
    return jnp.sum(product.reshape(half // planes, planes, half), axis=1)


def overlap_kernel(planes, n_fields, *refs):
    fields, image_ref, out_ref = refs[:n_fields], refs[n_fields], refs[n_fields + 1]
    for f, field_ref in enumerate(fields):
        value = overlaps(field_ref, image_ref, planes)
        out_ref[f * value.shape[0] : (f + 1) * value.shape[0], :] = value


def correlation_kernel(
    planes, scale, own_ref, pair_ref, third_ref, fourth_ref, ward_ref, early_ref, last_ref, out_ref
):
    half = own_ref.shape[0] // 2
    orbs = half // planes
    ward = [overlaps(ref, ward_ref, planes) for ref in (own_ref, pair_ref, third_ref, fourth_ref)]
    wide = jnp.concatenate(
        [
            jnp.concatenate([early_ref[...], last_ref[...]], axis=0),
            jnp.concatenate(ward, axis=0),
        ],
        axis=1,
    )
    row = lax.broadcasted_iota(jnp.int32, (2 * half, 2 * orbs), 0)
    col = lax.broadcasted_iota(jnp.int32, (2 * half, 2 * orbs), 1)
    gather = jnp.where(row // planes == col, scale, 0.0)
    out_ref[...] = jnp.dot(
        wide, gather, precision=lax.Precision.HIGHEST, preferred_element_type=jnp.float32
    )


def sum_kernel(*refs):
    rows = refs[-1].shape[0]
    total = refs[0][...]
    for ref in refs[1:-1]:
        total = total + ref[:rows, :]
    refs[-1][...] = total


def correlation_sum_kernel(part_ref, other_ref, out_ref, sent_ref):
    total = part_ref[...] + other_ref[...]
    out_ref[...] = total
    sent_ref[: total.shape[0], : total.shape[1]] = total


def spread_out(corr, planes):
    n_a, n_b = corr.shape
    shift = planes.bit_length() - 1
    shape = (n_b * planes, n_a * planes)

    def iota(shape, dim):
        return lax.broadcasted_iota(jnp.int32, shape, dim)

    def ones_where(mask):
        return jnp.where(mask, 1.0, 0.0).astype(jnp.bfloat16)

    take_b = ones_where(
        jnp.right_shift(iota((shape[0], n_b), 0), shift) == iota((shape[0], n_b), 1)
    )
    take_a = ones_where(
        jnp.right_shift(iota((n_a, shape[1]), 1), shift) == iota((n_a, shape[1]), 0)
    )
    same_plane = (jnp.bitwise_xor(iota(shape, 0), iota(shape, 1)) & (planes - 1)) == 0

    def spread(part):
        rows = lax.dot_general(
            take_b, part, (((1,), (1,)), ((), ())), preferred_element_type=jnp.float32
        ).astype(jnp.bfloat16)
        full = jnp.dot(rows, take_a, preferred_element_type=jnp.float32)
        return jnp.where(same_plane, full, 0.0).astype(jnp.bfloat16)

    high, low = two_parts(corr * step_length)
    return spread(high), spread(low)


def projections(high, low, fields, chunk):
    half = fields[0].shape[0] // 2
    total = None
    for f in range(0, len(fields), 2):
        pair = fields[f : f + 2]
        terms = [
            (low[:, f * half : (f + 2) * half], jnp.concatenate([r[:half, chunk] for r in pair], 0))
        ]
        for g, field_ref in enumerate(pair):
            here = high[:, (f + g) * half : (f + g + 1) * half]
            terms.append((jnp.concatenate([here, here], axis=1), field_ref[:, chunk]))
        for left, right in terms:
            term = jnp.dot(left, right, preferred_element_type=jnp.float32)
            total = term if total is None else total + term
    return total


def step_kernel(
    own_phi, pair_phi, own_parts, pair_parts, third_parts, fourth_parts, image_ref, ward_ref,
    corr_ref, kept_ref, out1_ref, out2_ref, out3_ref, new_ref, all_ref,
):
    orbs, planes, grid_p = image_ref.shape
    width = 2 * lanes
    share = grid_p // 4

    @pl.when(on_inner())
    def _():
        high, low = spread_out(corr_ref[...], planes)
        fields = (own_parts, pair_parts, third_parts, fourth_parts)
        for c in range(grid_p // width):
            chunk = slice(c * width, (c + 1) * width)
            change = projections(high, low, fields, chunk)
            density = jnp.zeros((planes, width), jnp.float32)
            for f, (phi_ref, half_ref) in enumerate(((own_phi, image_ref), (pair_phi, ward_ref))):
                for a in range(orbs):
                    at = (f * orbs + a) * planes
                    value = (
                        phi_ref[a * planes : (a + 1) * planes, chunk]
                        - step_length * half_ref[a, :, chunk]
                        + change[at : at + planes]
                    )
                    density = density + value * value
                    if f == 0:
                        new_ref[a, :, chunk] = value
            all_ref[:, chunk] = density * (1.0 / (4 * orbs))
        for k, part_ref in enumerate((kept_ref, out1_ref, out2_ref, out3_ref)):
            first = pl.multiple_of(jnp.bitwise_xor(lax.axis_index("orb"), k) * share, share)
            part_ref[:planes, :] = all_ref[:, pl.ds(first, share)]


def outer_split_kernel(third_ref, fourth_ref, live_ref, third_parts, fourth_parts):
    @pl.when(jnp.logical_not(on_inner()))
    def _():
        split_into(third_parts, third_ref, live_ref, 2)
        split_into(fourth_parts, fourth_ref, live_ref, 3)


def finish_kernel(
    own_phi, own_parts, pair_parts, third_parts, fourth_parts, image_ref, corr_ref, inner_new,
    new_ref, own_new, sem,
):
    orbs, planes, grid_p = image_ref.shape
    width = 2 * lanes

    def write(values_ref):
        copy = pltpu.make_async_copy(values_ref, new_ref, sem)
        copy.start()
        copy.wait()

    @pl.when(on_inner())
    def _():
        write(inner_new)

    @pl.when(jnp.logical_not(on_inner()))
    def _():
        corr = corr_ref[: 4 * orbs, orbs : 2 * orbs]
        corr = jnp.concatenate([corr[orbs : 2 * orbs], corr[:orbs], corr[2 * orbs :]], axis=0)
        high, low = spread_out(corr, planes)
        fields = (own_parts, pair_parts, third_parts, fourth_parts)
        for c in range(grid_p // width):
            chunk = slice(c * width, (c + 1) * width)
            change = projections(high, low, fields, chunk)
            for a in range(orbs):
                at = slice(a * planes, (a + 1) * planes)
                own_new[a, :, chunk] = (
                    own_phi[at, chunk] - step_length * image_ref[a, :, chunk] + change[at]
                )
        write(own_new)


def last_kernel(sent2_ref, sent3_ref, given_ref, kept_ref, density_ref):
    planes = density_ref.shape[0]

    @pl.when(on_inner())
    def _():
        density_ref[...] = kept_ref[...] + sent3_ref[...]

    @pl.when(jnp.logical_not(on_inner()))
    def _():
        density_ref[...] = given_ref[:planes] + sent2_ref[:planes]


def call(kernel, out_shape, specs, scratch=(), out_specs=None):
    kinds = {"s": pltpu.SMEM, "v": pltpu.VMEM, "a": pl.ANY}
    if out_specs is None:
        out_specs = "v" * len(jax.tree.leaves(out_shape))
    places = [pl.BlockSpec(memory_space=kinds[kind]) for kind in out_specs]
    return pl.pallas_call(
        kernel,
        out_shape=out_shape,
        in_specs=[pl.BlockSpec(memory_space=kinds[kind]) for kind in specs],
        out_specs=places if isinstance(out_shape, (tuple, list)) else places[0],
        scratch_shapes=list(scratch),
        compiler_params=pltpu.CompilerParams(vmem_limit_bytes=10 * 2**20),
        cost_estimate=pl.CostEstimate(flops=1, bytes_accessed=1, transcendentals=0),
    )


def line_device(psi, potential, extent):
    orbs, planes, grid_p = psi.shape
    n_cmp = lax.axis_size("cmp")
    rows = orbs * planes
    cells = planes * n_cmp * grid_p
    swap = [(0, 1), (1, 0), (2, 3), (3, 2)]
    line = ("orb", "cmp")
    to_near = [(i, i ^ 1) for i in range(n_cmp)]
    to_far = [(i, i ^ 3) for i in range(n_cmp)]

    def with_outer(inner_pairs):
        outer_pairs = [(z * n_cmp + i, z * n_cmp + k) for z in (0, 3) for i, k in to_near]
        return inner_pairs + outer_pairs

    across = with_outer([(z * n_cmp + i, (3 - z) * n_cmp + i) for z in (1, 2) for i in range(n_cmp)])
    inner_far = with_outer([(z * n_cmp + i, z * n_cmp + k) for z in (1, 2) for i, k in to_far])

    block = jax.ShapeDtypeStruct(psi.shape, jnp.float32)
    parts = jax.ShapeDtypeStruct((2 * rows, grid_p), jnp.bfloat16)
    flat = jax.ShapeDtypeStruct((rows, grid_p), jnp.float32)
    columns = jnp.asarray(column_band())
    bands = jnp.asarray(plane_bands(planes))

    pair = lax.ppermute(psi, "orb", swap)
    third = lax.ppermute(psi, line, across)
    grid = call(columns_kernel, jax.ShapeDtypeStruct((8, grid_p), jnp.int32), "")()
    slab, grid = lax.optimization_barrier((psi, grid))
    near = lax.ppermute(slab, "cmp", to_near)
    far = lax.ppermute(slab, "cmp", to_far)

    live = call(live_kernel, jax.ShapeDtypeStruct((4 * orbs, grid_p), jnp.float32), "vs")(
        grid, extent
    )
    local, own_parts, own_phi = call(
        functools.partial(local_kernel, 0), (block, parts, flat), "vvvv"
    )(psi, potential, live, columns)
    pair, local, own_parts = lax.optimization_barrier((pair, local, own_parts))
    fourth = lax.ppermute(pair, line, across)
    third_out = lax.ppermute(third, "orb", swap)
    third_parts = call(functools.partial(split_kernel, 2), parts, "vv")(third, live)
    turn, third_parts = lax.optimization_barrier((pair, third_parts))
    pair_far = lax.ppermute(turn, line, inner_far)
    pair_near = lax.ppermute(pair, "cmp", to_near)

    image, image_parts = call(functools.partial(plane_kernel, 0), (block, parts), "vvvvvv")(
        far, psi, near, local, live, bands
    )
    ward_local, pair_parts, pair_phi = call(
        functools.partial(local_kernel, 1), (block, parts, flat), "vvvv"
    )(pair, potential, live, columns)
    early = call(
        functools.partial(overlap_kernel, planes, 3),
        jax.ShapeDtypeStruct((3 * orbs, rows), jnp.float32),
        "vvvv",
    )(own_parts, pair_parts, third_parts, image_parts)

    fourth, ward_local, early = lax.optimization_barrier((fourth, ward_local, early))
    fourth_out = lax.ppermute(fourth, "orb", swap)
    ward, ward_parts = call(functools.partial(plane_kernel, 1), (block, parts), "vvvvvv")(
        pair_far, pair, pair_near, ward_local, live, bands
    )
    fourth_parts = call(functools.partial(split_kernel, 3), parts, "vv")(fourth, live)
    fourth_parts, third_out = lax.optimization_barrier((fourth_parts, third_out))
    last = call(
        functools.partial(overlap_kernel, planes, 1),
        jax.ShapeDtypeStruct((orbs, rows), jnp.float32),
        "vv",
    )(fourth_parts, image_parts)
    part = call(
        functools.partial(correlation_kernel, planes, 1.0 / cells),
        jax.ShapeDtypeStruct((4 * orbs, 2 * orbs), jnp.float32),
        "vvvvvvv",
    )(own_parts, pair_parts, third_parts, fourth_parts, ward_parts, early, last)
    small = jax.ShapeDtypeStruct(part.shape, jnp.float32)
    chip = call(sum_kernel, small, "vv")(part, lax.ppermute(part, "cmp", to_near))
    correlation, sent = call(
        correlation_sum_kernel,
        (small, jax.ShapeDtypeStruct((5 * orbs, grid_p // 4), jnp.float32)),
        "vv",
    )(chip, lax.ppermute(chip, line, inner_far))

    given_correlation = lax.ppermute(sent, "orb", swap)

    share = jax.ShapeDtypeStruct((planes, grid_p // 4), jnp.float32)
    wide = jax.ShapeDtypeStruct((planes + orbs, grid_p // 4), jnp.float32)
    first_sent = jax.ShapeDtypeStruct((2 * planes, grid_p // 4), jnp.float32)
    kept, first, second, last, inner_new = call(
        step_kernel,
        [share, wide, first_sent, share, block],
        "vvvvvvvvv",
        [pltpu.VMEM((planes, grid_p), jnp.float32)],
    )(
        own_phi, pair_phi, own_parts, pair_parts, third_parts, fourth_parts, image, ward,
        correlation,
    )
    given = lax.ppermute(first, "orb", swap)
    sent2 = lax.ppermute(second, "orb", [(i, i ^ 2) for i in range(4)])
    sent3 = lax.ppermute(last, line, across)
    third_held, fourth_held = call(outer_split_kernel, (parts, parts), "vvv")(
        third_out, fourth_out, live
    )
    new = call(
        finish_kernel,
        block,
        "vvvvvvvv",
        [pltpu.VMEM(block.shape, jnp.float32), pltpu.SemaphoreType.DMA],
        "a",
    )(
        own_phi, own_parts, pair_parts, third_held, fourth_held, image, given_correlation,
        inner_new,
    )
    sent2, sent3, given, new = lax.optimization_barrier((sent2, sent3, given, new))
    density = call(last_kernel, share, "vvvv")(sent2, sent3, given, kept)
    return (new, density)


def per_device(psi, potential, extent):
    orbs, planes, grid_p = psi.shape
    fits = (
        lax.axis_size("orb") == 4
        and lax.axis_size("cmp") == 4
        and orbs == 8
        and planes == 16
        and grid_p % (4 * lanes) == 0
    )
    return (line_device if fits else general_device)(psi, potential, extent)


def solution(mesh):
    return jax.shard_map(
        per_device,
        mesh=mesh,
        in_specs=(P(("grp", "orb"), "cmp", None), P(("grp", "cmp"), None), P("grp")),
        out_specs=(P(("grp", "orb"), "cmp", None), P(("grp", "cmp"), "orb")),
        check_vma=False,
    )
```

```python
import functools
import math

import jax
import jax.numpy as jnp
import numpy as np
from jax import lax
from jax.experimental import pallas as pl
from jax.experimental.pallas import tpu as pltpu
from jax.sharding import PartitionSpec as P

step_length = 0.2
reach = 14
lanes = 128


def padded_2(cells, sides, width):
    for axis, dim in sides:
        count = lax.axis_size(axis)
        head = lax.slice_in_dim(cells, 0, width, axis=dim)
        tail = lax.slice_in_dim(cells, cells.shape[dim] - width, cells.shape[dim], axis=dim)
        cells = jnp.concatenate(
            [
                lax.ppermute(tail, axis, [(i, (i + 1) % count) for i in range(count)]),
                cells,
                lax.ppermute(head, axis, [((i + 1) % count, i) for i in range(count)]),
            ],
            axis=dim,
        )
    return cells


def band_matrix(length):
    rows = lax.broadcasted_iota(jnp.int32, (length + 2 * reach, length), 0)
    cols = lax.broadcasted_iota(jnp.int32, (length + 2 * reach, length), 1)
    spread = jnp.abs(rows - reach - cols)
    safe = jnp.maximum(spread, 1).astype(jnp.float32)
    signed = jnp.where(spread % 2 == 1, 2.0, -2.0) / (safe * safe)
    value = jnp.where(spread == 0, -math.pi**2 / 3.0, signed)
    return jnp.where(spread <= reach, value, 0.0)


def across_planes(padded, planes):
    return jnp.einsum("awp,wy->ayp", padded, band_matrix(planes), precision=lax.Precision.HIGHEST)


def along_grid(field):
    orbs, planes, grid_p = field.shape
    width = 128
    blocks = field.reshape(orbs, planes, grid_p // width, width)
    before = jnp.roll(blocks[..., width - reach :], 1, axis=2)
    after = jnp.roll(blocks[..., :reach], -1, axis=2)
    window = jnp.concatenate([before, blocks, after], axis=3)
    result = jnp.einsum(
        "axnw,wq->axnq", window, band_matrix(width), precision=lax.Precision.HIGHEST
    )
    return result.reshape(orbs, planes, grid_p)


def general_device(psi, potential, extent):
    orb_dev, planes, grid_p = psi.shape
    n_orb = lax.axis_size("orb")
    norbitals = orb_dev * n_orb
    cells = planes * lax.axis_size("cmp") * grid_p
    column = lax.broadcasted_iota(jnp.int32, (norbitals, grid_p), 1)
    live_all = (column < extent[:, None]).astype(jnp.float32)
    own_live = lax.dynamic_slice_in_dim(live_all, lax.axis_index("orb") * orb_dev, orb_dev, 0)
    phi = psi * own_live[:, None, :]
    padded = padded_2(phi, (("cmp", 1),), reach)
    kinetic = -0.5 * (across_planes(padded, planes) + along_grid(phi))
    hphi = own_live[:, None, :] * (kinetic + potential[None] * phi)
    phi_c, hphi_c = (
        lax.all_to_all(phi, "orb", split_axis=2, concat_axis=0, tiled=True),
        lax.all_to_all(hphi, "orb", split_axis=2, concat_axis=0, tiled=True),
    )
    flat_phi = phi_c.reshape(norbitals, -1)
    flat_h = hphi_c.reshape(norbitals, -1)
    partial_correlation = lax.dot_general(
        flat_phi,
        flat_h,
        (((1,), (1,)), ((), ())),
        precision=lax.Precision.HIGHEST,
        preferred_element_type=jnp.float32,
    )
    correlation = lax.psum(partial_correlation, ("orb", "cmp")) / cells
    grad_c = (flat_h - jnp.dot(correlation.T, flat_phi, precision=lax.Precision.HIGHEST)).reshape(
        phi_c.shape
    )
    grad = lax.all_to_all(grad_c, "orb", split_axis=0, concat_axis=2, tiled=True)
    psi_new = phi - step_length * grad
    density = (
        lax.psum_scatter(jnp.sum(psi_new * psi_new, axis=0), "orb", scatter_dimension=1, tiled=True)
        / norbitals
    )
    return (psi_new, density)


def weight(spread):
    spread = np.abs(spread)
    safe = np.maximum(spread, 1).astype(np.float64)
    value = np.where(spread % 2 == 1, 2.0, -2.0) / (safe * safe)
    value = np.where(spread == 0, -math.pi**2 / 3.0, value)
    return np.where(spread <= reach, value, 0.0).astype(np.float32)


def two_parts(value):
    high = value.astype(jnp.bfloat16)
    return high, (value - high.astype(np.float32)).astype(jnp.bfloat16)


def column_band():
    rows = np.arange(2 * lanes)[:, None]
    cols = np.arange(lanes)[None, :]
    high, low = two_parts(weight(rows - cols - reach))
    return np.concatenate([high, low], axis=1)


def plane_bands(planes):
    rows = np.arange(planes)[:, None]
    cols = np.arange(planes)[None, :]
    both = []
    for side in (-planes, planes):
        band = np.concatenate(
            [weight(cols + side - rows), weight(cols - rows), weight(cols - side - rows)], axis=1
        )
        high, low = two_parts(band)
        both.append(np.concatenate([high, high, low], axis=1))
    return np.stack(both)


def columns_kernel(out_ref):
    out_ref[...] = lax.broadcasted_iota(jnp.int32, out_ref.shape, 1)


def owner_of(f):
    z = lax.axis_index("orb")
    if f < 2:
        return z if f == 0 else jnp.where(z % 2 == 0, z + 1, z - 1)
    left, right = (2, 1) if f == 2 else (3, 0)
    return jnp.where(z < 2, left, right)


def on_inner():
    z = lax.axis_index("orb")
    return (z == 1) | (z == 2)


def live_kernel(columns_ref, extent_ref, out_ref):
    orbs = out_ref.shape[0] // 4
    for f in range(4):
        owner = owner_of(f)
        for a in range(orbs):
            row = jnp.where(columns_ref[:1, :] < extent_ref[owner * orbs + a], 1.0, 0.0)
            out_ref[f * orbs + a : f * orbs + a + 1, :] = row


def masked(field_ref, a, live_ref, f):
    at = f * (live_ref.shape[0] // 4) + a
    return field_ref[a] * live_ref[at : at + 1, :]


def split_one(parts_ref, value, a):
    planes = value.shape[0]
    half = parts_ref.shape[0] // 2
    high, low = two_parts(value)
    parts_ref[a * planes : (a + 1) * planes, :] = high
    parts_ref[half + a * planes : half + (a + 1) * planes, :] = low


def split_into(parts_ref, field_ref, live_ref, f):
    for a in range(field_ref.shape[0]):
        split_one(parts_ref, masked(field_ref, a, live_ref, f), a)


def split_kernel(f, field_ref, live_ref, parts_ref):
    split_into(parts_ref, field_ref, live_ref, f)


def short_rows(planes):
    spare = planes - reach
    for parity, first in ((0, 0), (1, spare)):
        free = reach if parity == 0 else 0
        each = reach // spare
        yield parity, [(free + p // each, p % each, first + p) for p in range(reach)]


def shorten_kernel(psi_ref, short_ref):
    orbs, planes, _ = psi_ref.shape
    width = short_ref.shape[2]
    short_ref[...] = psi_ref[:, :, :width]
    for parity, moves in short_rows(planes):

        @pl.when(lax.axis_index("cmp") % 2 == parity)
        def _():
            for a in range(orbs):
                for row, place, plane in moves:
                    short_ref[a, row : row + 1, place * lanes : (place + 1) * lanes] = psi_ref[
                        a, plane : plane + 1, width:
                    ]


def local_kernel(f, psi_ref, potential_ref, live_ref, band_ref, out_ref, parts_ref, phi_ref):
    orbs, planes, grid_p = psi_ref.shape
    tiles = grid_p // lanes
    for a in range(orbs):
        phi = masked(psi_ref, a, live_ref, f)
        phi_ref[a * planes : (a + 1) * planes, :] = phi
        high, low = two_parts(phi)
        parts_ref[a * planes : (a + 1) * planes, :] = high
        parts_ref[(orbs + a) * planes : (orbs + a + 1) * planes, :] = low
    high, low = two_parts(pltpu.roll(phi_ref[...], reach, 1))
    for t in range(tiles):
        here, after = t * lanes, (t + 1) % tiles * lanes
        high_t = jnp.concatenate([high[:, here : here + lanes], high[:, after : after + lanes]], 1)
        low_t = jnp.concatenate([low[:, here : here + lanes], low[:, after : after + lanes]], 1)
        both = jnp.dot(high_t, band_ref[...], preferred_element_type=jnp.float32)
        rest = jnp.dot(low_t, band_ref[:, :lanes], preferred_element_type=jnp.float32)
        second = both[:, :lanes] + both[:, lanes:] + rest
        field = phi_ref[:, here : here + lanes].reshape(orbs, planes, lanes)
        out_ref[:, :, here : here + lanes] = (
            potential_ref[:, here : here + lanes][None] * field
            - 0.5 * second.reshape(orbs, planes, lanes)
        )


def plane_kernel(
    f, far_ref, psi_ref, near_ref, local_ref, live_ref, band_ref, out_ref, parts_ref, *rest_ref
):
    orbs, planes, _ = psi_ref.shape
    band = band_ref[lax.axis_index("cmp") % 2]
    for ref in rest_ref:
        ref[...] = jnp.zeros_like(ref)
        for parity, moves in short_rows(planes):

            @pl.when(lax.axis_index("cmp") % 2 != parity)
            def _():
                for a in range(orbs):
                    for row, place, plane in moves:
                        ref[a, plane : plane + 1, :] = far_ref[
                            a, row : row + 1, place * lanes : (place + 1) * lanes
                        ]

    for a in range(orbs):
        far = jnp.concatenate([far_ref[a]] + [ref[a] for ref in rest_ref], axis=1)
        slab = jnp.concatenate([far, psi_ref[a], near_ref[a]], axis=0)
        high, low = two_parts(slab)
        second = jnp.dot(
            band, jnp.concatenate([high, low, high], axis=0), preferred_element_type=jnp.float32
        )
        image = (local_ref[a] - 0.5 * second) * live_ref[f * orbs + a : f * orbs + a + 1, :]
        out_ref[a] = image
        high, low = two_parts(image)
        parts_ref[a * planes : (a + 1) * planes, :] = high
        parts_ref[(orbs + a) * planes : (orbs + a + 1) * planes, :] = low


def overlaps(field_ref, image_ref, planes):
    half = field_ref.shape[0] // 2
    product = lax.dot_general(
        field_ref[...],
        image_ref[...],
        (((1,), (1,)), ((), ())),
        preferred_element_type=jnp.float32,
    )
    product = product[:half] + product[half:]
    product = product[:, :half] + product[:, half:]
    row = lax.broadcasted_iota(jnp.int32, (half, half), 0)
    col = lax.broadcasted_iota(jnp.int32, (half, half), 1)
    product = jnp.where(row % planes == col % planes, product, 0.0)
    return jnp.sum(product.reshape(half // planes, planes, half), axis=1)


def overlap_kernel(planes, n_fields, *refs):
    fields, image_ref, out_ref = refs[:n_fields], refs[n_fields], refs[n_fields + 1]
    for f, field_ref in enumerate(fields):
        value = overlaps(field_ref, image_ref, planes)
        out_ref[f * value.shape[0] : (f + 1) * value.shape[0], :] = value


def correlation_kernel(
    planes, scale, own_ref, pair_ref, third_ref, fourth_ref, ward_ref, early_ref, last_ref, out_ref
):
    half = own_ref.shape[0] // 2
    orbs = half // planes
    ward = [overlaps(ref, ward_ref, planes) for ref in (own_ref, pair_ref, third_ref, fourth_ref)]
    wide = jnp.concatenate(
        [
            jnp.concatenate([early_ref[...], last_ref[...]], axis=0),
            jnp.concatenate(ward, axis=0),
        ],
        axis=1,
    )
    row = lax.broadcasted_iota(jnp.int32, (2 * half, 2 * orbs), 0)
    col = lax.broadcasted_iota(jnp.int32, (2 * half, 2 * orbs), 1)
    gather = jnp.where(row // planes == col, scale, 0.0)
    out_ref[...] = jnp.dot(
        wide, gather, precision=lax.Precision.HIGHEST, preferred_element_type=jnp.float32
    )


def sum_kernel(*refs):
    rows = refs[-1].shape[0]
    total = refs[0][...]
    for ref in refs[1:-1]:
        total = total + ref[:rows, :]
    refs[-1][...] = total


def correlation_sum_kernel(part_ref, other_ref, fourth_ref, out_ref, sent_ref):
    orbs, planes, _ = fourth_ref.shape
    width = sent_ref.shape[1]
    total = part_ref[...] + other_ref[...]
    out_ref[...] = total
    across = total.shape[1]
    for k in range(4):
        sent_ref[:orbs, k * across : (k + 1) * across] = total[k * orbs : (k + 1) * orbs]
        first = orbs + k * planes
        sent_ref[first : first + planes, :] = fourth_ref[orbs - 1, :, k * width : (k + 1) * width]


def spread_out(corr, planes):
    n_a, n_b = corr.shape
    shift = planes.bit_length() - 1
    shape = (n_b * planes, n_a * planes)

    def iota(shape, dim):
        return lax.broadcasted_iota(jnp.int32, shape, dim)

    def ones_where(mask):
        return jnp.where(mask, 1.0, 0.0).astype(jnp.bfloat16)

    take_b = ones_where(
        jnp.right_shift(iota((shape[0], n_b), 0), shift) == iota((shape[0], n_b), 1)
    )
    take_a = ones_where(
        jnp.right_shift(iota((n_a, shape[1]), 1), shift) == iota((n_a, shape[1]), 0)
    )
    same_plane = (jnp.bitwise_xor(iota(shape, 0), iota(shape, 1)) & (planes - 1)) == 0

    def spread(part):
        rows = lax.dot_general(
            take_b, part, (((1,), (1,)), ((), ())), preferred_element_type=jnp.float32
        ).astype(jnp.bfloat16)
        full = jnp.dot(rows, take_a, preferred_element_type=jnp.float32)
        return jnp.where(same_plane, full, 0.0).astype(jnp.bfloat16)

    high, low = two_parts(corr * step_length)
    return spread(high), spread(low)


def projections(high, low, fields, chunk):
    half = fields[0].shape[0] // 2
    total = None
    for f in range(0, len(fields), 2):
        pair = fields[f : f + 2]
        terms = [
            (low[:, f * half : (f + 2) * half], jnp.concatenate([r[:half, chunk] for r in pair], 0))
        ]
        for g, field_ref in enumerate(pair):
            here = high[:, (f + g) * half : (f + g + 1) * half]
            terms.append((jnp.concatenate([here, here], axis=1), field_ref[:, chunk]))
        for left, right in terms:
            term = jnp.dot(left, right, preferred_element_type=jnp.float32)
            total = term if total is None else total + term
    return total


def step_kernel(
    own_phi, pair_phi, own_parts, pair_parts, third_parts, fourth_parts, image_ref, ward_ref,
    corr_ref, kept_ref, out1_ref, out2_ref, out3_ref, new_ref, all_ref,
):
    orbs, planes, grid_p = image_ref.shape
    width = 2 * lanes
    share = grid_p // 4

    @pl.when(on_inner())
    def _():
        high, low = spread_out(corr_ref[...], planes)
        fields = (own_parts, pair_parts, third_parts, fourth_parts)
        for c in range(grid_p // width):
            chunk = slice(c * width, (c + 1) * width)
            change = projections(high, low, fields, chunk)
            density = jnp.zeros((planes, width), jnp.float32)
            for f, (phi_ref, half_ref) in enumerate(((own_phi, image_ref), (pair_phi, ward_ref))):
                for a in range(orbs):
                    at = (f * orbs + a) * planes
                    value = (
                        phi_ref[a * planes : (a + 1) * planes, chunk]
                        - step_length * half_ref[a, :, chunk]
                        + change[at : at + planes]
                    )
                    density = density + value * value
                    if f == 0:
                        new_ref[a, :, chunk] = value
            all_ref[:, chunk] = density * (1.0 / (4 * orbs))
        for k, part_ref in enumerate((kept_ref, out1_ref, out2_ref, out3_ref)):
            first = pl.multiple_of(jnp.bitwise_xor(lax.axis_index("orb"), k) * share, share)
            part_ref[:planes, :] = all_ref[:, pl.ds(first, share)]


def all_but_last_kernel(field_ref, out_ref):
    out_ref[...] = field_ref[: out_ref.shape[0]]


def outer_split_kernel(third_ref, fourth_ref, sent_ref, live_ref, third_parts, fourth_parts):
    orbs, planes, _ = third_ref.shape

    @pl.when(jnp.logical_not(on_inner()))
    def _():
        split_into(third_parts, third_ref, live_ref, 2)
        split_into(fourth_parts, fourth_ref, live_ref, 3)
        first = orbs
        value = jnp.concatenate(
            [sent_ref[first + k * planes : first + (k + 1) * planes, :] for k in range(4)], axis=1
        )
        at = 4 * orbs - 1
        split_one(fourth_parts, value * live_ref[at : at + 1, :], orbs - 1)


def finish_kernel(
    own_phi, own_parts, pair_parts, third_parts, fourth_parts, image_ref, corr_ref, inner_new,
    new_ref, own_new, sem,
):
    orbs, planes, grid_p = image_ref.shape
    width = 2 * lanes

    def write(values_ref):
        copy = pltpu.make_async_copy(values_ref, new_ref, sem)
        copy.start()
        copy.wait()

    @pl.when(on_inner())
    def _():
        write(inner_new)

    @pl.when(jnp.logical_not(on_inner()))
    def _():
        corr = jnp.concatenate(
            [corr_ref[:orbs, (2 * k + 1) * orbs : (2 * k + 2) * orbs] for k in (1, 0, 2, 3)], axis=0
        )
        high, low = spread_out(corr, planes)
        fields = (own_parts, pair_parts, third_parts, fourth_parts)
        for c in range(grid_p // width):
            chunk = slice(c * width, (c + 1) * width)
            change = projections(high, low, fields, chunk)
            for a in range(orbs):
                at = slice(a * planes, (a + 1) * planes)
                own_new[a, :, chunk] = (
                    own_phi[at, chunk] - step_length * image_ref[a, :, chunk] + change[at]
                )
        write(own_new)


def last_kernel(sent2_ref, sent3_ref, given_ref, kept_ref, density_ref):
    planes = density_ref.shape[0]

    @pl.when(on_inner())
    def _():
        density_ref[...] = kept_ref[...] + sent3_ref[...]

    @pl.when(jnp.logical_not(on_inner()))
    def _():
        density_ref[...] = given_ref[:planes] + sent2_ref[:planes]


def call(kernel, out_shape, specs, scratch=(), out_specs=None):
    kinds = {"s": pltpu.SMEM, "v": pltpu.VMEM, "a": pl.ANY}
    if out_specs is None:
        out_specs = "v" * len(jax.tree.leaves(out_shape))
    places = [pl.BlockSpec(memory_space=kinds[kind]) for kind in out_specs]
    return pl.pallas_call(
        kernel,
        out_shape=out_shape,
        in_specs=[pl.BlockSpec(memory_space=kinds[kind]) for kind in specs],
        out_specs=places if isinstance(out_shape, (tuple, list)) else places[0],
        scratch_shapes=list(scratch),
        compiler_params=pltpu.CompilerParams(vmem_limit_bytes=10 * 2**20),
        cost_estimate=pl.CostEstimate(flops=1, bytes_accessed=1, transcendentals=0),
    )


def line_device(psi, potential, extent):
    orbs, planes, grid_p = psi.shape
    n_cmp = lax.axis_size("cmp")
    rows = orbs * planes
    cells = planes * n_cmp * grid_p
    swap = [(0, 1), (1, 0), (2, 3), (3, 2)]
    line = ("orb", "cmp")
    to_near = [(i, i ^ 1) for i in range(n_cmp)]
    to_far = [(i, i ^ 3) for i in range(n_cmp)]

    def with_outer(inner_pairs):
        outer_pairs = [(z * n_cmp + i, z * n_cmp + k) for z in (0, 3) for i, k in to_near]
        return inner_pairs + outer_pairs

    across = with_outer([(z * n_cmp + i, (3 - z) * n_cmp + i) for z in (1, 2) for i in range(n_cmp)])
    inner_far = with_outer([(z * n_cmp + i, z * n_cmp + k) for z in (1, 2) for i, k in to_far])

    block = jax.ShapeDtypeStruct(psi.shape, jnp.float32)
    parts = jax.ShapeDtypeStruct((2 * rows, grid_p), jnp.bfloat16)
    flat = jax.ShapeDtypeStruct((rows, grid_p), jnp.float32)
    columns = jnp.asarray(column_band())
    bands = jnp.asarray(plane_bands(planes))

    pair = lax.ppermute(psi, "orb", swap)
    third = lax.ppermute(psi, line, across)
    grid = call(columns_kernel, jax.ShapeDtypeStruct((8, grid_p), jnp.int32), "")()
    slab, grid = lax.optimization_barrier((psi, grid))
    near = lax.ppermute(slab, "cmp", to_near)
    far = lax.ppermute(slab, "cmp", to_far)

    live = call(live_kernel, jax.ShapeDtypeStruct((4 * orbs, grid_p), jnp.float32), "vs")(
        grid, extent
    )
    local, own_parts, own_phi = call(
        functools.partial(local_kernel, 0), (block, parts, flat), "vvvv"
    )(psi, potential, live, columns)
    pair, local, own_parts = lax.optimization_barrier((pair, local, own_parts))
    fourth = lax.ppermute(pair, line, across)
    third_out = lax.ppermute(third, "orb", swap)
    third_parts = call(functools.partial(split_kernel, 2), parts, "vv")(third, live)
    short = jax.ShapeDtypeStruct((orbs, planes, grid_p - lanes), jnp.float32)
    pair_far = lax.ppermute(call(shorten_kernel, short, "v")(pair), line, inner_far)
    pair_near = lax.ppermute(pair, "cmp", to_near)

    image, image_parts = call(functools.partial(plane_kernel, 0), (block, parts), "vvvvvv")(
        far, psi, near, local, live, bands
    )
    ward_local, pair_parts, pair_phi = call(
        functools.partial(local_kernel, 1), (block, parts, flat), "vvvv"
    )(pair, potential, live, columns)
    early = call(
        functools.partial(overlap_kernel, planes, 3),
        jax.ShapeDtypeStruct((3 * orbs, rows), jnp.float32),
        "vvvv",
    )(own_parts, pair_parts, third_parts, image_parts)

    fourth, ward_local, early = lax.optimization_barrier((fourth, ward_local, early))
    most = jax.ShapeDtypeStruct((orbs - 1, planes, grid_p), jnp.float32)
    fourth_out = lax.ppermute(call(all_but_last_kernel, most, "v")(fourth), "orb", swap)
    pair_far, third_out = lax.optimization_barrier((pair_far, third_out))
    ward, ward_parts = call(
        functools.partial(plane_kernel, 1),
        (block, parts),
        "vvvvvv",
        [pltpu.VMEM((orbs, planes, lanes), jnp.float32)],
    )(
        pair_far, pair, pair_near, ward_local, live, bands
    )
    fourth_parts = call(functools.partial(split_kernel, 3), parts, "vv")(fourth, live)
    last = call(
        functools.partial(overlap_kernel, planes, 1),
        jax.ShapeDtypeStruct((orbs, rows), jnp.float32),
        "vv",
    )(fourth_parts, image_parts)
    part = call(
        functools.partial(correlation_kernel, planes, 1.0 / cells),
        jax.ShapeDtypeStruct((4 * orbs, 2 * orbs), jnp.float32),
        "vvvvvvv",
    )(own_parts, pair_parts, third_parts, fourth_parts, ward_parts, early, last)
    small = jax.ShapeDtypeStruct(part.shape, jnp.float32)
    chip = call(sum_kernel, small, "vv")(part, lax.ppermute(part, "cmp", to_near))
    correlation, sent = call(
        correlation_sum_kernel,
        (small, jax.ShapeDtypeStruct((orbs + 4 * planes, grid_p // 4), jnp.float32)),
        "vvv",
    )(chip, lax.ppermute(chip, line, inner_far), fourth)

    given_correlation = lax.ppermute(sent, "orb", swap)

    share = jax.ShapeDtypeStruct((planes, grid_p // 4), jnp.float32)
    wide = jax.ShapeDtypeStruct((planes + orbs, grid_p // 4), jnp.float32)
    first_sent = jax.ShapeDtypeStruct((2 * planes, grid_p // 4), jnp.float32)
    kept, first, second, last, inner_new = call(
        step_kernel,
        [share, wide, first_sent, share, block],
        "vvvvvvvvv",
        [pltpu.VMEM((planes, grid_p), jnp.float32)],
    )(
        own_phi, pair_phi, own_parts, pair_parts, third_parts, fourth_parts, image, ward,
        correlation,
    )
    given = lax.ppermute(first, "orb", swap)
    sent2 = lax.ppermute(second, "orb", [(i, i ^ 2) for i in range(4)])
    sent3 = lax.ppermute(last, line, across)
    third_held, fourth_held = call(outer_split_kernel, (parts, parts), "vvvv")(
        third_out, fourth_out, given_correlation, live
    )
    new = call(
        finish_kernel,
        block,
        "vvvvvvvv",
        [pltpu.VMEM(block.shape, jnp.float32), pltpu.SemaphoreType.DMA],
        "a",
    )(
        own_phi, own_parts, pair_parts, third_held, fourth_held, image, given_correlation,
        inner_new,
    )
    sent2, sent3, given, new = lax.optimization_barrier((sent2, sent3, given, new))
    density = call(last_kernel, share, "vvvv")(sent2, sent3, given, kept)
    return (new, density)


def per_device(psi, potential, extent):
    orbs, planes, grid_p = psi.shape
    fits = (
        lax.axis_size("orb") == 4
        and lax.axis_size("cmp") == 4
        and orbs == 8
        and planes == 16
        and grid_p == lanes * (reach // (planes - reach) + 1)
    )
    return (line_device if fits else general_device)(psi, potential, extent)


def solution(mesh):
    return jax.shard_map(
        per_device,
        mesh=mesh,
        in_specs=(P(("grp", "orb"), "cmp", None), P(("grp", "cmp"), None), P("grp")),
        out_specs=(P(("grp", "orb"), "cmp", None), P(("grp", "cmp"), "orb")),
        check_vma=False,
    )
```

```python
import functools
import math

import jax
import jax.numpy as jnp
import numpy as np
from jax import lax
from jax.experimental import pallas as pl
from jax.experimental.pallas import tpu as pltpu
from jax.sharding import PartitionSpec as P

step_length = 0.2
reach = 14
lanes = 128


def padded_2(cells, sides, width):
    for axis, dim in sides:
        count = lax.axis_size(axis)
        head = lax.slice_in_dim(cells, 0, width, axis=dim)
        tail = lax.slice_in_dim(cells, cells.shape[dim] - width, cells.shape[dim], axis=dim)
        cells = jnp.concatenate(
            [
                lax.ppermute(tail, axis, [(i, (i + 1) % count) for i in range(count)]),
                cells,
                lax.ppermute(head, axis, [((i + 1) % count, i) for i in range(count)]),
            ],
            axis=dim,
        )
    return cells


def band_matrix(length):
    rows = lax.broadcasted_iota(jnp.int32, (length + 2 * reach, length), 0)
    cols = lax.broadcasted_iota(jnp.int32, (length + 2 * reach, length), 1)
    spread = jnp.abs(rows - reach - cols)
    safe = jnp.maximum(spread, 1).astype(jnp.float32)
    signed = jnp.where(spread % 2 == 1, 2.0, -2.0) / (safe * safe)
    value = jnp.where(spread == 0, -math.pi**2 / 3.0, signed)
    return jnp.where(spread <= reach, value, 0.0)


def across_planes(padded, planes):
    return jnp.einsum("awp,wy->ayp", padded, band_matrix(planes), precision=lax.Precision.HIGHEST)


def along_grid(field):
    orbs, planes, grid_p = field.shape
    width = 128
    blocks = field.reshape(orbs, planes, grid_p // width, width)
    before = jnp.roll(blocks[..., width - reach :], 1, axis=2)
    after = jnp.roll(blocks[..., :reach], -1, axis=2)
    window = jnp.concatenate([before, blocks, after], axis=3)
    result = jnp.einsum(
        "axnw,wq->axnq", window, band_matrix(width), precision=lax.Precision.HIGHEST
    )
    return result.reshape(orbs, planes, grid_p)


def general_device(psi, potential, extent):
    orb_dev, planes, grid_p = psi.shape
    n_orb = lax.axis_size("orb")
    norbitals = orb_dev * n_orb
    cells = planes * lax.axis_size("cmp") * grid_p
    column = lax.broadcasted_iota(jnp.int32, (norbitals, grid_p), 1)
    live_all = (column < extent[:, None]).astype(jnp.float32)
    own_live = lax.dynamic_slice_in_dim(live_all, lax.axis_index("orb") * orb_dev, orb_dev, 0)
    phi = psi * own_live[:, None, :]
    padded = padded_2(phi, (("cmp", 1),), reach)
    kinetic = -0.5 * (across_planes(padded, planes) + along_grid(phi))
    hphi = own_live[:, None, :] * (kinetic + potential[None] * phi)
    phi_c, hphi_c = (
        lax.all_to_all(phi, "orb", split_axis=2, concat_axis=0, tiled=True),
        lax.all_to_all(hphi, "orb", split_axis=2, concat_axis=0, tiled=True),
    )
    flat_phi = phi_c.reshape(norbitals, -1)
    flat_h = hphi_c.reshape(norbitals, -1)
    partial_correlation = lax.dot_general(
        flat_phi,
        flat_h,
        (((1,), (1,)), ((), ())),
        precision=lax.Precision.HIGHEST,
        preferred_element_type=jnp.float32,
    )
    correlation = lax.psum(partial_correlation, ("orb", "cmp")) / cells
    grad_c = (flat_h - jnp.dot(correlation.T, flat_phi, precision=lax.Precision.HIGHEST)).reshape(
        phi_c.shape
    )
    grad = lax.all_to_all(grad_c, "orb", split_axis=0, concat_axis=2, tiled=True)
    psi_new = phi - step_length * grad
    density = (
        lax.psum_scatter(jnp.sum(psi_new * psi_new, axis=0), "orb", scatter_dimension=1, tiled=True)
        / norbitals
    )
    return (psi_new, density)


def weight(spread):
    spread = np.abs(spread)
    safe = np.maximum(spread, 1).astype(np.float64)
    value = np.where(spread % 2 == 1, 2.0, -2.0) / (safe * safe)
    value = np.where(spread == 0, -math.pi**2 / 3.0, value)
    return np.where(spread <= reach, value, 0.0).astype(np.float32)


def two_parts(value):
    high = value.astype(jnp.bfloat16)
    return high, (value - high.astype(np.float32)).astype(jnp.bfloat16)


def three_parts(value):
    high, rest = two_parts(value)
    middle, low = two_parts(value - high.astype(np.float32))
    del rest
    return high, middle, low


def column_band():
    rows = np.arange(2 * lanes)[:, None]
    cols = np.arange(lanes)[None, :]
    return np.concatenate(three_parts(weight(rows - cols - reach)), axis=1)


def six_products(band):
    high, middle, low = three_parts(band)
    return np.concatenate([high, high, high, middle, middle, low], axis=1)


def plane_bands(planes):
    rows = np.arange(planes)[:, None]
    cols = np.arange(planes)[None, :]
    sides = [
        np.concatenate([weight(cols + side - rows), weight(cols - side - rows)], axis=1)
        for side in (-planes, planes)
    ]
    return six_products(weight(cols - rows)), np.stack([six_products(band) for band in sides])


def columns_kernel(out_ref):
    out_ref[...] = lax.broadcasted_iota(jnp.int32, out_ref.shape, 1)


def owner_of(f):
    z = lax.axis_index("orb")
    if f < 2:
        return z if f == 0 else jnp.where(z % 2 == 0, z + 1, z - 1)
    left, right = (2, 1) if f == 2 else (3, 0)
    return jnp.where(z < 2, left, right)


def on_inner():
    z = lax.axis_index("orb")
    return (z == 1) | (z == 2)


def live_kernel(columns_ref, extent_ref, out_ref):
    orbs = out_ref.shape[0] // 4
    for f in range(4):
        owner = owner_of(f)
        for a in range(orbs):
            row = jnp.where(columns_ref[:1, :] < extent_ref[owner * orbs + a], 1.0, 0.0)
            out_ref[f * orbs + a : f * orbs + a + 1, :] = row


def masked(field_ref, a, live_ref, f):
    at = f * (live_ref.shape[0] // 4) + a
    return field_ref[a] * live_ref[at : at + 1, :]


def split_one(parts_ref, value, a):
    planes = value.shape[0]
    half = parts_ref.shape[0] // 2
    high, low = two_parts(value)
    parts_ref[a * planes : (a + 1) * planes, :] = high
    parts_ref[half + a * planes : half + (a + 1) * planes, :] = low


def split_into(parts_ref, field_ref, live_ref, f):
    for a in range(field_ref.shape[0]):
        split_one(parts_ref, masked(field_ref, a, live_ref, f), a)


def split_kernel(f, field_ref, live_ref, parts_ref):
    split_into(parts_ref, field_ref, live_ref, f)


def short_rows(planes):
    spare = planes - reach
    for parity, first in ((0, 0), (1, spare)):
        free = reach if parity == 0 else 0
        each = reach // spare
        yield parity, [(free + p // each, p % each, first + p) for p in range(reach)]


def shorten_kernel(psi_ref, short_ref):
    orbs, planes, _ = psi_ref.shape
    width = short_ref.shape[2]
    short_ref[...] = psi_ref[:, :, :width]
    for parity, moves in short_rows(planes):

        @pl.when(lax.axis_index("cmp") % 2 == parity)
        def _():
            for a in range(orbs):
                for row, place, plane in moves:
                    short_ref[a, row : row + 1, place * lanes : (place + 1) * lanes] = psi_ref[
                        a, plane : plane + 1, width:
                    ]


def band_product(band, slabs):
    high, middle, low = three_parts(slabs)
    return jnp.dot(
        band,
        jnp.concatenate([high, middle, low, high, middle, high], axis=0),
        preferred_element_type=jnp.float32,
    )


def local_kernel(
    f, psi_ref, potential_ref, live_ref, band_ref, own_band_ref, out_ref, parts_ref, phi_ref
):
    orbs, planes, grid_p = psi_ref.shape
    tiles = grid_p // lanes
    for a in range(orbs):
        phi = masked(psi_ref, a, live_ref, f)
        phi_ref[a * planes : (a + 1) * planes, :] = phi
        high, low = two_parts(phi)
        parts_ref[a * planes : (a + 1) * planes, :] = high
        parts_ref[(orbs + a) * planes : (orbs + a + 1) * planes, :] = low
    fields = three_parts(pltpu.roll(phi_ref[...], reach, 1))
    for t in range(tiles):
        here, after = t * lanes, (t + 1) % tiles * lanes
        second = None
        for n in (1, 2, 3):
            field = fields[3 - n]
            wide = jnp.concatenate(
                [field[:, here : here + lanes], field[:, after : after + lanes]], axis=1
            )
            product = jnp.dot(
                wide, band_ref[:, : n * lanes], preferred_element_type=jnp.float32
            )
            for k in reversed(range(n)):
                term = product[:, k * lanes : (k + 1) * lanes]
                second = term if second is None else second + term
        field = phi_ref[:, here : here + lanes].reshape(orbs, planes, lanes)
        out_ref[:, :, here : here + lanes] = (
            potential_ref[:, here : here + lanes][None] * field
            - 0.5 * second.reshape(orbs, planes, lanes)
        )
    for a in range(orbs):
        out_ref[a] = out_ref[a] - 0.5 * band_product(own_band_ref[...], psi_ref[a])


def plane_kernel(
    f, far_ref, near_ref, local_ref, live_ref, band_ref, out_ref, parts_ref, *rest_ref
):
    orbs, planes, _ = near_ref.shape
    band = band_ref[lax.axis_index("cmp") % 2]
    for ref in rest_ref:
        ref[...] = jnp.zeros_like(ref)
        for parity, moves in short_rows(planes):

            @pl.when(lax.axis_index("cmp") % 2 != parity)
            def _():
                for a in range(orbs):
                    for row, place, plane in moves:
                        ref[a, plane : plane + 1, :] = far_ref[
                            a, row : row + 1, place * lanes : (place + 1) * lanes
                        ]

    for a in range(orbs):
        far = jnp.concatenate([far_ref[a]] + [ref[a] for ref in rest_ref], axis=1)
        second = band_product(band, jnp.concatenate([far, near_ref[a]], axis=0))
        image = (local_ref[a] - 0.5 * second) * live_ref[f * orbs + a : f * orbs + a + 1, :]
        out_ref[a] = image
        high, low = two_parts(image)
        parts_ref[a * planes : (a + 1) * planes, :] = high
        parts_ref[(orbs + a) * planes : (orbs + a + 1) * planes, :] = low


def overlaps(field_ref, image_ref, planes):
    half = field_ref.shape[0] // 2
    product = lax.dot_general(
        field_ref[...],
        image_ref[...],
        (((1,), (1,)), ((), ())),
        preferred_element_type=jnp.float32,
    )
    product = product[:half] + product[half:]
    product = product[:, :half] + product[:, half:]
    row = lax.broadcasted_iota(jnp.int32, (half, half), 0)
    col = lax.broadcasted_iota(jnp.int32, (half, half), 1)
    product = jnp.where(row % planes == col % planes, product, 0.0)
    return jnp.sum(product.reshape(half // planes, planes, half), axis=1)


def overlap_kernel(planes, n_fields, *refs):
    fields, image_ref, out_ref = refs[:n_fields], refs[n_fields], refs[n_fields + 1]
    for f, field_ref in enumerate(fields):
        value = overlaps(field_ref, image_ref, planes)
        out_ref[f * value.shape[0] : (f + 1) * value.shape[0], :] = value


def correlation_kernel(
    planes, scale, own_ref, pair_ref, third_ref, fourth_ref, ward_ref, early_ref, last_ref, out_ref
):
    half = own_ref.shape[0] // 2
    orbs = half // planes
    ward = [overlaps(ref, ward_ref, planes) for ref in (own_ref, pair_ref, third_ref, fourth_ref)]
    wide = jnp.concatenate(
        [
            jnp.concatenate([early_ref[...], last_ref[...]], axis=0),
            jnp.concatenate(ward, axis=0),
        ],
        axis=1,
    )
    row = lax.broadcasted_iota(jnp.int32, (2 * half, 2 * orbs), 0)
    col = lax.broadcasted_iota(jnp.int32, (2 * half, 2 * orbs), 1)
    gather = jnp.where(row // planes == col, scale, 0.0)
    out_ref[...] = jnp.dot(
        wide, gather, precision=lax.Precision.HIGHEST, preferred_element_type=jnp.float32
    )


def sum_kernel(*refs):
    rows = refs[-1].shape[0]
    total = refs[0][...]
    for ref in refs[1:-1]:
        total = total + ref[:rows, :]
    refs[-1][...] = total


def correlation_sum_kernel(part_ref, other_ref, fourth_ref, out_ref, sent_ref):
    orbs, planes, _ = fourth_ref.shape
    width = sent_ref.shape[1]
    total = part_ref[...] + other_ref[...]
    out_ref[...] = total
    across = total.shape[1]
    for k in range(4):
        sent_ref[:orbs, k * across : (k + 1) * across] = total[k * orbs : (k + 1) * orbs]
        first = orbs + k * planes
        sent_ref[first : first + planes, :] = fourth_ref[orbs - 1, :, k * width : (k + 1) * width]


def spread_out(corr, planes):
    n_a, n_b = corr.shape
    shift = planes.bit_length() - 1
    shape = (n_b * planes, n_a * planes)

    def iota(shape, dim):
        return lax.broadcasted_iota(jnp.int32, shape, dim)

    def ones_where(mask):
        return jnp.where(mask, 1.0, 0.0).astype(jnp.bfloat16)

    take_b = ones_where(
        jnp.right_shift(iota((shape[0], n_b), 0), shift) == iota((shape[0], n_b), 1)
    )
    take_a = ones_where(
        jnp.right_shift(iota((n_a, shape[1]), 1), shift) == iota((n_a, shape[1]), 0)
    )
    same_plane = (jnp.bitwise_xor(iota(shape, 0), iota(shape, 1)) & (planes - 1)) == 0

    def spread(part):
        rows = lax.dot_general(
            take_b, part, (((1,), (1,)), ((), ())), preferred_element_type=jnp.float32
        ).astype(jnp.bfloat16)
        full = jnp.dot(rows, take_a, preferred_element_type=jnp.float32)
        return jnp.where(same_plane, full, 0.0).astype(jnp.bfloat16)

    high, low = two_parts(corr * step_length)
    return spread(high), spread(low)


def projections(high, low, fields, chunk):
    half = fields[0].shape[0] // 2
    total = None
    for f in range(0, len(fields), 2):
        pair = fields[f : f + 2]
        terms = [
            (low[:, f * half : (f + 2) * half], jnp.concatenate([r[:half, chunk] for r in pair], 0))
        ]
        for g, field_ref in enumerate(pair):
            here = high[:, (f + g) * half : (f + g + 1) * half]
            terms.append((jnp.concatenate([here, here], axis=1), field_ref[:, chunk]))
        for left, right in terms:
            term = jnp.dot(left, right, preferred_element_type=jnp.float32)
            total = term if total is None else total + term
    return total


def step_kernel(
    own_phi, pair_phi, own_parts, pair_parts, third_parts, fourth_parts, image_ref, ward_ref,
    corr_ref, kept_ref, out1_ref, out2_ref, out3_ref, new_ref, all_ref,
):
    orbs, planes, grid_p = image_ref.shape
    width = 2 * lanes
    share = grid_p // 4

    @pl.when(on_inner())
    def _():
        high, low = spread_out(corr_ref[...], planes)
        fields = (own_parts, pair_parts, third_parts, fourth_parts)
        for c in range(grid_p // width):
            chunk = slice(c * width, (c + 1) * width)
            change = projections(high, low, fields, chunk)
            density = jnp.zeros((planes, width), jnp.float32)
            for f, (phi_ref, half_ref) in enumerate(((own_phi, image_ref), (pair_phi, ward_ref))):
                for a in range(orbs):
                    at = (f * orbs + a) * planes
                    value = (
                        phi_ref[a * planes : (a + 1) * planes, chunk]
                        - step_length * half_ref[a, :, chunk]
                        + change[at : at + planes]
                    )
                    density = density + value * value
                    if f == 0:
                        new_ref[a, :, chunk] = value
            all_ref[:, chunk] = density * (1.0 / (4 * orbs))
        for k, part_ref in enumerate((kept_ref, out1_ref, out2_ref, out3_ref)):
            first = pl.multiple_of(jnp.bitwise_xor(lax.axis_index("orb"), k) * share, share)
            part_ref[:planes, :] = all_ref[:, pl.ds(first, share)]


def all_but_last_kernel(field_ref, out_ref):
    out_ref[...] = field_ref[: out_ref.shape[0]]


def outer_split_kernel(third_ref, fourth_ref, sent_ref, live_ref, third_parts, fourth_parts):
    orbs, planes, _ = third_ref.shape

    @pl.when(jnp.logical_not(on_inner()))
    def _():
        split_into(third_parts, third_ref, live_ref, 2)
        split_into(fourth_parts, fourth_ref, live_ref, 3)
        first = orbs
        value = jnp.concatenate(
            [sent_ref[first + k * planes : first + (k + 1) * planes, :] for k in range(4)], axis=1
        )
        at = 4 * orbs - 1
        split_one(fourth_parts, value * live_ref[at : at + 1, :], orbs - 1)


def finish_kernel(
    own_phi, own_parts, pair_parts, third_parts, fourth_parts, image_ref, corr_ref, inner_new,
    new_ref, own_new, sem,
):
    orbs, planes, grid_p = image_ref.shape
    width = 2 * lanes

    def write(values_ref):
        copy = pltpu.make_async_copy(values_ref, new_ref, sem)
        copy.start()
        copy.wait()

    @pl.when(on_inner())
    def _():
        write(inner_new)

    @pl.when(jnp.logical_not(on_inner()))
    def _():
        corr = jnp.concatenate(
            [corr_ref[:orbs, (2 * k + 1) * orbs : (2 * k + 2) * orbs] for k in (1, 0, 2, 3)], axis=0
        )
        high, low = spread_out(corr, planes)
        fields = (own_parts, pair_parts, third_parts, fourth_parts)
        for c in range(grid_p // width):
            chunk = slice(c * width, (c + 1) * width)
            change = projections(high, low, fields, chunk)
            for a in range(orbs):
                at = slice(a * planes, (a + 1) * planes)
                own_new[a, :, chunk] = (
                    own_phi[at, chunk] - step_length * image_ref[a, :, chunk] + change[at]
                )
        write(own_new)


def last_kernel(sent2_ref, sent3_ref, given_ref, kept_ref, density_ref):
    planes = density_ref.shape[0]

    @pl.when(on_inner())
    def _():
        density_ref[...] = kept_ref[...] + sent3_ref[...]

    @pl.when(jnp.logical_not(on_inner()))
    def _():
        density_ref[...] = given_ref[:planes] + sent2_ref[:planes]


def call(kernel, out_shape, specs, scratch=(), out_specs=None):
    kinds = {"s": pltpu.SMEM, "v": pltpu.VMEM, "a": pl.ANY}
    if out_specs is None:
        out_specs = "v" * len(jax.tree.leaves(out_shape))
    places = [pl.BlockSpec(memory_space=kinds[kind]) for kind in out_specs]
    return pl.pallas_call(
        kernel,
        out_shape=out_shape,
        in_specs=[pl.BlockSpec(memory_space=kinds[kind]) for kind in specs],
        out_specs=places if isinstance(out_shape, (tuple, list)) else places[0],
        scratch_shapes=list(scratch),
        compiler_params=pltpu.CompilerParams(vmem_limit_bytes=10 * 2**20),
        cost_estimate=pl.CostEstimate(flops=1, bytes_accessed=1, transcendentals=0),
    )


def line_device(psi, potential, extent):
    orbs, planes, grid_p = psi.shape
    n_cmp = lax.axis_size("cmp")
    rows = orbs * planes
    cells = planes * n_cmp * grid_p
    swap = [(0, 1), (1, 0), (2, 3), (3, 2)]
    line = ("orb", "cmp")
    to_near = [(i, i ^ 1) for i in range(n_cmp)]
    to_far = [(i, i ^ 3) for i in range(n_cmp)]

    def with_outer(inner_pairs):
        outer_pairs = [(z * n_cmp + i, z * n_cmp + k) for z in (0, 3) for i, k in to_near]
        return inner_pairs + outer_pairs

    across = with_outer([(z * n_cmp + i, (3 - z) * n_cmp + i) for z in (1, 2) for i in range(n_cmp)])
    inner_far = with_outer([(z * n_cmp + i, z * n_cmp + k) for z in (1, 2) for i, k in to_far])

    block = jax.ShapeDtypeStruct(psi.shape, jnp.float32)
    parts = jax.ShapeDtypeStruct((2 * rows, grid_p), jnp.bfloat16)
    flat = jax.ShapeDtypeStruct((rows, grid_p), jnp.float32)
    columns = jnp.asarray(column_band())
    own_band, bands = (jnp.asarray(band) for band in plane_bands(planes))

    pair = lax.ppermute(psi, "orb", swap)
    third = lax.ppermute(psi, line, across)
    grid = call(columns_kernel, jax.ShapeDtypeStruct((8, grid_p), jnp.int32), "")()
    slab, grid = lax.optimization_barrier((psi, grid))
    near = lax.ppermute(slab, "cmp", to_near)
    far = lax.ppermute(slab, "cmp", to_far)

    live = call(live_kernel, jax.ShapeDtypeStruct((4 * orbs, grid_p), jnp.float32), "vs")(
        grid, extent
    )
    local, own_parts, own_phi = call(
        functools.partial(local_kernel, 0), (block, parts, flat), "vvvvv"
    )(psi, potential, live, columns, own_band)
    pair, local, own_parts = lax.optimization_barrier((pair, local, own_parts))
    fourth = lax.ppermute(pair, line, across)
    third_out = lax.ppermute(third, "orb", swap)
    third_parts = call(functools.partial(split_kernel, 2), parts, "vv")(third, live)
    short = jax.ShapeDtypeStruct((orbs, planes, grid_p - lanes), jnp.float32)
    pair_far = lax.ppermute(call(shorten_kernel, short, "v")(pair), line, inner_far)
    pair_near = lax.ppermute(pair, "cmp", to_near)

    image, image_parts = call(functools.partial(plane_kernel, 0), (block, parts), "vvvvv")(
        far, near, local, live, bands
    )
    ward_local, pair_parts, pair_phi = call(
        functools.partial(local_kernel, 1), (block, parts, flat), "vvvvv"
    )(pair, potential, live, columns, own_band)
    early = call(
        functools.partial(overlap_kernel, planes, 3),
        jax.ShapeDtypeStruct((3 * orbs, rows), jnp.float32),
        "vvvv",
    )(own_parts, pair_parts, third_parts, image_parts)

    fourth, ward_local, early = lax.optimization_barrier((fourth, ward_local, early))
    most = jax.ShapeDtypeStruct((orbs - 1, planes, grid_p), jnp.float32)
    fourth_out = lax.ppermute(call(all_but_last_kernel, most, "v")(fourth), "orb", swap)
    pair_far, third_out = lax.optimization_barrier((pair_far, third_out))
    ward, ward_parts = call(
        functools.partial(plane_kernel, 1),
        (block, parts),
        "vvvvv",
        [pltpu.VMEM((orbs, planes, lanes), jnp.float32)],
    )(
        pair_far, pair_near, ward_local, live, bands
    )
    fourth_parts = call(functools.partial(split_kernel, 3), parts, "vv")(fourth, live)
    last = call(
        functools.partial(overlap_kernel, planes, 1),
        jax.ShapeDtypeStruct((orbs, rows), jnp.float32),
        "vv",
    )(fourth_parts, image_parts)
    part = call(
        functools.partial(correlation_kernel, planes, 1.0 / cells),
        jax.ShapeDtypeStruct((4 * orbs, 2 * orbs), jnp.float32),
        "vvvvvvv",
    )(own_parts, pair_parts, third_parts, fourth_parts, ward_parts, early, last)
    small = jax.ShapeDtypeStruct(part.shape, jnp.float32)
    chip = call(sum_kernel, small, "vv")(part, lax.ppermute(part, "cmp", to_near))
    correlation, sent = call(
        correlation_sum_kernel,
        (small, jax.ShapeDtypeStruct((orbs + 4 * planes, grid_p // 4), jnp.float32)),
        "vvv",
    )(chip, lax.ppermute(chip, line, inner_far), fourth)

    given_correlation = lax.ppermute(sent, "orb", swap)

    share = jax.ShapeDtypeStruct((planes, grid_p // 4), jnp.float32)
    wide = jax.ShapeDtypeStruct((planes + orbs, grid_p // 4), jnp.float32)
    first_sent = jax.ShapeDtypeStruct((2 * planes, grid_p // 4), jnp.float32)
    kept, first, second, last, inner_new = call(
        step_kernel,
        [share, wide, first_sent, share, block],
        "vvvvvvvvv",
        [pltpu.VMEM((planes, grid_p), jnp.float32)],
    )(
        own_phi, pair_phi, own_parts, pair_parts, third_parts, fourth_parts, image, ward,
        correlation,
    )
    given = lax.ppermute(first, "orb", swap)
    sent2 = lax.ppermute(second, "orb", [(i, i ^ 2) for i in range(4)])
    sent3 = lax.ppermute(last, line, across)
    third_held, fourth_held = call(outer_split_kernel, (parts, parts), "vvvv")(
        third_out, fourth_out, given_correlation, live
    )
    new = call(
        finish_kernel,
        block,
        "vvvvvvvv",
        [pltpu.VMEM(block.shape, jnp.float32), pltpu.SemaphoreType.DMA],
        "a",
    )(
        own_phi, own_parts, pair_parts, third_held, fourth_held, image, given_correlation,
        inner_new,
    )
    sent2, sent3, given, new = lax.optimization_barrier((sent2, sent3, given, new))
    density = call(last_kernel, share, "vvvv")(sent2, sent3, given, kept)
    return (new, density)


def per_device(psi, potential, extent):
    orbs, planes, grid_p = psi.shape
    fits = (
        lax.axis_size("orb") == 4
        and lax.axis_size("cmp") == 4
        and orbs == 8
        and planes == 16
        and grid_p == lanes * (reach // (planes - reach) + 1)
    )
    return (line_device if fits else general_device)(psi, potential, extent)


def solution(mesh):
    return jax.shard_map(
        per_device,
        mesh=mesh,
        in_specs=(P(("grp", "orb"), "cmp", None), P(("grp", "cmp"), None), P("grp")),
        out_specs=(P(("grp", "orb"), "cmp", None), P(("grp", "cmp"), "orb")),
        check_vma=False,
    )
```
